32 devices in a mesh: fsdp: 4 (over z), context: 4 (over y, x), tensor: 2 (over core).
Axes of the slice: x: 2, y: 2, z: 4, core: 2. Of those that a mesh axis runs over, the one named last changes fastest.
Arguments:
- tokens_in: bfloat16 [4096, 768], P(('fsdp', 'context')), may hold values from -6 to 6
- chars_in: bfloat16 [6144, 768], P(('fsdp', 'context')), may hold values from -6 to 6
- segment_ids: int32 [4, 1024], P('fsdp'), may hold values from 0 to 3, never falling along the last dimension, each value on 1 to 512 neighbouring positions
- char_counts: int32 [16, 256], P(('fsdp', 'context')), may hold values from 1 to 4, 384 in all within a row
- valid: int32 [4, 1024], P('fsdp', 'context'), may hold values 0 or 1
- teacher_tokens: bfloat16 [4096, 768], P(('fsdp', 'context')), may hold values from -6 to 6
- teacher_chars: bfloat16 [6144, 768], P(('fsdp', 'context')), may hold values from -6 to 6
- w_qkv: bfloat16 [1, 768, 3, 768], P(None, 'fsdp', None, 'tensor'), may hold values from -0.21875 to 0.21875
- w_out: bfloat16 [1, 768, 768], P(None, 'tensor', 'fsdp'), may hold values from -0.3125 to 0.3125
- w_up: bfloat16 [1, 768, 3072], P(None, 'fsdp', 'tensor'), may hold values from -0.21875 to 0.21875
- w_down: bfloat16 [1, 3072, 768], P(None, 'tensor', 'fsdp'), may hold values from -0.15625 to 0.15625
- w_gru: bfloat16 [1, 768, 4, 384], P(None, 'fsdp', None, 'tensor'), may hold values from -0.21875 to 0.21875
- gru_bias: float32 [1, 2, 384], P(None, None, 'tensor'), may hold values from -7 to 0
- w_tok: bfloat16 [1, 768, 768], P(None, 'fsdp', 'tensor'), may hold values from -0.21875 to 0.21875
- w_char: bfloat16 [1, 2, 384, 768], P(None, None, 'tensor', 'fsdp'), may hold values from -0.625 to 0.625
- w_conv: bfloat16 [1, 3, 2, 768, 1536], P(None, None, None, 'tensor', 'fsdp'), may hold values from -0.09375 to 0.09375
- ln_gain: float32 [1, 4, 768], replicated, may hold values from 0.5 to 1.5
- ln_bias: float32 [1, 4, 768], replicated, may hold values from -2 to 2
Outputs:
- token_out: float32 [4096, 768], P(('fsdp', 'context'))
- char_out: float32 [6144, 768], P(('fsdp', 'context'))
- loss: float32 [], replicated
- grad_tokens: float32 [4096, 768], P(('fsdp', 'context'))
- grad_chars: float32 [6144, 768], P(('fsdp', 'context'))
- grad_qkv: float32 [1, 768, 3, 768], P(None, 'fsdp', None, 'tensor')
- grad_out: float32 [1, 768, 768], P(None, 'tensor', 'fsdp')
- grad_up: float32 [1, 768, 3072], P(None, 'fsdp', 'tensor')
- grad_down: float32 [1, 3072, 768], P(None, 'tensor', 'fsdp')
- grad_gru: float32 [1, 768, 4, 384], P(None, 'fsdp', None, 'tensor')
- grad_gru_bias: float32 [1, 2, 384], P(None, None, 'tensor')
- grad_tok: float32 [1, 768, 768], P(None, 'fsdp', 'tensor')
- grad_char: float32 [1, 2, 384, 768], P(None, None, 'tensor', 'fsdp')
- grad_conv: float32 [1, 3, 2, 768, 1536], P(None, None, None, 'tensor', 'fsdp')
- grad_gain: float32 [1, 4, 768], replicated
- grad_shift: float32 [1, 4, 768], replicated
The draws below stay inside these ranges and needn't reach their ends.
Inputs may be any that keep to these rules, and one draw needn't show every extreme that they name: `segment_ids`: in each sequence the ids never fall; each of the 4 documents covers one run of positions, at most 512 long, and one run has exactly 512. `char_counts`: each row sums to 384; its largest entry is exactly 4.
All inputs are finite; a program needn't handle non-finite values. No bound on the sum of `valid` on one device may be relied on, other than what follows from the above.
Results may differ from the reference program's by a relative error of at most 0.019.
Values may be sent and summed in bfloat16 or wider, within the bound.
No kernel may reach another device: no remote copies, remote signals or barrier semaphores. Data moves between devices by JAX's collectives and lax.ppermute only.
A program may use at most 192 MiB of HBM per device.

```python
import math
import jax
import jax.numpy as jnp
import numpy as np
from jax import lax

D = 768
HEADS = 12
HD = 64
FF = 3072
H = 384
LAYERS = 1
SPAN = 4
SEGS = 4
TOK_DEV = 256
LEN = 1024
TOKENS = 4096
CHAR_DEV = 384
CHARS = 6144
N_FSDP = 4
N_CONTEXT = 4


def plant(array, own_key, smallest, high):
    dims = array.shape
    index_at = [jax.random.randint(jax.random.fold_in(own_key, axis), (), 0, dims[axis]) for axis in range(len(dims))]
    array = array.at[tuple(index_at)].set(smallest)
    longest = dims.index(max(dims))
    index_at[longest] = (index_at[longest] + 1) % dims[longest]
    return array.at[tuple(index_at)].set(high)


def block_levels(stream_key, dims, split, least, largest):
    def one(axis_at, blocks):
        steps = jax.random.uniform(jax.random.fold_in(jax.random.fold_in(stream_key, 6), axis_at), (blocks,), jnp.float32, least / len(split), largest / len(split))
        return jnp.repeat(jnp.exp(steps), dims[axis_at] // blocks).reshape((-1,) + (1,) * (len(dims) - axis_at - 1))

    factor_of = one(*split[0])
    for cut in split[1:]:
        factor_of = factor_of * one(*cut)
    return factor_of


def split_up(number_of, total, reach, slope):
    loads = [(1 << 20) // math.isqrt(standing ** slope) + 1 for standing in range(2, number_of + 1)]
    rest, holding = total - reach - (number_of - 1), [1] * (number_of - 1)
    while rest > 0:
        candidates = [i for i in range(number_of - 1) if holding[i] < reach]
        whole, remaining = sum([loads[i] for i in candidates]), rest
        for i in candidates:
            more = min(reach - holding[i], max(1, remaining * loads[i] // whole), rest)
            holding[i] = holding[i] + more
            rest = rest - more
    return np.array([reach] + holding)


def uneven_parts(stream_key, count, total, limit, skew):
    if count == 2:
        one = jax.random.randint(stream_key, (), max(1, total - limit), min(limit, total - 1) + 1)
        return jnp.stack([one, total - one])
    sizes = jnp.asarray(split_up(count, total, limit, skew), jnp.int32)
    couples = (count - 1) // 2
    donor, receiver = sizes[1:1 + 2 * couples:2], sizes[2:2 + 2 * couples:2]
    slack = jnp.minimum(donor - 1, limit - receiver)
    shifted = jax.random.randint(jax.random.fold_in(stream_key, 1), (couples,), 0, 1 << 20) % (slack + 1)
    sizes = sizes.at[1:1 + 2 * couples:2].set(donor - shifted).at[2:2 + 2 * couples:2].set(receiver + shifted)
    return sizes[jax.random.permutation(jax.random.fold_in(stream_key, 2), count)]


def gaussian(key, shape, scale, limit, shards=(), held_as=jnp.bfloat16):
    values = scale * jax.random.normal(key, shape, jnp.float32)
    if shards:
        values = values * block_levels(key, shape, shards, -0.22, 0.18)
    return jnp.clip(values, -limit, limit).astype(held_as)


def setup_inputs(seed: int = 0) -> dict:
    key_of = jax.random.split(jax.random.key(seed), 19)
    tokens_in = gaussian(key_of[0], (TOKENS, D), 1.0, 6.0, ((0, 16),))
    chars_in = gaussian(key_of[1], (CHARS, D), 1.0, 6.0, ((0, 16),))
    segment_ids = jax.vmap(lambda own: jnp.searchsorted(jnp.cumsum(uneven_parts(own, SEGS, LEN, LEN // 2, 2)), jnp.arange(LEN), side="right"))(jax.random.split(key_of[2], N_FSDP)).reshape((N_FSDP, LEN)).astype(jnp.int32)
    char_counts = jax.vmap(lambda own: uneven_parts(own, TOK_DEV, CHAR_DEV, SPAN, 2))(jax.random.split(key_of[3], (N_FSDP * N_CONTEXT))).reshape((N_FSDP * N_CONTEXT, TOK_DEV)).astype(jnp.int32)
    valid = plant((jax.random.randint(key_of[4], (N_FSDP, LEN), 0, 4) < 3).astype(jnp.int32), jax.random.fold_in(key_of[4], 1), 0, 1)
    teacher_tokens = gaussian(key_of[5], (TOKENS, D), 1.0, 6.0, ((0, 16),))
    teacher_chars = gaussian(key_of[6], (CHARS, D), 1.0, 6.0, ((0, 16),))
    w_qkv = gaussian(key_of[7], (LAYERS, D, 3, D), D ** -0.5, 0.21875, ((1, 4), (3, 2)))
    w_out = gaussian(key_of[8], (LAYERS, D, D), (D // 2) ** -0.5, 0.3125, ((1, 2), (2, 4)))
    w_up = gaussian(key_of[9], (LAYERS, D, FF), D ** -0.5, 0.21875, ((1, 4), (2, 2)))
    w_down = gaussian(key_of[10], (LAYERS, FF, D), (FF // 2) ** -0.5, 0.15625, ((1, 2), (2, 4)))
    w_gru = gaussian(key_of[11], (LAYERS, D, 4, H), D ** -0.5, 0.21875, ((1, 4), (3, 2)))
    gru_bias = jnp.clip(-7.0 + 7.0 * jax.random.uniform(key_of[12], (LAYERS, 2, H), jnp.float32) ** block_levels(key_of[12], (LAYERS, 2, H), ((2, 2),), -0.2, 0.2), -7.0, 0.0)
    w_tok = gaussian(key_of[13], (LAYERS, D, D), D ** -0.5, 0.21875, ((1, 4), (2, 2)))
    w_char = gaussian(key_of[14], (LAYERS, 2, H, D), (D // 8) ** -0.5, 0.625, ((2, 2), (3, 4)))
    w_conv = gaussian(key_of[15], (LAYERS, 3, 2, D, 2 * D), (6 * D) ** -0.5, 0.09375, ((3, 2), (4, 4)))
    ln_gain = jnp.clip(1.0 + 0.1 * jax.random.normal(key_of[16], (LAYERS, 4, D), jnp.float32), 0.5, 1.5)
    ln_bias = gaussian(key_of[17], (LAYERS, 4, D), 0.3, 2.0, (), jnp.float32)
    return dict(tokens_in=tokens_in, chars_in=chars_in, segment_ids=segment_ids, char_counts=char_counts, valid=valid, teacher_tokens=teacher_tokens, teacher_chars=teacher_chars, w_qkv=w_qkv, w_out=w_out, w_up=w_up, w_down=w_down, w_gru=w_gru, gru_bias=gru_bias, w_tok=w_tok, w_char=w_char, w_conv=w_conv, ln_gain=ln_gain, ln_bias=ln_bias)


PRECISE = lax.Precision.HIGHEST
EPSILON = 1e-05
MASKED_SCORE = -1000000000.0

@jax.custom_vjp
def low(v):
    return lax.optimization_barrier(v.astype(jnp.bfloat16)).astype(jnp.float32)

@jax.custom_vjp
def low_back(v):
    return v

def low_keep(v):
    return (low(v), None)

def low_pass(kept, grad):
    return (grad,)

def back_keep(v):
    return (v, None)

def back_low(kept, grad):
    return (low(grad),)
low.defvjp(low_keep, low_pass)
low_back.defvjp(back_keep, back_low)

def rounded_both(value):
    return low_back(low(value))

def product(left, right):
    return jnp.dot(left, right, precision=PRECISE, preferred_element_type=jnp.float32)

def layer_norm(value, gain, shift):
    average = lax.optimization_barrier(jnp.mean(value, axis=-1, keepdims=True))
    centered = value - average
    spread = lax.optimization_barrier(jnp.mean(centered * centered, axis=-1, keepdims=True))
    return centered * lax.rsqrt(spread + EPSILON) * gain + shift

def affine(early, late):
    return (early[0] * late[0], late[0] * early[1] + late[1])

def attend(q_block, keys, values, seg_rows, seg_keys):
    scores = jnp.einsum('qhd,khd->hqk', q_block, keys, precision=PRECISE) * HD ** (-0.5)
    scores = jnp.where((seg_rows[:, None] == seg_keys[None, :])[None], scores, MASKED_SCORE)
    scores = low_back(scores)
    highest = lax.optimization_barrier(jnp.max(scores, axis=-1, keepdims=True))
    weights = jnp.exp(scores - highest)
    weights = weights / lax.optimization_barrier(jnp.sum(weights, axis=-1, keepdims=True))
    mixed = jnp.einsum('hqk,khd->qhd', low(weights), values, precision=PRECISE)
    return mixed.reshape(q_block.shape[0], HEADS * HD)

def attention(queries, keys, values, segment_ids):
    q_rows = min(512, LEN)
    blocks = LEN // q_rows

    def per_sequence(item):
        seq_q, seq_k, seq_v, seq_seg = item

        def per_block(block):
            return attend(block[0], seq_k, seq_v, block[1], seq_seg)
        mixed = lax.map(jax.checkpoint(per_block), (seq_q.reshape(blocks, q_rows, HEADS, HD), seq_seg.reshape(blocks, q_rows)))
        return mixed.reshape(LEN, D)
    shaped = (N_FSDP, LEN, HEADS, HD)
    result = lax.map(per_sequence, (queries.reshape(shaped), keys.reshape(shaped), values.reshape(shaped), segment_ids))
    return result.reshape(TOKENS, D)

def recurrence(chars, w_gru, gru_bias, keep_up, keep_down):
    proj = low_back(product(low(chars), w_gru.reshape(D, 4 * H))).reshape(-1, 4, H)
    gate_up = jax.nn.sigmoid(proj[:, 0] + gru_bias[0])
    gate_down = jax.nn.sigmoid(proj[:, 2] + gru_bias[1])
    shaped = (N_FSDP, -1, H)
    factor_up = ((1.0 - gate_up) * keep_up).reshape(shaped)
    factor_down = ((1.0 - gate_down) * keep_down).reshape(shaped)
    term_up = (gate_up * proj[:, 1]).reshape(shaped)
    term_down = (gate_down * proj[:, 3]).reshape(shaped)
    hidden_up = lax.associative_scan(affine, (factor_up, term_up), axis=1)[1]
    hidden_down = lax.associative_scan(affine, (factor_down, term_down), axis=1, reverse=True)[1]
    return jnp.concatenate([hidden_up.reshape(-1, H), hidden_down.reshape(-1, H)], axis=1)

def layer(tokens, chars, segment_ids, owner, counts, keep_up, keep_down, w_qkv, w_out, w_up, w_down, w_gru, gru_bias, w_tok, w_char, w_conv, gains, shifts):
    qkv = rounded_both(product(low(tokens), w_qkv.reshape(D, 3 * D))).reshape(-1, 3, D)
    mixed = rounded_both(attention(qkv[:, 0], qkv[:, 1], qkv[:, 2], segment_ids))
    first = layer_norm(tokens + low_back(product(mixed, w_out)), gains[0], shifts[0])
    pre_act = low_back(product(low(first), w_up))
    activated = jax.nn.gelu(pre_act, approximate=False)
    second = layer_norm(first + low_back(product(low(activated), w_down)), gains[1], shifts[1])
    hidden = recurrence(chars, w_gru, gru_bias, keep_up, keep_down)
    pooled = jax.ops.segment_sum(low(hidden), owner, num_segments=TOKENS) / counts[:, None]
    part_tok = low_back(product(low(second), w_tok))
    part_chr = low_back(product(low(pooled), w_char.reshape(2 * H, D)))
    joined = low(jnp.concatenate([part_tok, part_chr], axis=1)).reshape(N_FSDP, LEN, 2 * D)
    padded = jnp.pad(joined, ((0, 0), (1, 1), (0, 0)))
    kernel = w_conv.reshape(3, 2 * D, 2 * D)
    convolved = jnp.zeros((TOKENS, 2 * D), jnp.float32)
    for offset in range(3):
        convolved = convolved + product(padded[:, offset:offset + LEN].reshape(TOKENS, 2 * D), kernel[offset])
    convolved = low_back(convolved)
    tokens_new = layer_norm(second + convolved[:, :D], gains[2], shifts[2])
    chars_new = layer_norm(chars + convolved[:, D:][owner], gains[3], shifts[3])
    return (tokens_new, chars_new)

def reference(tokens_in, chars_in, segment_ids, char_counts, valid, teacher_tokens, teacher_chars, w_qkv, w_out, w_up, w_down, w_gru, gru_bias, w_tok, w_char, w_conv, ln_gain, ln_bias):
    starts = jnp.cumsum(char_counts, axis=1) - char_counts
    places = jnp.arange(CHAR_DEV, dtype=jnp.int32)
    local = lax.optimization_barrier(jnp.sum((starts[:, :, None] <= places[None, None, :]).astype(jnp.int32), axis=1)) - 1
    offsets = jnp.arange(N_FSDP * N_CONTEXT, dtype=jnp.int32)[:, None] * TOK_DEV
    owner = (local + offsets).reshape(-1).astype(jnp.int32)
    counts = char_counts.reshape(-1).astype(jnp.float32)
    char_seg = segment_ids.reshape(-1)[owner].reshape(N_FSDP, -1)
    same = (char_seg[:, 1:] == char_seg[:, :-1]).astype(jnp.float32)
    border = jnp.zeros((N_FSDP, 1), jnp.float32)
    keep_up = jnp.concatenate([border, same], axis=1).reshape(-1, 1)
    keep_down = jnp.concatenate([same, border], axis=1).reshape(-1, 1)
    valid_tok = valid.reshape(-1).astype(jnp.float32)
    valid_chr = valid_tok[owner]
    target_tok = teacher_tokens.astype(jnp.float32)
    target_chr = teacher_chars.astype(jnp.float32)

    def objective(tokens, chars, wq, wo, wu, wd, wg, gbias, wt, wc, wv, gains, shifts):
        for index in range(LAYERS):
            tokens, chars = layer(tokens, chars, segment_ids, owner, counts, keep_up, keep_down, wq[index], wo[index], wu[index], wd[index], wg[index], gbias[index], wt[index], wc[index], wv[index], gains[index], shifts[index])
        diff_tok = tokens - target_tok
        diff_chr = chars - target_chr
        total = 0.5 * jnp.sum(valid_tok[:, None] * diff_tok * diff_tok) + 0.5 * jnp.sum(valid_chr[:, None] * diff_chr * diff_chr)
        return (total, (tokens, chars))
    total, backward, outputs = jax.vjp(objective, tokens_in.astype(jnp.float32), chars_in.astype(jnp.float32), w_qkv.astype(jnp.float32), w_out.astype(jnp.float32), w_up.astype(jnp.float32), w_down.astype(jnp.float32), w_gru.astype(jnp.float32), gru_bias, w_tok.astype(jnp.float32), w_char.astype(jnp.float32), w_conv.astype(jnp.float32), ln_gain, ln_bias, has_aux=True)
    grads = backward(jnp.ones_like(total))
    loss = total / jnp.sum(valid_tok)
    return (outputs[0], outputs[1], loss, grads[0], grads[1], grads[2], grads[3], grads[4], grads[5], grads[6], grads[7], grads[8], grads[9], grads[10], grads[11], grads[12])
```

```python
import functools

import jax
import jax.numpy as jnp
from jax import lax
from jax.experimental import pallas as pl
from jax.experimental.pallas import tpu as pltpu
from jax.sharding import PartitionSpec as P

HD = 64
EPSILON = 1e-05
MASKED_SCORE = -1000000000.0
BF = jnp.bfloat16
F32 = jnp.float32
Z = "fsdp"
C = "context"
T = "tensor"
ROOM = 56 * 1024 * 1024


def dot(a, b, ca=1, cb=0):
    return lax.dot_general(a, b, (((ca,), (cb,)), ((), ())), preferred_element_type=F32)


def swap(x, axis, bit):
    size = lax.axis_size(axis)
    return lax.ppermute(x, axis, [(i, i ^ bit) for i in range(size)])


def turn(x, axis, k):
    size = lax.axis_size(axis)
    return lax.ppermute(x, axis, [(i, (i + k) % size) for i in range(size)])


def core_sum(x):
    return x + swap(x, T, 1)


def own_part(x, count, index, dim=0):
    width = x.shape[dim] // count
    return lax.dynamic_slice_in_dim(x, index * width, width, axis=dim)


def ordered(mine, other, first):
    return jnp.where(first, mine, other), jnp.where(first, other, mine)


def core_join(x, dim):
    other = swap(x, T, 1)
    low, high = ordered(x, other, lax.axis_index(T) == 0)
    return jnp.concatenate([low, high], axis=dim)


def assemble_kernel(nz, q, refs, out_ref, sems):
    z = lax.axis_index(Z)
    c = lax.axis_index(C)
    copies = []
    col = 0
    k = 0
    for quad, (b0, b1) in zip(refs, ((1, 2), (2, 1))):
        width = quad[0].shape[-1]
        for ref, mask in zip(quad, (0, b0, b1, b0 ^ b1)):
            for s in range(nz):
                zz = lax.rem(z - s + nz, nz)
                cc = jnp.bitwise_xor(c, mask)
                row = pl.multiple_of((zz * 4 + cc) * q, 16)
                cp = pltpu.make_async_copy(
                    ref.at[s], out_ref.at[pl.ds(row, q), pl.ds(col, width)], sems.at[k]
                )
                cp.start()
                copies.append(cp)
                k += 1
        col += width
    for cp in copies:
        cp.wait()


def assemble(nz, q, quads):
    n = sum(quad[0].shape[-1] for quad in quads)

    def kernel(*refs):
        ins = refs[:8]
        assemble_kernel(nz, q, (ins[:4], ins[4:8]), refs[8], refs[9])

    return pl.pallas_call(
        kernel,
        out_shape=jax.ShapeDtypeStruct((nz * 4 * q, n), BF),
        in_specs=[pl.BlockSpec(memory_space=pl.ANY)] * 8,
        out_specs=pl.BlockSpec(memory_space=pl.ANY),
        scratch_shapes=[pltpu.SemaphoreType.DMA((8 * nz,))],
        name="assemble",
    )(*quads[0], *quads[1])


def gather_rows(shard):
    nz = lax.axis_size(Z)
    rows, n = shard.shape
    q = rows // 4
    if q % 16:
        return lax.all_gather(shard, Z, axis=0, tiled=True)
    piece = own_part(shard, 4, lax.axis_index(C))
    got = [piece] + [turn(piece, Z, k) for k in range(1, nz)]
    half = n // 256 * 128
    quads = []
    for cut, (b0, b1) in ((slice(half), (1, 2)), (slice(half, n), (2, 1))):
        a = jnp.stack([g[:, cut] for g in got])
        b = swap(a, C, b0)
        both = swap(jnp.concatenate([a, b]), C, b1)
        quads.append((a, b, both[:nz], both[nz:]))
    return assemble(nz, q, quads)


def scatter_rows(full):
    nz = lax.axis_size(Z)
    z = lax.axis_index(Z)
    c = lax.axis_index(C)
    rows, n = full.shape
    q = rows // (4 * nz)
    half = n // 256 * 128
    bits = (jnp.bitwise_and(c, 1), jnp.right_shift(c, 1))
    outs = []
    for cut, (b0, b1) in ((slice(half), (1, 2)), (slice(half, n), (2, 1))):
        x = full[:, cut]
        span = x.shape[1]
        x = x.reshape(nz, 2, 2, q, span)
        ax0, ax1 = (2, 1) if b0 == 1 else (1, 2)
        i0, i1 = (bits[0], bits[1]) if b0 == 1 else (bits[1], bits[0])
        keep = lax.dynamic_slice_in_dim(x, i0, 1, axis=ax0)
        send = lax.dynamic_slice_in_dim(x, 1 - i0, 1, axis=ax0)
        x = keep + swap(send, C, b0)
        keep = lax.dynamic_slice_in_dim(x, i1, 1, axis=ax1)
        send = lax.dynamic_slice_in_dim(x, 1 - i1, 1, axis=ax1)
        x = (keep + swap(send, C, b1)).reshape(nz, q, span)
        total = lax.dynamic_index_in_dim(x, z, 0, keepdims=False).astype(F32)
        for k in range(1, nz):
            to = lax.dynamic_index_in_dim(x, lax.rem(z + k, nz), 0, keepdims=False)
            total = total + turn(to, Z, k).astype(F32)
        piece = total.astype(BF)
        other = swap(piece, C, b1)
        pair = jnp.stack([piece, other])
        rest = swap(pair, C, b0)
        parts = jnp.stack([pair[0], rest[0], pair[1], rest[1]])
        index = [jnp.bitwise_xor(c, j) for j in range(4)]
        if b0 == 2:
            index = [jnp.array([0, 2, 1, 3])[i] for i in index]
        outs.append(
            jnp.concatenate([lax.dynamic_index_in_dim(parts, i, 0, keepdims=False) for i in index])
        )
    return jnp.concatenate(outs, axis=1).astype(F32)


def gather_z(x):
    nz = lax.axis_size(Z)
    return jnp.stack([x] + [turn(x, Z, k) for k in range(1, nz)])


def to_z(x):
    nz = lax.axis_size(Z)
    z = lax.axis_index(Z)
    got = [lax.dynamic_index_in_dim(x, z, 0, keepdims=False)]
    for k in range(1, nz):
        to = lax.dynamic_index_in_dim(x, lax.rem(z + k, nz), 0, keepdims=False)
        got.append(turn(to, Z, k))
    return got


def by_source(got):
    nz = len(got)
    z = lax.axis_index(Z)
    stacked = jnp.stack(got)
    return [
        lax.dynamic_index_in_dim(stacked, lax.rem(z - s + nz, nz), 0, keepdims=False)
        for s in range(nz)
    ]


def scan_kernel(fu_ref, tu_ref, fd_ref, td_ref, cu_ref, hu_ref, cd_ref, hd_ref):
    n = fu_ref.shape[0]
    rows = lax.broadcasted_iota(jnp.int32, fu_ref.shape, 0)
    a, b = fu_ref[...], tu_ref[...]
    e, f = fd_ref[...], td_ref[...]
    step = 1
    while step < n:
        has = rows >= step
        pa = jnp.where(has, pltpu.roll(a, step, 0), 1.0)
        pb = jnp.where(has, pltpu.roll(b, step, 0), 0.0)
        b = b + a * pb
        a = a * pa
        has = rows < n - step
        pe = jnp.where(has, pltpu.roll(e, n - step, 0), 1.0)
        pf = jnp.where(has, pltpu.roll(f, n - step, 0), 0.0)
        f = f + e * pf
        e = e * pe
        step *= 2
    cu_ref[...], hu_ref[...], cd_ref[...], hd_ref[...] = a, b, e, f


def scans(fu, tu, fd, td):
    shape = jax.ShapeDtypeStruct(fu.shape, F32)
    cu, hu, cd, hd = pl.pallas_call(
        scan_kernel,
        out_shape=(shape,) * 4,
        compiler_params=pltpu.CompilerParams(vmem_limit_bytes=ROOM),
        name="scan",
    )(fu, tu, fd, td)
    c = lax.axis_index(C)
    ends = jnp.stack([cu[-1], hu[-1], cd[0], hd[0]])
    every = jnp.stack([ends, swap(ends, C, 1), swap(ends, C, 2), swap(ends, C, 3)])
    up = jnp.zeros_like(fu[0])
    down = jnp.zeros_like(fu[0])
    for j in range(4):
        part = lax.dynamic_index_in_dim(every, jnp.bitwise_xor(c, j), 0, keepdims=False)
        up = jnp.where(j < c, part[0] * up + part[1], up)
        j = 3 - j
        part = lax.dynamic_index_in_dim(every, jnp.bitwise_xor(c, j), 0, keepdims=False)
        down = jnp.where(j > c, part[2] * down + part[3], down)
    return hu + cu * up[None, :], up, hd + cd * down[None, :], down


def norm_rows(inputs, gain, shift):
    average = jnp.mean(inputs, axis=-1, keepdims=True)
    centered = inputs - average
    spread = jnp.mean(centered * centered, axis=-1, keepdims=True)
    inverse = lax.rsqrt(spread + EPSILON)
    normed = centered * inverse
    return (normed * gain + shift, normed, inverse)


def norm_back(upstream, normed, inverse, gain):
    scaled = upstream * gain
    mean_one = jnp.mean(scaled, axis=-1, keepdims=True)
    mean_two = jnp.mean(scaled * normed, axis=-1, keepdims=True)
    return (
        inverse * (scaled - mean_one - normed * mean_two),
        jnp.sum(upstream * normed, axis=0),
        jnp.sum(upstream, axis=0),
    )


def heads_of(matrix):
    return matrix.reshape(matrix.shape[0], matrix.shape[1] // HD, HD)


def einsum(spec, a, b):
    return jnp.einsum(spec, a, b, preferred_element_type=F32)


def gelu_slope(pre_act):
    cdf_part = 0.5 * (1.0 + lax.erf(pre_act * 0.7071067811865476))
    pdf_part = jnp.exp(-0.5 * pre_act * pre_act) * 0.3989422804014327
    return cdf_part + pre_act * pdf_part


def two_terms(x):
    high = x.astype(BF)
    return high, (x - high.astype(F32)).astype(BF)


def edges(x):
    size = lax.axis_size(C)
    up = [(i, i + 1) for i in range(size - 1)]
    down = [(j, i) for i, j in up]
    before = lax.ppermute(x[:, -1:], C, up)
    after = lax.ppermute(x[:, :1], C, down)
    return before, after


def body(
    tokens_in, chars_in, segment_ids, char_counts, valid, teacher_tokens, teacher_chars,
    w_qkv, w_out, w_up, w_down, w_gru, gru_bias, w_tok, w_char, w_conv, ln_gain, ln_bias,
):
    nz = lax.axis_size(Z)
    z = lax.axis_index(Z)
    c = lax.axis_index(C)
    t = lax.axis_index(T)
    first_core = t == 0
    rows, width = tokens_in.shape
    chars = chars_in.shape[0]
    half = width // 2
    units = gru_bias.shape[2]
    shard = w_qkv.shape[1]
    hidden = w_up.shape[2]

    w_a = gather_rows(jnp.concatenate([w_qkv[0].reshape(shard, -1), w_gru[0].reshape(shard, -1)], axis=1))
    w_small = lax.all_gather(
        jnp.concatenate([w_out[0].T, w_char[0].reshape(-1, shard).T, w_tok[0]], axis=1), Z, axis=0, tiled=True
    )
    mine = own_part(tokens_in, 2, t)
    others = jnp.stack([swap(mine, C, m) for m in (1, 2, 3)])
    others = core_join(others, 1)
    x_all = jnp.concatenate([tokens_in, others.reshape(3 * rows, width)])
    w_b = gather_rows(jnp.concatenate([w_up[0], w_down[0].T], axis=1))
    w_query = w_a[:, : 3 * half]
    w_recur = w_a[:, 3 * half :]
    w_mix_t = w_small[:, :half]
    w_charp_t = w_small[:, half : 2 * half]
    w_token = w_small[:, 2 * half :]
    w_upper = w_b[:, :hidden]
    w_lower_t = w_b[:, hidden:]

    ctx_size = lax.axis_size(C)
    seq_len = segment_ids.shape[1]
    offset_here = c * rows
    seg_full = segment_ids[0]
    seg_here = lax.dynamic_slice_in_dim(seg_full, offset_here, rows)
    seg_keys = jnp.concatenate(
        [lax.dynamic_slice_in_dim(seg_full, jnp.bitwise_xor(c, m) * rows, rows) for m in range(4)]
    )
    counts = char_counts[0]
    ends = jnp.cumsum(counts)
    starts = ends - counts
    places = jnp.arange(chars, dtype=jnp.int32)
    pick = jnp.logical_and(starts[:, None] <= places[None, :], places[None, :] < ends[:, None])
    select = pick.astype(BF)
    lengths = counts.astype(F32)[:, None]
    valid_tok = valid[0].astype(F32)
    char_seg = jnp.sum(jnp.where(pick, seg_here[:, None], 0), axis=0)
    valid_chr = jnp.sum(jnp.where(pick, valid_tok[:, None], 0.0), axis=0)
    prev_seg = seg_full[jnp.maximum(offset_here - 1, 0)]
    next_seg = seg_full[jnp.minimum(offset_here + rows, seq_len - 1)]
    first_keep = jnp.logical_and(c > 0, prev_seg == char_seg[0])
    last_keep = jnp.logical_and(c < ctx_size - 1, next_seg == char_seg[-1])
    same = char_seg[1:] == char_seg[:-1]
    keep_up = jnp.concatenate([first_keep[None], same]).astype(F32)[:, None]
    keep_down = jnp.concatenate([same, last_keep[None]]).astype(F32)[:, None]

    gains, shifts, gate_bias = ln_gain[0], ln_bias[0], gru_bias[0]
    stream_tok = tokens_in.astype(F32)
    stream_chr = chars_in.astype(F32)

    proj = dot(chars_in, w_recur)
    p_up, p_down = proj[:, units : 2 * units], proj[:, 3 * units :]
    gate_up = jax.nn.sigmoid(proj[:, :units] + gate_bias[0])
    gate_down = jax.nn.sigmoid(proj[:, 2 * units : 3 * units] + gate_bias[1])
    factor_up = (1.0 - gate_up) * keep_up
    factor_down = (1.0 - gate_down) * keep_down
    hidden_up, entry_up, hidden_down, entry_down = scans(
        factor_up, gate_up * p_up, factor_down, gate_down * p_down
    )
    hidden_low = jnp.concatenate([hidden_up, hidden_down], axis=1).astype(BF)
    pooled_low = (dot(select, hidden_low) / lengths).astype(BF)
    char_part = dot(pooled_low, w_charp_t, 1, 1)
    low, high = char_part[:, :half], char_part[:, half:]
    keep, send = ordered(low, high, first_core)
    fb = (keep + swap(send, T, 1)).astype(BF)
    fb_all = gather_z(fb)

    queries = dot(tokens_in, w_query[:, :half]).astype(BF)
    kv = dot(x_all, w_query[:, half:]).astype(BF)
    keys, values = kv[:, :half], kv[:, half:]
    allowed = (seg_here[:, None] == seg_keys[None, :])[None]
    scale = HD ** (-0.5)
    scores = jnp.where(allowed, einsum("qhd,khd->hqk", heads_of(queries), heads_of(keys)) * scale, MASKED_SCORE)
    highest = jnp.max(scores, axis=-1, keepdims=True)
    log_total = highest + jnp.log(jnp.sum(jnp.exp(scores - highest), axis=-1, keepdims=True))
    probs_low = jnp.exp(scores - log_total).astype(BF)
    mixed_low = einsum("hqk,khd->qhd", probs_low, heads_of(values)).reshape(rows, -1).astype(BF)
    attended = core_sum(dot(mixed_low, w_mix_t, 1, 1))
    first, normed_one, inverse_one = norm_rows(stream_tok + attended, gains[0], shifts[0])
    first_low = first.astype(BF)
    pre_act = dot(first_low, w_upper)
    act_low = jax.nn.gelu(pre_act, approximate=False).astype(BF)
    ffn_out = core_sum(dot(act_low, w_lower_t, 1, 1))
    second, normed_two, inverse_two = norm_rows(first + ffn_out, gains[1], shifts[1])
    second_low = second.astype(BF)
    fa = dot(second_low, w_token).astype(BF)
    fa_all = gather_z(fa)

    u_all = jnp.concatenate([fa_all, fb_all], axis=2)
    u_before, u_after = edges(u_all)
    cols = w_conv.shape[-1]
    kernel = w_conv[0].reshape(3, width, cols)
    u_pad = jnp.concatenate([u_before, u_all, u_after], axis=1)
    u_taps = [u_pad[:, m : m + rows].reshape(nz * rows, width) for m in range(3)]
    conv = sum(dot(u_taps[m], kernel[m]) for m in range(3)).reshape(nz, 2, rows // 2, cols)
    keep = lax.dynamic_index_in_dim(conv, t, 1, keepdims=False)
    send = lax.dynamic_index_in_dim(conv, 1 - t, 1, keepdims=False)
    conv = (keep + swap(send, T, 1)).astype(BF)
    got = [conv[0]] + [turn(conv[k], Z, nz - k) for k in range(1, nz)]
    stacked = jnp.stack(got)
    y_half = jnp.concatenate(
        [lax.dynamic_index_in_dim(stacked, lax.rem(s - z + nz, nz), 0, keepdims=False) for s in range(nz)], axis=1
    )
    y = core_join(y_half, 0)

    out_tok, normed_three, inverse_three = norm_rows(second + y[:, :width].astype(F32), gains[2], shifts[2])
    spread_chr = dot(select, y[:, width:], 0, 0)
    out_chr, normed_four, inverse_four = norm_rows(stream_chr + spread_chr, gains[3], shifts[3])

    diff_tok = out_tok - teacher_tokens.astype(F32)
    diff_chr = out_chr - teacher_chars.astype(F32)
    grad_tok = valid_tok[:, None] * diff_tok
    grad_chr = valid_chr[:, None] * diff_chr
    part_total = 0.5 * jnp.sum(grad_tok * diff_tok) + 0.5 * jnp.sum(grad_chr * diff_chr)
    count_here = jnp.sum(valid_tok)

    d_res_four, gain_four, shift_four = norm_back(grad_chr, normed_four, inverse_four, gains[3])
    d_res_three, gain_three, shift_three = norm_back(grad_tok, normed_three, inverse_three, gains[2])
    hi, lo = two_terms(d_res_four)
    d_conv = jnp.concatenate([d_res_three, dot(select, hi) + dot(select, lo)], axis=1).astype(BF)
    d_mine = own_part(d_conv, 2, t)
    slices = d_mine.reshape(rows // 2, nz, cols).transpose(1, 0, 2)
    dy_all = core_join(jnp.stack(to_z(slices)), 1)
    dy_before, dy_after = edges(dy_all)
    dy_pad = jnp.concatenate([dy_before, dy_all, dy_after], axis=1)
    du_parts = sum(
        dot(dy_pad[:, 2 - m : 2 - m + rows].reshape(nz * rows, cols), kernel[m], 1, 1) for m in range(3)
    ).astype(BF).reshape(nz, rows, width)
    du_tok, du_chr = du_parts[:, :, :half], du_parts[:, :, half:]

    def back_to_source(parts):
        total = parts[0].astype(F32)
        for k in range(1, nz):
            total = total + turn(parts[k], Z, nz - k).astype(F32)
        return total.astype(BF)

    dfa = back_to_source(du_tok)
    dfb = back_to_source(du_chr)
    dy_flat = dy_all.reshape(nz * rows, cols)
    grad_kernel = jnp.stack([dot(u_taps[m], dy_flat, 0, 0) for m in range(3)]).astype(BF)
    grad_kernel = lax.psum(grad_kernel, C).astype(F32)

    grad_token = dot(second_low, dfa, 0, 0)
    dfb_full = core_join(dfb, 1)
    grad_charp_t = dot(dfb_full, pooled_low, 0, 0)
    d_pooled = dot(dfb_full, w_charp_t) / lengths
    hi, lo = two_terms(d_pooled)
    d_hidden = dot(select, hi, 0, 0) + dot(select, lo, 0, 0)
    d_hid_up, d_hid_down = d_hidden[:, :units], d_hidden[:, units:]
    mu_down, enter_down, mu_up, enter_up = scans(
        factor_down, factor_down * d_hid_down, factor_up, factor_up * d_hid_up
    )
    lam_up = d_hid_up + jnp.concatenate([mu_up[1:], enter_up[None, :]], axis=0)
    lam_down = d_hid_down + jnp.concatenate([enter_down[None, :], mu_down[:-1]], axis=0)
    prev_up = jnp.concatenate([entry_up[None, :], hidden_up[:-1]], axis=0)
    next_down = jnp.concatenate([hidden_down[1:], entry_down[None, :]], axis=0)
    d_gate_up = lam_up * (p_up - keep_up * prev_up) * gate_up * (1.0 - gate_up)
    d_gate_down = lam_down * (p_down - keep_down * next_down) * gate_down * (1.0 - gate_down)
    d_proj = jnp.concatenate([d_gate_up, lam_up * gate_up, d_gate_down, lam_down * gate_down], axis=1).astype(BF)
    grad_bias = jnp.stack([jnp.sum(d_gate_up, axis=0), jnp.sum(d_gate_down, axis=0)])
    grad_recur = dot(chars_in, d_proj, 0, 0)
    d_chr_in = d_res_four + core_sum(dot(d_proj, w_recur, 1, 1))

    d_second = d_res_three + core_sum(dot(dfa, w_token, 1, 1))
    d_res_two, gain_two, shift_two = norm_back(d_second, normed_two, inverse_two, gains[1])
    d_ffn = d_res_two.astype(BF)
    grad_lower_t = dot(d_ffn, act_low, 0, 0)
    d_pre = (dot(d_ffn, w_lower_t) * gelu_slope(pre_act)).astype(BF)
    grad_upper = dot(first_low, d_pre, 0, 0)
    d_first = d_res_two + core_sum(dot(d_pre, w_upper, 1, 1))
    g_b = scatter_rows(jnp.concatenate([grad_upper.astype(BF), grad_lower_t.astype(BF)], axis=1))
    d_res_one, gain_one, shift_one = norm_back(d_first, normed_one, inverse_one, gains[0])
    d_att = d_res_one.astype(BF)
    grad_mix_t = dot(d_att, mixed_low, 0, 0)
    g_small = scatter_rows(
        jnp.concatenate([grad_mix_t, grad_charp_t, grad_token, grad_recur], axis=1).astype(BF)
    )
    d_mixed = dot(d_att, w_mix_t).astype(BF)
    probs = jnp.exp(scores - log_total)
    d_probs = einsum("qhd,khd->hqk", heads_of(d_mixed), heads_of(values))
    delta = jnp.sum(probs * d_probs, axis=-1, keepdims=True)
    d_scores = (probs * (d_probs - delta)).astype(BF)
    d_query = (einsum("hqk,khd->qhd", d_scores, heads_of(keys)) * scale).reshape(rows, half)
    d_key_all = (einsum("hqk,qhd->khd", d_scores, heads_of(queries)) * scale).reshape(-1, half)
    d_value_all = einsum("hqk,qhd->khd", probs_low, heads_of(d_mixed)).reshape(-1, half)
    d_kv = jnp.concatenate([d_key_all, d_value_all], axis=1).reshape(4, rows, width)
    d_kv_low = d_kv.astype(BF)
    total = d_kv[0]
    for m in (1, 2, 3):
        total = total + swap(d_kv_low[m], C, m).astype(F32)
    d_qkv = jnp.concatenate([d_query, total], axis=1).astype(BF)
    grad_query = dot(tokens_in, d_qkv, 0, 0)
    d_tok_in = d_res_one + core_sum(dot(d_qkv, w_query, 1, 1))
    g_query = scatter_rows(grad_query.astype(BF))

    scalars = jnp.zeros((width,), F32).at[0].set(part_total).at[1].set(count_here)
    bias_row = jnp.pad(grad_bias.reshape(-1), (0, width - 2 * units))
    packed = jnp.stack([
        gain_one, gain_two, gain_three, gain_four, shift_one, shift_two, shift_three, shift_four, scalars, bias_row,
    ])
    for bit in (1, 2):
        packed = packed + swap(packed, C, bit)
    bit = 1
    while bit < nz:
        packed = packed + swap(packed, Z, bit)
        bit *= 2
    loss = packed[8, 0] / packed[8, 1]
    bias_total = packed[9, : 2 * units].reshape(1, 2, units)
    g_mix, g_char, g_tok, g_gru = jnp.split(g_small, [half, 2 * half, 3 * half], axis=1)
    return (
        out_tok,
        out_chr,
        loss,
        d_tok_in,
        d_chr_in,
        g_query.reshape(w_qkv.shape),
        g_mix.T[None],
        g_b[:, :hidden][None],
        g_b[:, hidden:].T[None],
        g_gru.reshape(w_gru.shape),
        bias_total,
        g_tok[None],
        g_char.T.reshape(w_char.shape),
        grad_kernel.reshape(w_conv.shape),
        packed[None, :4],
        packed[None, 4:8],
    )


def solution(mesh):
    tok = P((Z, C), None)
    seq = P(Z, None)
    placed = (
        tok, tok, seq, tok, P(Z, C), tok, tok,
        P(None, Z, None, T), P(None, T, Z), P(None, Z, T), P(None, T, Z), P(None, Z, None, T),
        P(None, None, T), P(None, Z, T), P(None, None, T, Z), P(None, None, None, T, Z), P(), P(),
    )
    given = (
        tok, tok, P(), tok, tok,
        P(None, Z, None, T), P(None, T, Z), P(None, Z, T), P(None, T, Z), P(None, Z, None, T),
        P(None, None, T), P(None, Z, T), P(None, None, T, Z), P(None, None, None, T, Z), P(), P(),
    )
    return jax.shard_map(body, mesh=mesh, in_specs=placed, out_specs=given, check_vma=False)
```

```python
import functools

import jax
import jax.numpy as jnp
from jax import lax
from jax.experimental import pallas as pl
from jax.experimental.pallas import tpu as pltpu
from jax.sharding import PartitionSpec as P

HD = 64
EPSILON = 1e-05
MASKED_SCORE = -1000000000.0
BF = jnp.bfloat16
F32 = jnp.float32
Z = "fsdp"
C = "context"
T = "tensor"
ROOM = 56 * 1024 * 1024


def dot(a, b, ca=1, cb=0):
    return lax.dot_general(a, b, (((ca,), (cb,)), ((), ())), preferred_element_type=F32)


def swap(x, axis, bit):
    size = lax.axis_size(axis)
    return lax.ppermute(x, axis, [(i, i ^ bit) for i in range(size)])


def turn(x, axis, k):
    size = lax.axis_size(axis)
    return lax.ppermute(x, axis, [(i, (i + k) % size) for i in range(size)])


def core_sum(x):
    return x + swap(x, T, 1)


def own_part(x, count, index, dim=0):
    width = x.shape[dim] // count
    return lax.dynamic_slice_in_dim(x, index * width, width, axis=dim)


def ordered(mine, other, first):
    return jnp.where(first, mine, other), jnp.where(first, other, mine)


def core_join(x, dim):
    other = swap(x, T, 1)
    low, high = ordered(x, other, lax.axis_index(T) == 0)
    return jnp.concatenate([low, high], axis=dim)


def after(x, *deps):
    return lax.optimization_barrier((x, deps))[0]


def whole(shape, dtype):
    return jax.ShapeDtypeStruct(shape, dtype)


def call(kernel, outs, name, scratch=()):
    return pl.pallas_call(
        kernel,
        out_shape=outs,
        scratch_shapes=list(scratch),
        compiler_params=pltpu.CompilerParams(vmem_limit_bytes=ROOM),
        cost_estimate=pl.CostEstimate(flops=1, bytes_accessed=1, transcendentals=0),
        name=name,
    )


def context_quarter(shard):
    return own_part(shard, 4, lax.axis_index(C))


def round_context(stack, sides, widths, wait_for=()):
    n = stack.shape[2]
    half = n // 256 * 128
    cuts = (slice(half), slice(half, n)) if len(sides) == 2 else (slice(n),)
    firsts = [stack[:, :, cut] for cut in cuts]
    if wait_for:
        firsts = [after(a, *wait_for) for a in firsts]
    nears = [swap(a, C, b0) for a, (b0, _) in zip(firsts, sides)]
    fars = [swap(jnp.concatenate([a, b]), C, b1) for a, b, (_, b1) in zip(firsts, nears, sides)]
    return assemble(list(zip(firsts, nears, fars)), sides, widths), tuple(nears)


def assemble(quads, sides, widths):
    nz, q = quads[0][0].shape[:2]
    starts = [sum(widths[:i]) for i in range(len(widths))]

    def kernel(*refs):
        outs = refs[3 * len(sides) :]
        c = lax.axis_index(C)
        col = 0
        for side, (b0, b1) in enumerate(sides):
            own, near, far = refs[3 * side : 3 * side + 3]
            width = own.shape[-1]
            spans = []
            for out, begin, size in zip(outs, starts, widths):
                low, high = max(begin, col), min(begin + size, col + width)
                if low < high:
                    spans.append((out, slice(low - col, high - col), slice(low - begin, high - begin)))
            for ref, base, mask in ((own, 0, 0), (near, 0, b0), (far, 0, b1), (far, nz, b0 ^ b1)):
                for zz in range(nz):
                    row = pl.multiple_of((zz * 4 + jnp.bitwise_xor(c, mask)) * q, 16)
                    for out, src, dst in spans:
                        out[pl.ds(row, q), dst] = ref[base + zz, :, src]
            col += width

    shapes = tuple(whole((nz * 4 * q, w), BF) for w in widths)
    return call(kernel, shapes, "assemble")(*[x for quad in quads for x in quad])


BOTH = ((1, 2), (2, 1))


def sent_apart(products, b0, b1):
    rows, width = products[0][0].shape[1], products[0][1].shape[1]
    arrays = []
    places = []
    for pair in products:
        spots = []
        for x in pair:
            for i, y in enumerate(arrays):
                if y is x:
                    break
            else:
                i = len(arrays)
                arrays.append(x)
            spots.append(i)
        places.append(spots)
    count = len(arrays)

    def kernel(*refs):
        outs = refs[count:]
        c = lax.axis_index(C)
        for j, (l, r) in enumerate(places):
            part = dot(refs[l][...], refs[r][...], 0, 0).astype(BF)
            if b1 is None:
                for m in range(4):

                    @pl.when(jnp.bitwise_xor(c, j) == m)
                    def _():
                        outs[m][...] = part
            else:
                slot = (j & b1) // b1
                mine = jnp.bitwise_and(jnp.bitwise_xor(c, j), b0) == 0

                @pl.when(mine)
                def _():
                    outs[0][slot] = part

                @pl.when(jnp.logical_not(mine))
                def _():
                    outs[1][slot] = part

    if b1 is None:
        shapes = (whole((rows, width), BF),) * 4
    else:
        shapes = (whole((2, rows, width), BF),) * 2
    return call(kernel, shapes, "grads")(*arrays)


def z_split(parts):
    nz = lax.axis_size(Z)
    rows, width = parts[0].shape
    block = rows // nz

    def kernel(*refs):
        z = lax.axis_index(Z)
        for k, out in enumerate(refs[len(parts) :]):
            at = pl.ds(pl.multiple_of(lax.rem(z + k, nz) * block, 16), block)
            total = refs[0][at].astype(F32)
            for ref in refs[1 : len(parts)]:
                total = total + ref[at].astype(F32)
            out[...] = total.astype(BF)

    return call(kernel, (whole((block, width), BF),) * nz, "z_split")(*parts)


def exchange(copied, split):
    c = lax.axis_index(C)
    t = lax.axis_index(T)
    width = split.shape[1] // 4
    half = own_part(copied, 2, t, 1)
    pieces = [own_part(split, 4, jnp.bitwise_xor(c, m), 1) for m in range(4)]
    if half.shape[1] != width:
        came = [(swap(half, C, m), swap(pieces[m], C, m)) for m in (1, 2, 3)]
    else:
        rows = half.shape[0]
        came = [swap(jnp.concatenate([half, pieces[m]]), C, m) for m in (1, 2, 3)]
        came = [(x[:rows], x[rows:]) for x in came]
    halves = jnp.concatenate([a for a, _ in came])
    return jnp.concatenate([copied, core_join(halves, 1)]), jnp.concatenate([pieces[0]] + [b for _, b in came])


def last_join(parts):
    rows, width = parts[0].shape

    def kernel(*refs):
        c = lax.axis_index(C)
        for m in range(4):
            refs[4][jnp.bitwise_xor(c, m)] = refs[m][...].astype(F32)

    return call(kernel, whole((4, rows, width), F32), "join")(*parts)


def over_z(blocks):
    nz = len(blocks)
    total = blocks[0].astype(F32)
    for k in range(1, nz):
        total = total + turn(blocks[k], Z, k).astype(F32)
    return total.astype(BF)


def to_context(piece):
    return last_join([piece] + [swap(piece, C, m) for m in (1, 2, 3)])


def over_context(sent, wait_for=()):
    out = [after(x, *wait_for) for x in sent[1:]] if wait_for else sent[1:]
    return [sent[0]] + [swap(x, C, m) for m, x in zip((1, 2, 3), out)]


BESIDE = 1 << 20


def gather_beside(x, dim):
    nz = lax.axis_size(Z)
    extent = x.shape[dim]
    other = x.size // extent
    unit = 128 if dim else 16
    need = -(-BESIDE // (2 * nz * other * unit)) * unit
    if need > extent:
        pads = [(0, 0)] * x.ndim
        pads[dim] = (0, need - extent)
        x = jnp.pad(x, pads)
    return lax.slice_in_dim(lax.all_gather(x, Z), 0, extent, axis=dim + 1)


def gather_z(x):
    nz = lax.axis_size(Z)
    return jnp.stack([x] + [turn(x, Z, k) for k in range(1, nz)])


def to_z(x):
    nz = lax.axis_size(Z)
    z = lax.axis_index(Z)
    got = [lax.dynamic_index_in_dim(x, z, 0, keepdims=False)]
    for k in range(1, nz):
        to = lax.dynamic_index_in_dim(x, lax.rem(z + k, nz), 0, keepdims=False)
        got.append(turn(to, Z, k))
    return got


def by_source(got):
    nz = len(got)
    z = lax.axis_index(Z)
    stacked = jnp.stack(got)
    return [
        lax.dynamic_index_in_dim(stacked, lax.rem(z - s + nz, nz), 0, keepdims=False)
        for s in range(nz)
    ]


def shifted(x, by):
    rows = x.shape[0]
    at = lax.broadcasted_iota(jnp.int32, x.shape, 0)
    if by > 0:
        return jnp.where(at >= by, pltpu.roll(x, by, 0), 0.0)
    return jnp.where(at < rows + by, pltpu.roll(x, rows + by, 0), 0.0)


def block_of(k, nz):
    return lax.rem(lax.axis_index(Z) - k + nz, nz)


def conv_main(toks, chrs, kernel):
    nz = len(toks)
    rows, half = toks[0].shape
    cols = kernel.shape[-1]

    def run(*refs):
        c_ref, w_ref, out_ref = refs[nz:]
        for k in range(nz):
            u = jnp.concatenate([refs[k][...], c_ref[block_of(k, nz)]], axis=1)
            total = dot(u, w_ref[1])
            total = total + shifted(dot(u, w_ref[0]), 1)
            out_ref[k] = total + shifted(dot(u, w_ref[2]), -1)

    return call(run, whole((nz, rows, cols), F32), "conv")(*toks, chrs, kernel)


def conv_edges(inside, before, after_, kernel):
    nz, rows, cols = inside.shape
    half = rows // 2

    def run(in_ref, b_ref, a_ref, w_ref, keep_ref, send_ref):
        t = lax.axis_index(T)
        top = dot(b_ref[:, 0], w_ref[0])
        end = dot(a_ref[:, 0], w_ref[2])
        at = lax.broadcasted_iota(jnp.int32, (half, cols), 0)
        for k in range(nz):
            low = in_ref[k, :half] + jnp.where(at == 0, top[k : k + 1], 0.0)
            high = in_ref[k, half:] + jnp.where(at == half - 1, end[k : k + 1], 0.0)

            @pl.when(t == 0)
            def _():
                keep_ref[k] = low
                send_ref[k] = high

            @pl.when(t != 0)
            def _():
                keep_ref[k] = high
                send_ref[k] = low

    shape = whole((nz, half, cols), F32)
    return call(run, (shape, shape), "conv_edges")(inside, before, after_, kernel)


def add_split(keep, came):
    nz = keep.shape[0]

    def run(*refs):
        for k in range(nz):
            refs[2 + k][...] = (refs[0][k] + refs[1][k]).astype(BF)

    return call(run, (whole(keep.shape[1:], BF),) * nz, "add_split")(keep, came)


def side_by_side(parts, forward):
    nz = len(parts)
    rows, cols = parts[0].shape
    z = lax.axis_index(Z)
    if cols % 128:
        stacked = jnp.stack(parts)
        order = [lax.rem((s - z if forward else z - s) + nz, nz) for s in range(nz)]
        return jnp.concatenate([lax.dynamic_index_in_dim(stacked, i, 0, keepdims=False) for i in order], axis=1)

    def run(*refs):
        z = lax.axis_index(Z)
        for k in range(nz):
            s = lax.rem((z + k if forward else z - k + nz), nz)
            refs[nz][:, pl.ds(pl.multiple_of(s * cols, 128), cols)] = refs[k][...]

    return call(run, whole((rows, nz * cols), BF), "side_by_side")(*parts)


def column_slices(x, nz):
    cols = x.shape[1] // nz
    z = lax.axis_index(Z)
    return [lax.dynamic_slice_in_dim(x, lax.rem(z + k, nz) * cols, cols, axis=1) for k in range(nz)]


def row_norm(v):
    average = jnp.mean(v, axis=-1, keepdims=True)
    centered = v - average
    spread = jnp.mean(centered * centered, axis=-1, keepdims=True)
    inverse = lax.rsqrt(spread + EPSILON)
    return centered * inverse, inverse


def row_norm_back(e, n, inverse, gain):
    ge = e * gain
    one = jnp.mean(ge, axis=-1, keepdims=True)
    two = jnp.mean(ge * n, axis=-1, keepdims=True)
    return inverse * (ge - one - n * two)


def column_sum(x):
    return jnp.sum(x, axis=0, keepdims=True)


def close(second, y_mine, y_other, chars_in, teacher_tok, teacher_chr, pick, notes, marks, gains, shifts):
    rows, width = second.shape
    chars = chars_in.shape[0]
    half = rows // 2
    step = 128

    def run(
        s_ref, ym_ref, yo_ref, c_ref, tt_ref, tc_ref, pick_ref, vt_ref, vc_ref, g_ref, b_ref,
        tok_ref, chr_ref, d3_ref, d4_ref, dy_ref, stat_ref, y_ref, hi_ref, lo_ref,
    ):
        t = lax.axis_index(T)
        y_ref[pl.ds(pl.multiple_of(t * half, 16), half)] = ym_ref[...]
        y_ref[pl.ds(pl.multiple_of((1 - t) * half, 16), half)] = yo_ref[...]
        zero = jnp.zeros((1, width), F32)
        gain_sum, shift_sum, loss = zero, zero, zero
        for i in range(0, rows, step):
            at = slice(i, i + step)
            n, inverse = row_norm(s_ref[at] + y_ref[at, :width].astype(F32))
            out = n * g_ref[2:3] + b_ref[2:3]
            tok_ref[at] = out
            diff = out - tt_ref[at].astype(F32)
            e = vt_ref[at, 1:2] * diff
            loss += column_sum(e * diff)
            gain_sum += column_sum(e * n)
            shift_sum += column_sum(e)
            d3_ref[at] = row_norm_back(e, n, inverse, g_ref[2:3])
        stat_ref[0:1] = gain_sum
        stat_ref[2:3] = shift_sum
        gain_sum, shift_sum = zero, zero
        for i in range(0, chars, step):
            at = slice(i, i + step)
            spread = dot(pick_ref[:, at], y_ref[:, width:], 0, 0)
            n, inverse = row_norm(c_ref[at].astype(F32) + spread)
            out = n * g_ref[3:4] + b_ref[3:4]
            chr_ref[at] = out
            diff = out - tc_ref[at].astype(F32)
            e = vc_ref[at, 2:3] * diff
            loss += column_sum(e * diff)
            gain_sum += column_sum(e * n)
            shift_sum += column_sum(e)
            d = row_norm_back(e, n, inverse, g_ref[3:4])
            d4_ref[at] = d
            high = d.astype(BF)
            hi_ref[at] = high
            lo_ref[at] = (d - high.astype(F32)).astype(BF)
        stat_ref[1:2] = gain_sum
        stat_ref[3:4] = shift_sum
        stat_ref[4:5] = 0.5 * loss
        stat_ref[5:8] = jnp.zeros((3, width), F32)
        mine = pl.ds(pl.multiple_of(t * half, 16), half)
        own = pick_ref[mine]
        dy_ref[:, :width] = d3_ref[mine].astype(BF)
        dy_ref[:, width:] = (dot(own, hi_ref[...]) + dot(own, lo_ref[...])).astype(BF)

    return call(
        run,
        (
            whole((rows, width), F32), whole((chars, width), F32), whole((rows, width), F32),
            whole((chars, width), F32), whole((half, 2 * width), BF), whole((8, width), F32),
        ),
        "close",
        (pltpu.VMEM((rows, 2 * width), BF), pltpu.VMEM((chars, width), BF), pltpu.VMEM((chars, width), BF)),
    )(second, y_mine, y_other, chars_in, teacher_tok, teacher_chr, pick, notes, marks, gains, shifts)


def conv_back(dy, kernel):
    nz, rows, cols = dy.shape
    width = kernel.shape[1]

    def run(dy_ref, w_ref, out_ref):
        for k in range(nz):
            d = dy_ref[k].astype(F32)
            total = dot(dy_ref[k], w_ref[1], 1, 1)
            total = total + dot(shifted(d, -1).astype(BF), w_ref[0], 1, 1)
            out_ref[k] = total + dot(shifted(d, 1).astype(BF), w_ref[2], 1, 1)

    return call(run, whole((nz, rows, width), F32), "conv_back")(dy, kernel)


def conv_back_edges(inside, before, after_, kernel):
    nz, rows, width = inside.shape
    half = width // 2

    def run(*refs):
        in_ref, b_ref, a_ref, w_ref = refs[:4]
        outs = refs[4:]
        top = dot(b_ref[:, 0], w_ref[2], 1, 1)
        end = dot(a_ref[:, 0], w_ref[0], 1, 1)
        at = lax.broadcasted_iota(jnp.int32, (rows, width), 0)
        for k in range(nz):
            x = in_ref[k] + jnp.where(at == 0, top[k : k + 1], 0.0) + jnp.where(at == rows - 1, end[k : k + 1], 0.0)
            outs[k][...] = x[:, :half].astype(BF)
            outs[nz][block_of(k, nz)] = x[:, half:].astype(BF)

    shapes = (whole((rows, half), BF),) * nz + (whole((nz, rows, half), BF),)
    outs = call(run, shapes, "conv_back_edges")(inside, before, after_, kernel)
    return outs[:nz], outs[nz]


def conv_grads(toks, chrs, dy, before, after_):
    nz = len(toks)
    rows, half = toks[0].shape
    cols = dy.shape[2]

    def run(*refs):
        c_ref, dy_ref, b_ref, a_ref, out_ref, wide = refs[nz:]
        at = lax.broadcasted_iota(jnp.int32, (rows, cols), 0)
        for k in range(nz):
            d = dy_ref[k].astype(F32)
            here = slice(k * rows, (k + 1) * rows)
            wide[1, here] = dy_ref[k]
            wide[0, here] = jnp.where(at == rows - 1, a_ref[k].astype(F32), shifted(d, -1)).astype(BF)
            wide[2, here] = jnp.where(at == 0, b_ref[k].astype(F32), shifted(d, 1)).astype(BF)
        for m in range(3):
            for side in range(2):
                total = jnp.zeros((half, cols), F32)
                for k in range(nz):
                    u = c_ref[block_of(k, nz)] if side else refs[k][...]
                    total += dot(u, wide[m, k * rows : (k + 1) * rows], 0, 0)
                out_ref[m, side * half : (side + 1) * half] = total.astype(BF)

    return call(
        run, whole((3, 2 * half, cols), BF), "conv_grads", (pltpu.VMEM((3, nz * rows, cols), BF),)
    )(*toks, chrs, dy, before, after_)


def scan_pair(a, b, e, f):
    n = a.shape[0]
    rows = lax.broadcasted_iota(jnp.int32, a.shape, 0)
    step = 1
    while step < n:
        has = rows >= step
        pa = jnp.where(has, pltpu.roll(a, step, 0), 1.0)
        pb = jnp.where(has, pltpu.roll(b, step, 0), 0.0)
        b = b + a * pb
        a = a * pa
        has = rows < n - step
        pe = jnp.where(has, pltpu.roll(e, n - step, 0), 1.0)
        pf = jnp.where(has, pltpu.roll(f, n - step, 0), 0.0)
        f = f + e * pf
        e = e * pe
        step *= 2
    return a, b, e, f


def store_scans(scans, refs):
    a, b, e, f = scans
    n = a.shape[0]
    for ref, x in zip(refs[:4], scans):
        ref[...] = x
    ends = refs[4]
    ends[...] = jnp.zeros(ends.shape, F32)
    ends[0:1], ends[1:2], ends[2:3], ends[3:4] = a[n - 1 :], b[n - 1 :], e[:1], f[:1]


def scan_shapes(chars, units):
    return (whole((chars, units), F32),) * 4 + (whole((8, units), F32),)


def entering(refs):
    c = lax.axis_index(C)
    up = jnp.zeros((1, refs[0].shape[1]), F32)
    down = up
    for j in range(4):
        for m, ref in enumerate(refs):
            now = jnp.bitwise_xor(c, j) == m
            up = jnp.where(jnp.logical_and(now, j < c), ref[0:1] * up + ref[1:2], up)
    for j in (3, 2, 1, 0):
        for m, ref in enumerate(refs):
            now = jnp.bitwise_xor(c, j) == m
            down = jnp.where(jnp.logical_and(now, j > c), ref[2:3] * down + ref[3:4], down)
    return up, down


def sigmoid(x):
    return 1.0 / (1.0 + jnp.exp(-x))


def gates(proj_ref, bias_ref, units):
    up = sigmoid(proj_ref[:, :units] + bias_ref[0:1])
    down = sigmoid(proj_ref[:, 2 * units : 3 * units] + bias_ref[1:2])
    return up, down


def gru_open(chars_in, w_recur, bias, marks):
    chars = chars_in.shape[0]
    units = bias.shape[1]

    def run(c_ref, w_ref, b_ref, m_ref, proj_ref, *outs):
        proj_ref[...] = dot(c_ref[...], w_ref[...])
        up, down = gates(proj_ref, b_ref, units)
        store_scans(
            scan_pair(
                (1.0 - up) * m_ref[:, 0:1], up * proj_ref[:, units : 2 * units],
                (1.0 - down) * m_ref[:, 1:2], down * proj_ref[:, 3 * units :],
            ),
            outs,
        )

    return call(run, (whole((chars, 4 * units), F32),) + scan_shapes(chars, units), "gru_open")(
        chars_in, w_recur, bias, marks
    )


def gru_close(scans, ends, pick, notes, w_charp_t):
    chars, units = scans[0].shape
    rows = pick.shape[0]
    half = w_charp_t.shape[0] // 2

    def run(cu, hu, cd, hd, e0, e1, e2, e3, p_ref, n_ref, w_ref, up_ref, down_ref, in_ref, pool_ref, keep_ref, send_ref):
        up, down = entering((e0, e1, e2, e3))
        in_ref[...] = jnp.zeros(in_ref.shape, F32)
        in_ref[0:1], in_ref[1:2] = up, down
        up_ref[...] = hu[...] + cu[...] * up
        down_ref[...] = hd[...] + cd[...] * down
        for ref, at in ((up_ref, slice(units)), (down_ref, slice(units, 2 * units))):
            pool_ref[:, at] = (dot(p_ref[...], ref[...].astype(BF)) / n_ref[:, 0:1]).astype(BF)
        t = lax.axis_index(T)
        low = dot(pool_ref[...], w_ref[:half], 1, 1)
        high = dot(pool_ref[...], w_ref[half:], 1, 1)
        keep_ref[...] = jnp.where(t == 0, low, high)
        send_ref[...] = jnp.where(t == 0, high, low)

    state = whole((chars, units), F32)
    return call(
        run,
        (
            state, state, whole((8, units), F32), whole((rows, 2 * units), BF),
            whole((rows, half), F32), whole((rows, half), F32),
        ),
        "gru_close",
    )(*scans, *ends, pick, notes, w_charp_t)


def gru_back_open(dfb, proj, bias, marks, pick, notes, w_charp_t):
    chars = proj.shape[0]
    units = bias.shape[1]

    def run(d_ref, proj_ref, b_ref, m_ref, p_ref, n_ref, w_ref, dh_ref, *outs):
        pooled = dot(d_ref[...], w_ref[...]) / n_ref[:, 0:1]
        high = pooled.astype(BF)
        low = (pooled - high.astype(F32)).astype(BF)
        dh_ref[...] = dot(p_ref[...], high, 0, 0) + dot(p_ref[...], low, 0, 0)
        up, down = gates(proj_ref, b_ref, units)
        up = (1.0 - up) * m_ref[:, 0:1]
        down = (1.0 - down) * m_ref[:, 1:2]
        store_scans(scan_pair(down, down * dh_ref[:, units:], up, up * dh_ref[:, :units]), outs)

    return call(run, (whole((chars, 2 * units), F32),) + scan_shapes(chars, units), "gru_back_open")(
        dfb, proj, bias, marks, pick, notes, w_charp_t
    )


def gru_back_close(scans, ends, d_hidden, proj, bias, marks, states, entries, w_recur):
    chars, units = scans[0].shape
    width = w_recur.shape[0]

    def run(
        cd, md, cu, mu, e0, e1, e2, e3, dh_ref, proj_ref, b_ref, m_ref, hu_ref, hd_ref, in_ref, w_ref,
        low_ref, high_ref, stat_ref, part_ref,
    ):
        from_below, from_above = entering((e0, e1, e2, e3))
        at = lax.broadcasted_iota(jnp.int32, (chars, units), 0)
        first, last = at == 0, at == chars - 1
        up, down = gates(proj_ref, b_ref, units)
        m = mu[...] + cu[...] * from_above
        lam = dh_ref[:, :units] + jnp.where(last, from_above, pltpu.roll(m, chars - 1, 0))
        before = jnp.where(first, in_ref[0:1], pltpu.roll(hu_ref[...], 1, 0))
        d_gate = lam * (proj_ref[:, units : 2 * units] - m_ref[:, 0:1] * before) * up * (1.0 - up)
        low_ref[:, :units] = d_gate.astype(BF)
        low_ref[:, units:] = (lam * up).astype(BF)
        stat_ref[...] = jnp.zeros(stat_ref.shape, F32)
        stat_ref[0:1, :units] = column_sum(d_gate)
        m = md[...] + cd[...] * from_below
        lam = dh_ref[:, units:] + jnp.where(first, from_below, pltpu.roll(m, 1, 0))
        beyond = jnp.where(last, in_ref[1:2], pltpu.roll(hd_ref[...], chars - 1, 0))
        d_gate = lam * (proj_ref[:, 3 * units :] - m_ref[:, 1:2] * beyond) * down * (1.0 - down)
        high_ref[:, :units] = d_gate.astype(BF)
        high_ref[:, units:] = (lam * down).astype(BF)
        stat_ref[1:2, :units] = column_sum(d_gate)
        part_ref[...] = dot(low_ref[...], w_ref[:, : 2 * units], 1, 1) + dot(high_ref[...], w_ref[:, 2 * units :], 1, 1)

    part = whole((chars, 2 * units), BF)
    return call(
        run, (part, part, whole((8, width), F32), whole((chars, width), F32)), "gru_back_close"
    )(*scans, *ends, d_hidden, proj, bias, marks, *states, *entries, w_recur)


def score_block(k, q, seg_k, seg_q):
    s = dot(k, q, 1, 1) * HD ** (-0.5)
    return jnp.where(seg_k == seg_q, s, MASKED_SCORE)


def attend(x, others, w_query, w_mix_t, seg_keys, seg_here):
    rows, width = x.shape
    half = w_mix_t.shape[1]
    heads = half // HD
    keys = rows * (1 + others.shape[0])

    def run(x_ref, o_ref, w_ref, wm_ref, sk_ref, sq_ref, q_ref, kv_ref, lse_ref, att_ref, part_ref, turned):
        q_ref[...] = dot(x_ref[...], w_ref[:, :half]).astype(BF)
        kv_ref[:rows] = dot(x_ref[...], w_ref[:, half:]).astype(BF)
        for m in range(others.shape[0]):
            kv_ref[(m + 1) * rows : (m + 2) * rows] = dot(o_ref[m], w_ref[:, half:]).astype(BF)
        lse_ref[...] = jnp.zeros(lse_ref.shape, F32)
        for h in range(heads):
            at = slice(h * HD, (h + 1) * HD)
            s = score_block(kv_ref[:, at], q_ref[:, at], sk_ref[...], sq_ref[...])
            highest = jnp.max(s, axis=0, keepdims=True)
            lse = highest + jnp.log(jnp.sum(jnp.exp(s - highest), axis=0, keepdims=True))
            lse_ref[h : h + 1] = lse
            probs = jnp.exp(s - lse).astype(BF)
            turned[at] = dot(kv_ref[:, half + h * HD : half + (h + 1) * HD], probs, 0, 0)
        att_ref[...] = turned[...].T.astype(BF)
        part_ref[...] = dot(att_ref[...], wm_ref[...], 1, 1)

    return call(
        run,
        (
            whole((rows, half), BF), whole((keys, 2 * half), BF), whole((8, rows), F32),
            whole((rows, half), BF), whole((rows, width), F32),
        ),
        "attend",
        (pltpu.VMEM((half, rows), F32),),
    )(x, others, w_query, w_mix_t, seg_keys, seg_here)


def attend_back(d_two, mine, other, n_one, inv_one, gains, w_mix_t, q, kv, lse, seg_keys, seg_here):
    rows, width = d_two.shape
    half = q.shape[1]
    heads = half // HD
    keys = kv.shape[0]
    count = keys // rows

    def run(
        d_ref, a_ref, b_ref, n_ref, i_ref, g_ref, wm_ref, q_ref, kv_ref, lse_ref, sk_ref, sq_ref,
        d1_ref, datt_ref, stat_ref, dq_ref, own_ref, s1_ref, s2_ref, s3_ref, da_ref, turned,
    ):
        e = d_ref[...] + (a_ref[...] + b_ref[...])
        n = n_ref[...]
        stat_ref[...] = jnp.zeros(stat_ref.shape, F32)
        stat_ref[0:1] = column_sum(e * n)
        stat_ref[1:2] = column_sum(e)
        d = row_norm_back(e, n, i_ref[...], g_ref[0:1])
        d1_ref[...] = d
        datt_ref[...] = d.astype(BF)
        da_ref[...] = dot(datt_ref[...], wm_ref[...]).astype(BF)
        scale = HD ** (-0.5)
        sends = (None, s1_ref, s2_ref, s3_ref)
        for h in range(heads):
            at = slice(h * HD, (h + 1) * HD)
            vt = slice(half + h * HD, half + (h + 1) * HD)
            s = score_block(kv_ref[:, at], q_ref[:, at], sk_ref[...], sq_ref[...])
            p = jnp.exp(s - lse_ref[h : h + 1])
            dp = dot(kv_ref[:, vt], da_ref[:, at], 1, 1)
            delta = jnp.sum(p * dp, axis=0, keepdims=True)
            ds = (p * (dp - delta)).astype(BF)
            turned[at] = dot(kv_ref[:, at], ds, 0, 0) * scale
            dk = dot(ds, q_ref[:, at]) * scale
            dv = dot(p.astype(BF), da_ref[:, at])
            own_ref[:, at] = dk[:rows]
            own_ref[:, vt] = dv[:rows]
            for m in range(1, count):
                sends[m][:, at] = dk[m * rows : (m + 1) * rows].astype(BF)
                sends[m][:, vt] = dv[m * rows : (m + 1) * rows].astype(BF)
        dq_ref[...] = turned[...].T.astype(BF)

    send = whole((rows, 2 * half), BF)
    return call(
        run,
        (
            whole((rows, width), F32), whole((rows, width), BF), whole((8, width), F32), whole((rows, half), BF),
            whole((rows, 2 * half), F32), send, send, send,
        ),
        "attend_back",
        (pltpu.VMEM((rows, half), BF), pltpu.VMEM((half, rows), F32)),
    )(d_two, mine, other, n_one, inv_one, gains, w_mix_t, q, kv, lse, seg_keys, seg_here)


def query_grads(x, d_att, att, dq, own, came, w_query):
    rows, width = x.shape
    half = att.shape[1]

    def run(x_ref, da_ref, att_ref, dq_ref, own_ref, c1, c2, c3, w_ref, o0, o1, o2, o3, part_ref, kv_ref):
        c = lax.axis_index(C)
        kv_ref[...] = (own_ref[...] + c1[...].astype(F32) + c2[...].astype(F32) + c3[...].astype(F32)).astype(BF)
        pairs = (
            (da_ref, att_ref[...]), (x_ref, dq_ref[...]), (x_ref, kv_ref[:, :half]), (x_ref, kv_ref[:, half:]),
        )
        for j, (left, right) in enumerate(pairs):
            grad = dot(left[...], right, 0, 0).astype(BF)
            for m, out in enumerate((o0, o1, o2, o3)):

                @pl.when(jnp.bitwise_xor(c, j) == m)
                def _():
                    out[...] = grad

        part_ref[...] = dot(dq_ref[...], w_ref[:, :half], 1, 1) + dot(kv_ref[...], w_ref[:, half:], 1, 1)

    return call(
        run,
        (whole((width, half), BF),) * 4 + (whole((rows, width), F32),),
        "query_grads",
        (pltpu.VMEM((rows, 2 * half), BF),),
    )(x, d_att, att, dq, own, *came, w_query)


def gelu_parts(x):
    cdf = 0.5 * (1.0 + lax.erf(x * 0.7071067811865476))
    return cdf, jnp.exp(-0.5 * x * x) * 0.3989422804014327


def feed(x, mine, other, gains, shifts, w_upper, w_lower_t):
    rows, width = x.shape
    hidden = w_upper.shape[1]

    def run(x_ref, a_ref, b_ref, g_ref, s_ref, wu_ref, wd_ref, n_ref, i_ref, low_ref, pre_ref, act_ref, part_ref):
        n, inverse = row_norm(x_ref[...].astype(F32) + (a_ref[...] + b_ref[...]))
        n_ref[...] = n
        i_ref[...] = inverse
        low_ref[...] = (n * g_ref[0:1] + s_ref[0:1]).astype(BF)
        step = hidden // 4
        total = jnp.zeros((rows, width), F32)
        for i in range(4):
            at = slice(i * step, (i + 1) * step)
            pre = dot(low_ref[...], wu_ref[:, at])
            pre_ref[:, at] = pre
            act_ref[:, at] = (pre * gelu_parts(pre)[0]).astype(BF)
            total += dot(act_ref[:, at], wd_ref[:, at], 1, 1)
        part_ref[...] = total

    return call(
        run,
        (
            whole((rows, width), F32), whole((rows, 1), F32), whole((rows, width), BF), whole((rows, hidden), F32),
            whole((rows, hidden), BF), whole((rows, width), F32),
        ),
        "feed",
    )(x, mine, other, gains, shifts, w_upper, w_lower_t)


def feed_close(n_one, mine, other, gains, shifts, w_token):
    rows, width = n_one.shape
    half = w_token.shape[1]

    def run(n1_ref, a_ref, b_ref, g_ref, s_ref, w_ref, n_ref, i_ref, x2_ref, low_ref, fa_ref):
        first = n1_ref[...] * g_ref[0:1] + s_ref[0:1]
        n, inverse = row_norm(first + (a_ref[...] + b_ref[...]))
        n_ref[...] = n
        i_ref[...] = inverse
        second = n * g_ref[1:2] + s_ref[1:2]
        x2_ref[...] = second
        low_ref[...] = second.astype(BF)
        fa_ref[...] = dot(low_ref[...], w_ref[...]).astype(BF)

    return call(
        run,
        (
            whole((rows, width), F32), whole((rows, 1), F32), whole((rows, width), F32), whole((rows, width), BF),
            whole((rows, half), BF),
        ),
        "feed_close",
    )(n_one, mine, other, gains, shifts, w_token)


def join_back(parts, w_token):
    rows, half = parts[0].shape
    width = w_token.shape[0]

    def run(*refs):
        w_ref, low_ref, part_ref = refs[len(parts) :]
        total = refs[0][...].astype(F32)
        for ref in refs[1 : len(parts)]:
            total = total + ref[...].astype(F32)
        low_ref[...] = total.astype(BF)
        part_ref[...] = dot(low_ref[...], w_ref[...], 1, 1)

    return call(run, (whole((rows, half), BF), whole((rows, width), F32)), "join_back")(*parts, w_token)


def feed_back(d_three, mine, other, n_two, inv_two, gains, pre, w_upper, w_lower_t):
    rows, width = d_three.shape
    hidden = pre.shape[1]

    def run(d_ref, a_ref, b_ref, n_ref, i_ref, g_ref, pre_ref, wu_ref, wd_ref, d2_ref, low_ref, dpre_ref, part_ref, stat_ref):
        e = d_ref[...] + (a_ref[...] + b_ref[...])
        n = n_ref[...]
        stat_ref[...] = jnp.zeros(stat_ref.shape, F32)
        stat_ref[0:1] = column_sum(e * n)
        stat_ref[1:2] = column_sum(e)
        d = row_norm_back(e, n, i_ref[...], g_ref[1:2])
        d2_ref[...] = d
        low_ref[...] = d.astype(BF)
        step = hidden // 4
        total = jnp.zeros((rows, width), F32)
        for i in range(4):
            at = slice(i * step, (i + 1) * step)
            x = pre_ref[:, at]
            cdf, pdf = gelu_parts(x)
            dpre_ref[:, at] = (dot(low_ref[...], wd_ref[:, at]) * (cdf + x * pdf)).astype(BF)
            total += dot(dpre_ref[:, at], wu_ref[:, at], 1, 1)
        part_ref[...] = total

    return call(
        run,
        (
            whole((rows, width), F32), whole((rows, width), BF), whole((rows, hidden), BF), whole((rows, width), F32),
            whole((8, width), F32),
        ),
        "feed_back",
    )(d_three, mine, other, n_two, inv_two, gains, pre, w_upper, w_lower_t)


def neighbours(x):
    return [x] + [swap(x, C, m) for m in (1, 2, 3)]


def body(
    tokens_in, chars_in, segment_ids, char_counts, valid, teacher_tokens, teacher_chars,
    w_qkv, w_out, w_up, w_down, w_gru, gru_bias, w_tok, w_char, w_conv, ln_gain, ln_bias,
):
    nz = lax.axis_size(Z)
    c = lax.axis_index(C)
    t = lax.axis_index(T)
    rows, width = tokens_in.shape
    chars = chars_in.shape[0]
    half = width // 2
    units = gru_bias.shape[2]
    shard = w_qkv.shape[1]
    hidden = w_up.shape[2]
    gains, shifts, bias = ln_gain[0], ln_bias[0], gru_bias[0]

    widths = ((3 * half, 4 * units, half), (hidden, half, half))
    shards = (
        jnp.concatenate([w_qkv[0].reshape(shard, -1), w_gru[0].reshape(shard, -1), w_char[0].reshape(-1, shard).T], axis=1),
        jnp.concatenate([w_up[0], w_out[0].T, w_tok[0]], axis=1),
    )
    if shard % 64:
        w_first, w_one = [
            [lax.slice_in_dim(full, sum(w[:i]), sum(w[: i + 1]), axis=1) for i in range(3)]
            for full, w in zip((lax.all_gather(x, Z, axis=0, tiled=True) for x in shards), widths)
        ]
        near = ()
    else:
        cut = shards[0].shape[1]
        quarters = gather_beside(context_quarter(jnp.concatenate(shards, axis=1)), 1)
        w_first, near = round_context(quarters[:, :, :cut], BOTH, widths[0])
        w_one, near = round_context(quarters[:, :, cut:], BOTH, widths[1], near)
    w_query, w_recur, w_charp_t = w_first
    w_upper, w_mix_t, w_token = w_one
    w_lower_t = lax.all_gather(w_down[0].T, Z, axis=0, tiled=True)
    mine = own_part(tokens_in, 2, t)
    others = core_join(jnp.stack([swap(mine, C, m) for m in (1, 2, 3)]), 1)

    seq_len = segment_ids.shape[1]
    offset_here = c * rows
    seg_full = segment_ids[0]
    seg_here = lax.dynamic_slice_in_dim(seg_full, offset_here, rows)
    seg_keys = jnp.concatenate(
        [lax.dynamic_slice_in_dim(seg_full, jnp.bitwise_xor(c, m) * rows, rows) for m in range(4)]
    )[:, None]
    counts = char_counts[0]
    ends = jnp.cumsum(counts)
    starts = ends - counts
    places = jnp.arange(chars, dtype=jnp.int32)
    chosen = jnp.logical_and(starts[:, None] <= places[None, :], places[None, :] < ends[:, None])
    pick = chosen.astype(BF)
    valid_tok = valid[0].astype(F32)
    char_seg = jnp.sum(jnp.where(chosen, seg_here[:, None], 0), axis=0)
    valid_chr = jnp.sum(jnp.where(chosen, valid_tok[:, None], 0.0), axis=0)
    prev_seg = seg_full[jnp.maximum(offset_here - 1, 0)]
    next_seg = seg_full[jnp.minimum(offset_here + rows, seq_len - 1)]
    first_keep = jnp.logical_and(c > 0, prev_seg == char_seg[0])
    last_keep = jnp.logical_and(c < lax.axis_size(C) - 1, next_seg == char_seg[-1])
    same = char_seg[1:] == char_seg[:-1]
    keep_up = jnp.concatenate([first_keep[None], same]).astype(F32)
    keep_down = jnp.concatenate([same, last_keep[None]]).astype(F32)
    marks = jnp.stack([keep_up, keep_down, valid_chr], axis=1)
    notes = jnp.stack([counts.astype(F32), valid_tok], axis=1)
    seg_row = seg_here[None, :]

    proj, *scans, ends_here = gru_open(chars_in, w_recur, bias, marks)
    *states, entries, pooled_low, keep, send = gru_close(scans, neighbours(ends_here), pick, notes, w_charp_t)
    fb = (keep + swap(send, T, 1)).astype(BF)
    fbs = gather_beside(fb, 0)

    q, kv, lse, mixed_low, part = attend(
        after(tokens_in, *near, fb), others, w_query, w_mix_t, seg_keys, seg_row
    )
    n_one, inv_one, first_low, pre, act_low, part2 = feed(
        tokens_in, part, swap(part, T, 1), gains, shifts, w_upper, w_lower_t
    )
    first_all, act_part = exchange(first_low, act_low)
    n_two, inv_two, second, second_low, fa = feed_close(n_one, part2, swap(part2, T, 1), gains, shifts, w_token)
    fas = [fa] + [turn(fa, Z, k) for k in range(1, nz)]

    cols = w_conv.shape[-1]
    kernel = w_conv[0].reshape(3, width, cols)

    def edge(at):
        order = [lax.dynamic_index_in_dim(fbs[:, at], block_of(k, nz), 0, keepdims=False) for k in range(nz)]
        return jnp.stack([jnp.concatenate([a[at], b], axis=1) for a, b in zip(fas, order)])

    size = lax.axis_size(C)
    ups = [(i, i + 1) for i in range(size - 1)]
    downs = [(j, i) for i, j in ups]
    u_before = lax.ppermute(edge(slice(rows - 1, rows)), C, ups)
    u_after = lax.ppermute(edge(slice(0, 1)), C, downs)
    inside = conv_main(fas, fbs, kernel)
    keep, send = conv_edges(inside, u_before, u_after, kernel)
    conv = add_split(keep, swap(send, T, 1))
    y_half = side_by_side([conv[0]] + [turn(conv[k], Z, nz - k) for k in range(1, nz)], True)
    out_tok, out_chr, d_res_three, d_res_four, d_mine, stats = close(
        second, y_half, swap(y_half, T, 1), chars_in, teacher_tokens, teacher_chars, pick,
        notes, marks, gains, shifts,
    )

    slices = column_slices(d_mine, nz)
    dy_mine = jnp.stack([slices[0]] + [turn(slices[k], Z, k) for k in range(1, nz)])
    dy_all = core_join(dy_mine, 1)
    dy_before = lax.ppermute(dy_all[:, -1:], C, ups)
    dy_after = lax.ppermute(dy_all[:, :1], C, downs)
    inside = conv_back(dy_all, kernel)
    du_tok, du_chr = conv_back_edges(inside, dy_before, dy_after, kernel)
    dfa, part = join_back([du_tok[0]] + [turn(du_tok[k], Z, nz - k) for k in range(1, nz)], w_token)
    dfb = lax.psum_scatter(du_chr.reshape(nz * rows, half), Z, scatter_dimension=0, tiled=True)
    grad_kernel = lax.psum(conv_grads(fas, fbs, dy_all, dy_before, dy_after), C)

    d_res_two, d_ffn, d_pre, part, stats_two = feed_back(
        d_res_three, part, swap(part, T, 1), n_two, inv_two, gains, pre, w_upper, w_lower_t
    )
    ffn_all, pre_part = exchange(d_ffn, d_pre)

    dfb_full = core_join(after(dfb, d_pre), 1)
    d_hidden, *scans, ends_here = gru_back_open(dfb_full, proj, bias, marks, pick, notes, w_charp_t)
    d_low, d_high, stats_bias, part_chr = gru_back_close(
        scans, neighbours(ends_here), d_hidden, proj, bias, marks, states, (entries,), w_recur
    )
    d_chr_in = d_res_four + core_sum(part_chr)
    sent = sent_apart(((second_low, dfa), (dfb_full, pooled_low), (chars_in, d_low), (chars_in, d_high)), 1, None)
    chars_parts = over_context(sent)

    pre_part = after(pre_part, sent)
    ffn_blocks = z_split(
        [jnp.concatenate([dot(first_all, pre_part, 0, 0), dot(ffn_all, act_part, 0, 0)], axis=1).astype(BF)]
    )
    d_res_one, d_att, stats_one, dq, dkv_own, *dkv_sends = attend_back(
        after(d_res_two, ffn_blocks), part, swap(part, T, 1), n_one, inv_one, gains, w_mix_t, q, kv, lse, seg_keys, seg_row
    )
    ffn_piece = over_z(ffn_blocks)
    came = [swap(after(x, *chars_parts[1:]), C, m) for m, x in zip((1, 2, 3), dkv_sends)]
    *sent, part = query_grads(tokens_in, d_att, mixed_low, dq, dkv_own, came, w_query)
    query_parts = over_context(sent)
    d_tok_in = d_res_one + core_sum(part)
    chars_parts[0] = after(chars_parts[0], sent)
    chars_piece = over_z(z_split(chars_parts))
    query_blocks = z_split(query_parts)
    g_ffn = to_context(after(ffn_piece, query_blocks))
    g_chars = to_context(after(chars_piece, query_blocks))
    g_query = to_context(over_z(query_blocks))
    grad_kernel = after(grad_kernel, query_blocks).astype(F32)

    counted = jnp.full((1, width), jnp.sum(valid_tok))
    packed = jnp.concatenate([stats[:5], counted, stats_bias[:2], stats_one[:2], stats_two[:2]])
    packed = after(packed, query_blocks)
    for bit in (1, 2):
        packed = packed + swap(packed, C, bit)
    bit = 1
    while bit < nz:
        packed = packed + swap(packed, Z, bit)
        bit *= 2
    loss = jnp.sum(packed[4]) / packed[5, 0]
    gain_total = jnp.stack([packed[8], packed[10], packed[0], packed[1]])[None]
    shift_total = jnp.stack([packed[9], packed[11], packed[2], packed[3]])[None]
    bias_total = packed[None, 6:8, :units]
    g_ffn = [g_ffn[j] for j in range(4)]
    g_gru = jnp.concatenate([g_chars[2], g_chars[3]], axis=1)
    return (
        out_tok,
        out_chr,
        loss,
        d_tok_in,
        d_chr_in,
        jnp.stack([g_query[1], g_query[2], g_query[3]], axis=1)[None],
        g_query[0].T[None],
        jnp.concatenate([g[:, : hidden // 4] for g in g_ffn], axis=1)[None],
        jnp.concatenate([g[:, hidden // 4 :].T for g in g_ffn])[None],
        g_gru.reshape(w_gru.shape),
        bias_total,
        g_chars[0][None],
        g_chars[1].T.reshape(w_char.shape),
        grad_kernel.reshape(w_conv.shape),
        gain_total,
        shift_total,
    )


def solution(mesh):
    tok = P((Z, C), None)
    seq = P(Z, None)
    placed = (
        tok, tok, seq, tok, P(Z, C), tok, tok,
        P(None, Z, None, T), P(None, T, Z), P(None, Z, T), P(None, T, Z), P(None, Z, None, T),
        P(None, None, T), P(None, Z, T), P(None, None, T, Z), P(None, None, None, T, Z), P(), P(),
    )
    given = (
        tok, tok, P(), tok, tok,
        P(None, Z, None, T), P(None, T, Z), P(None, Z, T), P(None, T, Z), P(None, Z, None, T),
        P(None, None, T), P(None, Z, T), P(None, None, T, Z), P(None, None, None, T, Z), P(), P(),
    )
    return jax.shard_map(body, mesh=mesh, in_specs=placed, out_specs=given, check_vma=False)
```

```python
import functools

import jax
import jax.numpy as jnp
from jax import lax
from jax.experimental import pallas as pl
from jax.experimental.pallas import tpu as pltpu
from jax.sharding import PartitionSpec as P

HD = 64
EPSILON = 1e-05
MASKED_SCORE = -1000000000.0
BF = jnp.bfloat16
F32 = jnp.float32
Z = "fsdp"
C = "context"
T = "tensor"
ROOM = 56 * 1024 * 1024


def dot(a, b, ca=1, cb=0):
    return lax.dot_general(a, b, (((ca,), (cb,)), ((), ())), preferred_element_type=F32)


def swap(x, axis, bit):
    size = lax.axis_size(axis)
    return lax.ppermute(x, axis, [(i, i ^ bit) for i in range(size)])


def turn(x, axis, k):
    size = lax.axis_size(axis)
    return lax.ppermute(x, axis, [(i, (i + k) % size) for i in range(size)])


def core_sum(x):
    return x + swap(x, T, 1)


def own_part(x, count, index, dim=0):
    width = x.shape[dim] // count
    return lax.dynamic_slice_in_dim(x, index * width, width, axis=dim)


def ordered(mine, other, first):
    return jnp.where(first, mine, other), jnp.where(first, other, mine)


def core_join(x, dim):
    other = swap(x, T, 1)
    low, high = ordered(x, other, lax.axis_index(T) == 0)
    return jnp.concatenate([low, high], axis=dim)


def after(x, *deps):
    return lax.optimization_barrier((x, deps))[0]


def whole(shape, dtype):
    return jax.ShapeDtypeStruct(shape, dtype)


def call(kernel, outs, name, scratch=()):
    return pl.pallas_call(
        kernel,
        out_shape=outs,
        scratch_shapes=list(scratch),
        compiler_params=pltpu.CompilerParams(vmem_limit_bytes=ROOM),
        cost_estimate=pl.CostEstimate(flops=1, bytes_accessed=1, transcendentals=0),
        name=name,
    )


def context_quarter(shard):
    return own_part(shard, 4, lax.axis_index(C))


def first_round(stack, wait_for):
    nz, _, n = stack.shape
    z = lax.axis_index(Z)
    half = n // 256 * 128
    index = [lax.rem(z + k, nz) for k in range(1, nz)]
    others = jnp.concatenate([lax.dynamic_slice_in_dim(stack, i, 1) for i in index])
    firsts = [after(others[:, :, cut], *wait_for) for cut in (slice(half), slice(half, n))]
    return firsts, [swap(a, C, b0) for a, (b0, _) in zip(firsts, BOTH)]


def second_round(firsts, nears, wait_for=()):
    both = [jnp.concatenate([a, b]) for a, b in zip(firsts, nears)]
    return [swap(after(x, *wait_for), C, b1) for x, (_, b1) in zip(both, BOTH)]


def assemble(shard, quads, widths):
    count, q = quads[0][0].shape[:2]
    nz = count + 1
    starts = [sum(widths[:i]) for i in range(len(widths))]

    def kernel(*refs):
        outs = refs[7:]
        z = lax.axis_index(Z)
        c = lax.axis_index(C)
        own = pl.ds(pl.multiple_of(z * 4 * q, 16), 4 * q)
        for out, begin, size in zip(outs, starts, widths):
            out[own] = refs[6][:, begin : begin + size]
        col = 0
        for side, (b0, b1) in enumerate(BOTH):
            first, near, far = refs[3 * side : 3 * side + 3]
            width = first.shape[-1]
            spans = []
            for out, begin, size in zip(outs, starts, widths):
                low, high = max(begin, col), min(begin + size, col + width)
                if low < high:
                    spans.append((out, slice(low - col, high - col), slice(low - begin, high - begin)))
            for ref, base, mask in ((first, 0, 0), (near, 0, b0), (far, 0, b1), (far, count, b0 ^ b1)):
                for s in range(count):
                    block = lax.rem(z + 1 + s, nz) * 4 + jnp.bitwise_xor(c, mask)
                    row = pl.multiple_of(block * q, 16)
                    for out, src, dst in spans:
                        out[pl.ds(row, q), dst] = ref[base + s, :, src]
            col += width

    shapes = tuple(whole((nz * 4 * q, w), BF) for w in widths)
    return call(kernel, shapes, "assemble")(*[x for quad in quads for x in quad], shard)


BOTH = ((1, 2), (2, 1))


def sent_apart(products, b0, b1):
    rows, width = products[0][0].shape[1], products[0][1].shape[1]
    arrays = []
    places = []
    for pair in products:
        spots = []
        for x in pair:
            for i, y in enumerate(arrays):
                if y is x:
                    break
            else:
                i = len(arrays)
                arrays.append(x)
            spots.append(i)
        places.append(spots)
    count = len(arrays)

    def kernel(*refs):
        outs = refs[count:]
        c = lax.axis_index(C)
        for j, (l, r) in enumerate(places):
            part = dot(refs[l][...], refs[r][...], 0, 0).astype(BF)
            if b1 is None:
                for m in range(4):

                    @pl.when(jnp.bitwise_xor(c, j) == m)
                    def _():
                        outs[m][...] = part
            else:
                slot = (j & b1) // b1
                mine = jnp.bitwise_and(jnp.bitwise_xor(c, j), b0) == 0

                @pl.when(mine)
                def _():
                    outs[0][slot] = part

                @pl.when(jnp.logical_not(mine))
                def _():
                    outs[1][slot] = part

    if b1 is None:
        shapes = (whole((rows, width), BF),) * 4
    else:
        shapes = (whole((2, rows, width), BF),) * 2
    return call(kernel, shapes, "grads")(*arrays)


def z_split(parts):
    nz = lax.axis_size(Z)
    rows, width = parts[0].shape
    block = rows // nz

    def kernel(*refs):
        z = lax.axis_index(Z)
        for k, out in enumerate(refs[len(parts) :]):
            at = pl.ds(pl.multiple_of(lax.rem(z + k, nz) * block, 16), block)
            total = refs[0][at].astype(F32)
            for ref in refs[1 : len(parts)]:
                total = total + ref[at].astype(F32)
            out[...] = total.astype(BF)

    return call(kernel, (whole((block, width), BF),) * nz, "z_split")(*parts)


def exchange(copied, split, wait_for=()):
    c = lax.axis_index(C)
    half = after(own_part(copied, 2, lax.axis_index(T), 1), *wait_for)
    pieces = [own_part(split, 4, jnp.bitwise_xor(c, m), 1) for m in range(4)]
    if half.shape[1] != pieces[0].shape[1]:
        return pieces[0], [(swap(half, C, m), swap(pieces[m], C, m)) for m in (1, 2, 3)]
    return pieces[0], [swap(jnp.concatenate([half, pieces[m]]), C, m) for m in (1, 2, 3)]


def collected(copied, own, came):
    rows = copied.shape[0]
    came = [x if isinstance(x, tuple) else (x[:rows], x[rows:]) for x in came]
    halves = jnp.concatenate([a for a, _ in came])
    return jnp.concatenate([copied, core_join(halves, 1)]), jnp.concatenate([own] + [b for _, b in came])


def by_context(parts, outs, stores, name):
    def kernel(*refs):
        c = lax.axis_index(C)
        for m in range(4):
            for j, store in enumerate(stores):

                @pl.when(jnp.bitwise_xor(c, m) == j)
                def _():
                    store(refs[m][...].astype(F32), refs[4:])

    return call(kernel, outs, name)(*parts)


def early_join(copies):
    _, rows, width = copies.shape
    third = width // 3

    def run(in_ref, up_ref, down_ref, tok_ref, char_ref, gru_ref):
        for j in range(4):
            at = slice(j * third, (j + 1) * third)
            up_ref[:, at] = in_ref[j, :, :third].astype(F32)
            down_ref[at] = in_ref[j, :, third : 2 * third].astype(F32).T
        tok_ref[...] = in_ref[0, :, 2 * third :].astype(F32)
        char_ref[...] = in_ref[1, :, 2 * third :].astype(F32).T
        gru_ref[:, :third] = in_ref[2, :, 2 * third :].astype(F32)
        gru_ref[:, third:] = in_ref[3, :, 2 * third :].astype(F32)

    shapes = (
        whole((rows, 4 * third), F32), whole((4 * third, rows), F32), whole((rows, third), F32),
        whole((third, rows), F32), whole((rows, 2 * third), F32),
    )
    return call(run, shapes, "early_join")(copies)


def query_join(parts):
    rows, width = parts[0].shape

    def put_out(x, outs):
        outs[0][...] = x.T

    def store(i):
        def put(x, outs):
            outs[1][:, i] = x

        return put

    outs = (whole((width, rows), F32), whole((rows, 3, width), F32))
    return by_context(parts, outs, (put_out, store(0), store(1), store(2)), "query_join")


def turned(blocks):
    return [turn(blocks[k], Z, k) for k in range(1, len(blocks))]


def summed(own, came):
    total = own.astype(F32)
    for x in came:
        total = total + x.astype(F32)
    return total.astype(BF)


def turned_all(x):
    return [x] + [turn(x, Z, k) for k in range(1, lax.axis_size(Z))]


def swapped(x):
    return [swap(x, C, m) for m in (1, 2, 3)]


BESIDE = 1 << 20


def gather_beside(x, dim):
    nz = lax.axis_size(Z)
    extent = x.shape[dim]
    other = x.size // extent
    unit = 128 if dim else 16
    need = -(-BESIDE // (2 * nz * other * unit)) * unit
    if need > extent:
        pads = [(0, 0)] * x.ndim
        pads[dim] = (0, need - extent)
        x = jnp.pad(x, pads)
    return lax.all_gather(x, Z)


def from_neighbours(first, last):
    c = lax.axis_index(C)
    size = lax.axis_size(C)
    both = jnp.stack([first, last])
    near, far = swap(both, C, 1), swap(both, C, 3)
    odd = jnp.bitwise_and(c, 1) == 1
    before = jnp.where(odd, near[1], far[1])
    beyond = jnp.where(odd, far[0], near[0])
    return jnp.where(c > 0, before, 0), jnp.where(c < size - 1, beyond, 0)


def shifted(x, by):
    rows = x.shape[0]
    at = lax.broadcasted_iota(jnp.int32, x.shape, 0)
    if by > 0:
        return jnp.where(at >= by, pltpu.roll(x, by, 0), 0.0)
    return jnp.where(at < rows + by, pltpu.roll(x, rows + by, 0), 0.0)


def block_of(k, nz):
    return lax.rem(lax.axis_index(Z) - k + nz, nz)


def conv_main(toks, chrs, kernel):
    nz = len(toks)
    half = toks[0].shape[1]
    rows = toks[0].shape[0] - 16
    cols = kernel.shape[-1]
    part = rows // 2

    def run(*refs):
        c_ref, w_ref, keep_ref, send_ref = refs[nz:]
        t = lax.axis_index(T)
        at = lax.broadcasted_iota(jnp.int32, (rows, cols), 0)
        for k in range(nz):
            j = block_of(k, nz)
            u = jnp.concatenate([refs[k][:rows], c_ref[j, :rows]], axis=1)
            rim = refs[k][rows:]
            rim = jnp.concatenate([rim[:2], rim[2:4]], axis=1)
            rim = jnp.concatenate([rim, jnp.zeros((14, 2 * half), BF)])
            total = dot(u, w_ref[1])
            total = total + jnp.where(at == 0, dot(rim, w_ref[0])[0:1], pltpu.roll(dot(u, w_ref[0]), 1, 0))
            total = total + jnp.where(at == rows - 1, dot(rim, w_ref[2])[1:2], pltpu.roll(dot(u, w_ref[2]), rows - 1, 0))

            @pl.when(t == 0)
            def _():
                keep_ref[k] = total[:part]
                send_ref[k] = total[part:]

            @pl.when(t != 0)
            def _():
                keep_ref[k] = total[part:]
                send_ref[k] = total[:part]

    shape = whole((nz, part, cols), F32)
    return call(run, (shape, shape), "conv")(*toks, chrs, kernel)


def add_split(keep, came):
    nz = keep.shape[0]

    def run(*refs):
        for k in range(nz):
            refs[2 + k][...] = (refs[0][k] + refs[1][k]).astype(BF)

    return call(run, (whole(keep.shape[1:], BF),) * nz, "add_split")(keep, came)


def side_by_side(parts, forward):
    nz = len(parts)
    rows, cols = parts[0].shape
    z = lax.axis_index(Z)
    if cols % 128:
        stacked = jnp.stack(parts)
        order = [lax.rem((s - z if forward else z - s) + nz, nz) for s in range(nz)]
        return jnp.concatenate([lax.dynamic_index_in_dim(stacked, i, 0, keepdims=False) for i in order], axis=1)

    def run(*refs):
        z = lax.axis_index(Z)
        for k in range(nz):
            s = lax.rem((z + k if forward else z - k + nz), nz)
            refs[nz][:, pl.ds(pl.multiple_of(s * cols, 128), cols)] = refs[k][...]

    return call(run, whole((rows, nz * cols), BF), "side_by_side")(*parts)


def column_slices(x, nz):
    cols = x.shape[1] // nz
    z = lax.axis_index(Z)
    return [lax.dynamic_slice_in_dim(x, lax.rem(z + k, nz) * cols, cols, axis=1) for k in range(nz)]


def row_norm(v):
    average = jnp.mean(v, axis=-1, keepdims=True)
    centered = v - average
    spread = jnp.mean(centered * centered, axis=-1, keepdims=True)
    inverse = lax.rsqrt(spread + EPSILON)
    return centered * inverse, inverse


def row_norm_back(e, n, inverse, gain):
    ge = e * gain
    one = jnp.mean(ge, axis=-1, keepdims=True)
    two = jnp.mean(ge * n, axis=-1, keepdims=True)
    return inverse * (ge - one - n * two)


def column_sum(x):
    return jnp.sum(x, axis=0, keepdims=True)


def close(second, y_mine, y_other, chars_in, teacher_tok, teacher_chr, pick, notes, marks, gains, shifts):
    rows, width = second.shape
    chars = chars_in.shape[0]
    half = rows // 2
    step = 128

    def run(
        s_ref, ym_ref, yo_ref, c_ref, tt_ref, tc_ref, pick_ref, vt_ref, vc_ref, g_ref, b_ref,
        tok_ref, chr_ref, d3_ref, d4_ref, dy_ref, stat_ref, y_ref, hi_ref, lo_ref,
    ):
        t = lax.axis_index(T)
        y_ref[pl.ds(pl.multiple_of(t * half, 16), half)] = ym_ref[...]
        y_ref[pl.ds(pl.multiple_of((1 - t) * half, 16), half)] = yo_ref[...]
        zero = jnp.zeros((1, width), F32)
        gain_sum, shift_sum, loss = zero, zero, zero
        for i in range(0, rows, step):
            at = slice(i, i + step)
            n, inverse = row_norm(s_ref[at] + y_ref[at, :width].astype(F32))
            out = n * g_ref[2:3] + b_ref[2:3]
            tok_ref[at] = out
            diff = out - tt_ref[at].astype(F32)
            e = vt_ref[at, 1:2] * diff
            loss += column_sum(e * diff)
            gain_sum += column_sum(e * n)
            shift_sum += column_sum(e)
            d3_ref[at] = row_norm_back(e, n, inverse, g_ref[2:3])
        stat_ref[0:1] = gain_sum
        stat_ref[2:3] = shift_sum
        gain_sum, shift_sum = zero, zero
        for i in range(0, chars, step):
            at = slice(i, i + step)
            spread = dot(pick_ref[:, at], y_ref[:, width:], 0, 0)
            n, inverse = row_norm(c_ref[at].astype(F32) + spread)
            out = n * g_ref[3:4] + b_ref[3:4]
            chr_ref[at] = out
            diff = out - tc_ref[at].astype(F32)
            e = vc_ref[at, 2:3] * diff
            loss += column_sum(e * diff)
            gain_sum += column_sum(e * n)
            shift_sum += column_sum(e)
            d = row_norm_back(e, n, inverse, g_ref[3:4])
            d4_ref[at] = d
            high = d.astype(BF)
            hi_ref[at] = high
            lo_ref[at] = (d - high.astype(F32)).astype(BF)
        stat_ref[1:2] = gain_sum
        stat_ref[3:4] = shift_sum
        stat_ref[4:5] = 0.5 * loss
        stat_ref[5:8] = jnp.zeros((3, width), F32)
        mine = pl.ds(pl.multiple_of(t * half, 16), half)
        own = pick_ref[mine]
        dy_ref[:, :width] = d3_ref[mine].astype(BF)
        dy_ref[:, width:] = (dot(own, hi_ref[...]) + dot(own, lo_ref[...])).astype(BF)

    return call(
        run,
        (
            whole((rows, width), F32), whole((chars, width), F32), whole((rows, width), F32),
            whole((chars, width), F32), whole((half, 2 * width), BF), whole((8, width), F32),
        ),
        "close",
        (pltpu.VMEM((rows, 2 * width), BF), pltpu.VMEM((chars, width), BF), pltpu.VMEM((chars, width), BF)),
    )(second, y_mine, y_other, chars_in, teacher_tok, teacher_chr, pick, notes, marks, gains, shifts)


def spread_taps(mine_ref, other_ref, wide, whole_ref):
    nz, part, cols = mine_ref.shape
    part -= 16
    rows = 2 * part
    t = lax.axis_index(T)
    at = lax.broadcasted_iota(jnp.int32, (rows, cols), 0)
    for k in range(nz):
        whole_ref[pl.ds(pl.multiple_of(t * part, 16), part)] = mine_ref[k, :part]
        whole_ref[pl.ds(pl.multiple_of((1 - t) * part, 16), part)] = other_ref[k, :part]
        a = mine_ref[k, part:].astype(F32)[0:1]
        b = other_ref[k, part:].astype(F32)[0:1]
        above, below = jnp.where(t == 0, a, b), jnp.where(t == 0, b, a)
        d = whole_ref[...].astype(F32)
        wide[1, k] = whole_ref[...]
        wide[0, k] = jnp.where(at == rows - 1, above, pltpu.roll(d, rows - 1, 0)).astype(BF)
        wide[2, k] = jnp.where(at == 0, below, pltpu.roll(d, 1, 0)).astype(BF)


def tap_scratch(mine):
    nz, part, cols = mine.shape
    rows = 2 * (part - 16)
    return pltpu.VMEM((3, nz, rows, cols), BF), pltpu.VMEM((rows, cols), BF)


def conv_back(mine, other, kernel):
    nz, part, cols = mine.shape
    rows = 2 * (part - 16)
    half = kernel.shape[1] // 2

    def run(*refs):
        m_ref, o_ref, w_ref = refs[:3]
        outs, (wide, whole_ref) = refs[3 : 3 + 2 * nz], refs[3 + 2 * nz :]
        spread_taps(m_ref, o_ref, wide, whole_ref)
        for k in range(nz):
            for side in range(2):
                at = slice(side * half, (side + 1) * half)
                x = sum(dot(wide[m, k], w_ref[m, at], 1, 1) for m in range(3)).astype(BF)
                if side:
                    outs[nz + k][...] = x
                else:
                    outs[k][...] = x

    shapes = (whole((rows, half), BF),) * (2 * nz)
    outs = call(run, shapes, "conv_back", tap_scratch(mine))(mine, other, kernel)
    return outs[:nz], outs[nz:]


def conv_grads(toks, chrs, mine, other):
    nz, part, cols = mine.shape
    rows = 2 * (part - 16)
    half = toks[0].shape[1]

    def run(*refs):
        c_ref, m_ref, o_ref, out_ref, wide, whole_ref = refs[nz:]
        spread_taps(m_ref, o_ref, wide, whole_ref)
        for m in range(3):
            for side in range(2):
                total = jnp.zeros((half, cols), F32)
                for k in range(nz):
                    u = c_ref[block_of(k, nz), :rows] if side else refs[k][:rows]
                    total += dot(u, wide[m, k], 0, 0)
                for r in range(2):
                    out_ref[2 * side + r, m] = total[r * half // 2 : (r + 1) * half // 2].astype(BF)

    shape = whole((4, 3, half // 2, cols), BF)
    return call(run, shape, "conv_grads", tap_scratch(mine))(*toks, chrs, mine, other)


def scan_pair(a, b, e, f):
    n = a.shape[0]
    rows = lax.broadcasted_iota(jnp.int32, a.shape, 0)
    step = 1
    while step < n:
        has = rows >= step
        pa = jnp.where(has, pltpu.roll(a, step, 0), 1.0)
        pb = jnp.where(has, pltpu.roll(b, step, 0), 0.0)
        b = b + a * pb
        a = a * pa
        has = rows < n - step
        pe = jnp.where(has, pltpu.roll(e, n - step, 0), 1.0)
        pf = jnp.where(has, pltpu.roll(f, n - step, 0), 0.0)
        f = f + e * pf
        e = e * pe
        step *= 2
    return a, b, e, f


def store_scans(scans, refs):
    a, b, e, f = scans
    n = a.shape[0]
    for ref, x in zip(refs[:4], scans):
        ref[...] = x
    ends = refs[4]
    ends[...] = jnp.zeros(ends.shape, F32)
    ends[0:1], ends[1:2], ends[2:3], ends[3:4] = a[n - 1 :], b[n - 1 :], e[:1], f[:1]


def scan_shapes(chars, units):
    return (whole((chars, units), F32),) * 4 + (whole((8, units), F32),)


def entering(refs):
    c = lax.axis_index(C)
    up = jnp.zeros((1, refs[0].shape[1]), F32)
    down = up
    for j in range(4):
        for m, ref in enumerate(refs):
            now = jnp.bitwise_xor(c, j) == m
            up = jnp.where(jnp.logical_and(now, j < c), ref[0:1] * up + ref[1:2], up)
    for j in (3, 2, 1, 0):
        for m, ref in enumerate(refs):
            now = jnp.bitwise_xor(c, j) == m
            down = jnp.where(jnp.logical_and(now, j > c), ref[2:3] * down + ref[3:4], down)
    return up, down


def gates(proj_ref, bias_ref, units):
    up = jax.nn.sigmoid(proj_ref[:, :units] + bias_ref[0:1])
    down = jax.nn.sigmoid(proj_ref[:, 2 * units : 3 * units] + bias_ref[1:2])
    return up, down


def gru_open(chars_in, w_recur, bias, marks):
    chars = chars_in.shape[0]
    units = bias.shape[1]

    def run(c_ref, w_ref, b_ref, m_ref, proj_ref, *outs):
        proj_ref[...] = dot(c_ref[...], w_ref[...])
        up, down = gates(proj_ref, b_ref, units)
        store_scans(
            scan_pair(
                (1.0 - up) * m_ref[:, 0:1], up * proj_ref[:, units : 2 * units],
                (1.0 - down) * m_ref[:, 1:2], down * proj_ref[:, 3 * units :],
            ),
            outs,
        )

    return call(run, (whole((chars, 4 * units), F32),) + scan_shapes(chars, units), "gru_open")(
        chars_in, w_recur, bias, marks
    )


def gru_close(scans, ends, pick, notes, w_charp_t):
    chars, units = scans[0].shape
    rows = pick.shape[0]
    half = w_charp_t.shape[0] // 2

    def run(cu, hu, cd, hd, e0, e1, e2, e3, p_ref, n_ref, w_ref, up_ref, down_ref, in_ref, pool_ref, keep_ref, send_ref):
        up, down = entering((e0, e1, e2, e3))
        in_ref[...] = jnp.zeros(in_ref.shape, F32)
        in_ref[0:1], in_ref[1:2] = up, down
        up_ref[...] = hu[...] + cu[...] * up
        down_ref[...] = hd[...] + cd[...] * down
        for ref, at in ((up_ref, slice(units)), (down_ref, slice(units, 2 * units))):
            pool_ref[:, at] = (dot(p_ref[...], ref[...].astype(BF)) / n_ref[:, 0:1]).astype(BF)
        t = lax.axis_index(T)
        low = dot(pool_ref[...], w_ref[:half], 1, 1)
        high = dot(pool_ref[...], w_ref[half:], 1, 1)
        keep_ref[...] = jnp.where(t == 0, low, high)
        send_ref[...] = jnp.where(t == 0, high, low)

    state = whole((chars, units), F32)
    return call(
        run,
        (
            state, state, whole((8, units), F32), whole((rows, 2 * units), BF),
            whole((rows, half), F32), whole((rows, half), F32),
        ),
        "gru_close",
    )(*scans, *ends, pick, notes, w_charp_t)


def gru_back_open(dfb, proj, bias, marks, pick, notes, w_charp_t):
    chars = proj.shape[0]
    units = bias.shape[1]

    def run(d_ref, proj_ref, b_ref, m_ref, p_ref, n_ref, w_ref, dh_ref, *outs):
        pooled = dot(d_ref[...], w_ref[...]) / n_ref[:, 0:1]
        high = pooled.astype(BF)
        low = (pooled - high.astype(F32)).astype(BF)
        dh_ref[...] = dot(p_ref[...], high, 0, 0) + dot(p_ref[...], low, 0, 0)
        up, down = gates(proj_ref, b_ref, units)
        up = (1.0 - up) * m_ref[:, 0:1]
        down = (1.0 - down) * m_ref[:, 1:2]
        store_scans(scan_pair(down, down * dh_ref[:, units:], up, up * dh_ref[:, :units]), outs)

    return call(run, (whole((chars, 2 * units), F32),) + scan_shapes(chars, units), "gru_back_open")(
        dfb, proj, bias, marks, pick, notes, w_charp_t
    )


def gru_back_close(scans, ends, d_hidden, proj, bias, marks, states, entries, w_recur):
    chars, units = scans[0].shape
    width = w_recur.shape[0]

    def run(
        cd, md, cu, mu, e0, e1, e2, e3, dh_ref, proj_ref, b_ref, m_ref, hu_ref, hd_ref, in_ref, w_ref,
        low_ref, high_ref, stat_ref, part_ref,
    ):
        from_below, from_above = entering((e0, e1, e2, e3))
        at = lax.broadcasted_iota(jnp.int32, (chars, units), 0)
        first, last = at == 0, at == chars - 1
        up, down = gates(proj_ref, b_ref, units)
        m = mu[...] + cu[...] * from_above
        lam = dh_ref[:, :units] + jnp.where(last, from_above, pltpu.roll(m, chars - 1, 0))
        before = jnp.where(first, in_ref[0:1], pltpu.roll(hu_ref[...], 1, 0))
        d_gate = lam * (proj_ref[:, units : 2 * units] - m_ref[:, 0:1] * before) * up * (1.0 - up)
        low_ref[:, :units] = d_gate.astype(BF)
        low_ref[:, units:] = (lam * up).astype(BF)
        stat_ref[...] = jnp.zeros(stat_ref.shape, F32)
        stat_ref[0:1, :units] = column_sum(d_gate)
        m = md[...] + cd[...] * from_below
        lam = dh_ref[:, units:] + jnp.where(first, from_below, pltpu.roll(m, 1, 0))
        beyond = jnp.where(last, in_ref[1:2], pltpu.roll(hd_ref[...], chars - 1, 0))
        d_gate = lam * (proj_ref[:, 3 * units :] - m_ref[:, 1:2] * beyond) * down * (1.0 - down)
        high_ref[:, :units] = d_gate.astype(BF)
        high_ref[:, units:] = (lam * down).astype(BF)
        stat_ref[1:2, :units] = column_sum(d_gate)
        part_ref[...] = dot(low_ref[...], w_ref[:, : 2 * units], 1, 1) + dot(high_ref[...], w_ref[:, 2 * units :], 1, 1)

    part = whole((chars, 2 * units), BF)
    return call(
        run, (part, part, whole((8, width), F32), whole((chars, width), F32)), "gru_back_close"
    )(*scans, *ends, d_hidden, proj, bias, marks, *states, *entries, w_recur)


def score_block(k, q, seg_k, seg_q):
    s = dot(k, q, 1, 1) * HD ** (-0.5)
    return jnp.where(seg_k == seg_q, s, MASKED_SCORE)


def attend(x, others, w_query, w_mix_t, seg_keys, seg_here):
    rows, width = x.shape
    half = w_mix_t.shape[1]
    heads = half // HD
    keys = rows * (1 + others.shape[0])

    def run(x_ref, o_ref, w_ref, wm_ref, sk_ref, sq_ref, q_ref, kv_ref, lse_ref, att_ref, part_ref, turned):
        q_ref[...] = dot(x_ref[...], w_ref[:, :half]).astype(BF)
        kv_ref[:rows] = dot(x_ref[...], w_ref[:, half:]).astype(BF)
        for m in range(others.shape[0]):
            kv_ref[(m + 1) * rows : (m + 2) * rows] = dot(o_ref[m], w_ref[:, half:]).astype(BF)
        lse_ref[...] = jnp.zeros(lse_ref.shape, F32)
        for h in range(heads):
            at = slice(h * HD, (h + 1) * HD)
            s = score_block(kv_ref[:, at], q_ref[:, at], sk_ref[...], sq_ref[...])
            highest = jnp.max(s, axis=0, keepdims=True)
            lse = highest + jnp.log(jnp.sum(jnp.exp(s - highest), axis=0, keepdims=True))
            lse_ref[h : h + 1] = lse
            probs = jnp.exp(s - lse).astype(BF)
            turned[at] = dot(kv_ref[:, half + h * HD : half + (h + 1) * HD], probs, 0, 0)
        att_ref[...] = turned[...].T.astype(BF)
        part_ref[...] = dot(att_ref[...], wm_ref[...], 1, 1)

    return call(
        run,
        (
            whole((rows, half), BF), whole((keys, 2 * half), BF), whole((8, rows), F32),
            whole((rows, half), BF), whole((rows, width), F32),
        ),
        "attend",
        (pltpu.VMEM((half, rows), F32),),
    )(x, others, w_query, w_mix_t, seg_keys, seg_here)


def attend_back(d_two, mine, other, n_one, inv_one, gains, w_mix_t, q, kv, lse, seg_keys, seg_here):
    rows, width = d_two.shape
    half = q.shape[1]
    heads = half // HD
    keys = kv.shape[0]
    count = keys // rows

    def run(
        d_ref, a_ref, b_ref, n_ref, i_ref, g_ref, wm_ref, q_ref, kv_ref, lse_ref, sk_ref, sq_ref,
        d1_ref, datt_ref, stat_ref, dq_ref, own_ref, s1_ref, s2_ref, s3_ref, da_ref, turned,
    ):
        e = d_ref[...] + (a_ref[...] + b_ref[...])
        n = n_ref[...]
        stat_ref[...] = jnp.zeros(stat_ref.shape, F32)
        stat_ref[0:1] = column_sum(e * n)
        stat_ref[1:2] = column_sum(e)
        d = row_norm_back(e, n, i_ref[...], g_ref[0:1])
        d1_ref[...] = d
        datt_ref[...] = d.astype(BF)
        da_ref[...] = dot(datt_ref[...], wm_ref[...]).astype(BF)
        scale = HD ** (-0.5)
        sends = (None, s1_ref, s2_ref, s3_ref)
        for h in range(heads):
            at = slice(h * HD, (h + 1) * HD)
            vt = slice(half + h * HD, half + (h + 1) * HD)
            s = score_block(kv_ref[:, at], q_ref[:, at], sk_ref[...], sq_ref[...])
            p = jnp.exp(s - lse_ref[h : h + 1])
            dp = dot(kv_ref[:, vt], da_ref[:, at], 1, 1)
            delta = jnp.sum(p * dp, axis=0, keepdims=True)
            ds = (p * (dp - delta)).astype(BF)
            turned[at] = dot(kv_ref[:, at], ds, 0, 0) * scale
            dk = dot(ds, q_ref[:, at]) * scale
            dv = dot(p.astype(BF), da_ref[:, at])
            own_ref[:, at] = dk[:rows]
            own_ref[:, vt] = dv[:rows]
            for m in range(1, count):
                sends[m][:, at] = dk[m * rows : (m + 1) * rows].astype(BF)
                sends[m][:, vt] = dv[m * rows : (m + 1) * rows].astype(BF)
        dq_ref[...] = turned[...].T.astype(BF)

    send = whole((rows, 2 * half), BF)
    return call(
        run,
        (
            whole((rows, width), F32), whole((rows, width), BF), whole((8, width), F32), whole((rows, half), BF),
            whole((rows, 2 * half), F32), send, send, send,
        ),
        "attend_back",
        (pltpu.VMEM((rows, half), BF), pltpu.VMEM((half, rows), F32)),
    )(d_two, mine, other, n_one, inv_one, gains, w_mix_t, q, kv, lse, seg_keys, seg_here)


def query_grads(x, d_att, att, dq, own, came, w_query):
    rows, width = x.shape
    half = att.shape[1]

    def run(x_ref, da_ref, att_ref, dq_ref, own_ref, c1, c2, c3, w_ref, o0, o1, o2, o3, part_ref, kv_ref):
        c = lax.axis_index(C)
        kv_ref[...] = (own_ref[...] + c1[...].astype(F32) + c2[...].astype(F32) + c3[...].astype(F32)).astype(BF)
        pairs = (
            (da_ref, att_ref[...]), (x_ref, dq_ref[...]), (x_ref, kv_ref[:, :half]), (x_ref, kv_ref[:, half:]),
        )
        for j, (left, right) in enumerate(pairs):
            grad = dot(left[...], right, 0, 0).astype(BF)
            for m, out in enumerate((o0, o1, o2, o3)):

                @pl.when(jnp.bitwise_xor(c, j) == m)
                def _():
                    out[...] = grad

        part_ref[...] = dot(dq_ref[...], w_ref[:, :half], 1, 1) + dot(kv_ref[...], w_ref[:, half:], 1, 1)

    return call(
        run,
        (whole((width, half), BF),) * 4 + (whole((rows, width), F32),),
        "query_grads",
        (pltpu.VMEM((rows, 2 * half), BF),),
    )(x, d_att, att, dq, own, *came, w_query)


def gelu_parts(x):
    cdf = 0.5 * (1.0 + lax.erf(x * 0.7071067811865476))
    return cdf, jnp.exp(-0.5 * x * x) * 0.3989422804014327


def feed(x, mine, other, gains, shifts, w_upper, w_lower_t):
    rows, width = x.shape
    hidden = w_upper.shape[1]

    def run(x_ref, a_ref, b_ref, g_ref, s_ref, wu_ref, wd_ref, n_ref, i_ref, low_ref, pre_ref, act_ref, part_ref):
        n, inverse = row_norm(x_ref[...].astype(F32) + (a_ref[...] + b_ref[...]))
        n_ref[...] = n
        i_ref[...] = inverse
        low_ref[...] = (n * g_ref[0:1] + s_ref[0:1]).astype(BF)
        step = hidden // 4
        total = jnp.zeros((rows, width), F32)
        for i in range(4):
            at = slice(i * step, (i + 1) * step)
            pre = dot(low_ref[...], wu_ref[:, at])
            pre_ref[:, at] = pre
            act_ref[:, at] = (pre * gelu_parts(pre)[0]).astype(BF)
            total += dot(act_ref[:, at], wd_ref[:, at], 1, 1)
        part_ref[...] = total

    return call(
        run,
        (
            whole((rows, width), F32), whole((rows, 1), F32), whole((rows, width), BF), whole((rows, hidden), F32),
            whole((rows, hidden), BF), whole((rows, width), F32),
        ),
        "feed",
    )(x, mine, other, gains, shifts, w_upper, w_lower_t)


def feed_close(n_one, mine, other, gains, shifts, w_token):
    rows, width = n_one.shape
    half = w_token.shape[1]

    def run(n1_ref, a_ref, b_ref, g_ref, s_ref, w_ref, n_ref, i_ref, x2_ref, low_ref, fa_ref):
        first = n1_ref[...] * g_ref[0:1] + s_ref[0:1]
        n, inverse = row_norm(first + (a_ref[...] + b_ref[...]))
        n_ref[...] = n
        i_ref[...] = inverse
        second = n * g_ref[1:2] + s_ref[1:2]
        x2_ref[...] = second
        low_ref[...] = second.astype(BF)
        fa_ref[...] = dot(low_ref[...], w_ref[...]).astype(BF)

    return call(
        run,
        (
            whole((rows, width), F32), whole((rows, 1), F32), whole((rows, width), F32), whole((rows, width), BF),
            whole((rows, half), BF),
        ),
        "feed_close",
    )(n_one, mine, other, gains, shifts, w_token)


def join_back(parts, w_token):
    rows, half = parts[0].shape
    width = w_token.shape[0]

    def run(*refs):
        w_ref, low_ref, part_ref = refs[len(parts) :]
        total = refs[0][...].astype(F32)
        for ref in refs[1 : len(parts)]:
            total = total + ref[...].astype(F32)
        low_ref[...] = total.astype(BF)
        part_ref[...] = dot(low_ref[...], w_ref[...], 1, 1)

    return call(run, (whole((rows, half), BF), whole((rows, width), F32)), "join_back")(*parts, w_token)


def feed_back(d_three, mine, other, n_two, inv_two, gains, pre, w_upper, w_lower_t):
    rows, width = d_three.shape
    hidden = pre.shape[1]

    def run(d_ref, a_ref, b_ref, n_ref, i_ref, g_ref, pre_ref, wu_ref, wd_ref, d2_ref, low_ref, dpre_ref, part_ref, stat_ref):
        e = d_ref[...] + (a_ref[...] + b_ref[...])
        n = n_ref[...]
        stat_ref[...] = jnp.zeros(stat_ref.shape, F32)
        stat_ref[0:1] = column_sum(e * n)
        stat_ref[1:2] = column_sum(e)
        d = row_norm_back(e, n, i_ref[...], g_ref[1:2])
        d2_ref[...] = d
        low_ref[...] = d.astype(BF)
        step = hidden // 4
        total = jnp.zeros((rows, width), F32)
        for i in range(4):
            at = slice(i * step, (i + 1) * step)
            x = pre_ref[:, at]
            cdf, pdf = gelu_parts(x)
            dpre_ref[:, at] = (dot(low_ref[...], wd_ref[:, at]) * (cdf + x * pdf)).astype(BF)
            total += dot(dpre_ref[:, at], wu_ref[:, at], 1, 1)
        part_ref[...] = total

    return call(
        run,
        (
            whole((rows, width), F32), whole((rows, width), BF), whole((rows, hidden), BF), whole((rows, width), F32),
            whole((8, width), F32),
        ),
        "feed_back",
    )(d_three, mine, other, n_two, inv_two, gains, pre, w_upper, w_lower_t)


def neighbours(x):
    return [x] + [swap(x, C, m) for m in (1, 2, 3)]


def body(
    tokens_in, chars_in, segment_ids, char_counts, valid, teacher_tokens, teacher_chars,
    w_qkv, w_out, w_up, w_down, w_gru, gru_bias, w_tok, w_char, w_conv, ln_gain, ln_bias,
):
    nz = lax.axis_size(Z)
    c = lax.axis_index(C)
    t = lax.axis_index(T)
    rows, width = tokens_in.shape
    chars = chars_in.shape[0]
    half = width // 2
    units = gru_bias.shape[2]
    shard = w_qkv.shape[1]
    hidden = w_up.shape[2]
    gains, shifts, bias = ln_gain[0], ln_bias[0], gru_bias[0]

    mine = own_part(tokens_in, 2, t)
    others = core_join(jnp.stack([swap(mine, C, m) for m in (1, 2, 3)]), 1)
    widths = ((3 * half, 4 * units, half, half), (hidden, half, hidden))
    shards = (
        jnp.concatenate(
            [w_qkv[0].reshape(shard, -1), w_gru[0].reshape(shard, -1), w_char[0].reshape(-1, shard).T, w_out[0].T], axis=1
        ),
        jnp.concatenate([w_up[0], w_tok[0], w_down[0].T], axis=1),
    )
    quartered = shard % 64 == 0
    if quartered:
        stacks = [gather_beside(context_quarter(x), 1) for x in shards]
        firsts, nears = first_round(stacks[0][:, :, : shards[0].shape[1]], (others,))
        fars = second_round(firsts, nears)
        stacks[1] = after(stacks[1], fars)
        w_query, w_recur, w_charp_t, w_mix_t = assemble(shards[0], list(zip(firsts, nears, fars)), widths[0])
        firsts, nears = first_round(stacks[1][:, :, : shards[1].shape[1]], ())
    else:
        full = [lax.all_gather(x, Z, axis=0, tiled=True) for x in shards]
        w_query, w_recur, w_charp_t, w_mix_t = jnp.split(full[0], [3 * half, 3 * half + 4 * units, 4 * half + 4 * units], axis=1)
    seq_len = segment_ids.shape[1]
    offset_here = c * rows
    seg_full = segment_ids[0]
    seg_here = lax.dynamic_slice_in_dim(seg_full, offset_here, rows)
    seg_keys = jnp.concatenate(
        [lax.dynamic_slice_in_dim(seg_full, jnp.bitwise_xor(c, m) * rows, rows) for m in range(4)]
    )[:, None]
    counts = char_counts[0]
    ends = jnp.cumsum(counts)
    starts = ends - counts
    places = jnp.arange(chars, dtype=jnp.int32)
    chosen = jnp.logical_and(starts[:, None] <= places[None, :], places[None, :] < ends[:, None])
    pick = chosen.astype(BF)
    valid_tok = valid[0].astype(F32)
    char_seg = jnp.sum(jnp.where(chosen, seg_here[:, None], 0), axis=0)
    valid_chr = jnp.sum(jnp.where(chosen, valid_tok[:, None], 0.0), axis=0)
    prev_seg = seg_full[jnp.maximum(offset_here - 1, 0)]
    next_seg = seg_full[jnp.minimum(offset_here + rows, seq_len - 1)]
    first_keep = jnp.logical_and(c > 0, prev_seg == char_seg[0])
    last_keep = jnp.logical_and(c < lax.axis_size(C) - 1, next_seg == char_seg[-1])
    same = char_seg[1:] == char_seg[:-1]
    keep_up = jnp.concatenate([first_keep[None], same]).astype(F32)
    keep_down = jnp.concatenate([same, last_keep[None]]).astype(F32)
    marks = jnp.stack([keep_up, keep_down, valid_chr], axis=1)
    notes = jnp.stack([counts.astype(F32), valid_tok], axis=1)
    seg_row = seg_here[None, :]

    proj, *scans, ends_here = gru_open(chars_in, w_recur, bias, marks)
    ends_all = neighbours(ends_here)
    if quartered:
        fars = second_round(firsts, nears, ends_all[1:])
    *states, entries, pooled_low, keep, send = gru_close(
        scans, ends_all, pick, after(notes, nears) if quartered else notes, w_charp_t
    )
    fb = (keep + swap(send, T, 1)).astype(BF)
    fbs = gather_beside(fb, 0)

    q, kv, lse, mixed_low, part = attend(after(tokens_in, fb), others, w_query, w_mix_t, seg_keys, seg_row)
    if quartered:
        fars = after(fars, part)
        w_upper, w_token, w_lower_t = assemble(shards[1], list(zip(firsts, nears, fars)), widths[1])
    else:
        w_upper, w_token, w_lower_t = jnp.split(full[1], [hidden, hidden + half], axis=1)
    n_one, inv_one, first_low, pre, act_low, part2 = feed(
        after(tokens_in, fbs), part, swap(part, T, 1), gains, shifts, w_upper, w_lower_t
    )
    gathered = lax.all_gather(jnp.concatenate([own_part(first_low, 2, t, 1), act_low], axis=1), C)
    n_two, inv_two, second, second_low, fa = feed_close(n_one, part2, swap(part2, T, 1), gains, shifts, w_token)
    ends_u = [jnp.concatenate([fa[at], fb[at]]) for at in (slice(0, 1), slice(rows - 1, rows))]
    before, beyond = from_neighbours(*ends_u)
    rim = jnp.concatenate([before[:1], beyond[:1], before[1:], beyond[1:], jnp.zeros((12, half), BF)])
    fas = turned_all(jnp.concatenate([fa, rim]))

    cols = w_conv.shape[-1]
    kernel = w_conv[0].reshape(3, width, cols)
    keep, send = conv_main(fas, fbs, kernel)
    conv = add_split(keep, swap(send, T, 1))
    y_half = side_by_side([conv[0]] + [turn(conv[k], Z, nz - k) for k in range(1, nz)], True)
    out_tok, out_chr, d_res_three, d_res_four, d_mine, stats = close(
        second, y_half, swap(y_half, T, 1), chars_in, teacher_tokens, teacher_chars, pick,
        notes, marks, gains, shifts,
    )

    before, beyond = from_neighbours(d_mine[:1], d_mine[-1:])
    rim = jnp.where(t == 0, beyond, before)
    d_mine = jnp.concatenate([d_mine, rim, jnp.zeros((15, 2 * width), BF)])
    slices = column_slices(d_mine, nz)
    dy_mine = jnp.stack([slices[0]] + [turn(slices[k], Z, k) for k in range(1, nz)])
    dy_other = swap(dy_mine, T, 1)
    du_tok, du_chr = conv_back(after(dy_mine, gathered), dy_other, kernel)
    grad_kernel = conv_grads(fas, fbs, dy_mine, dy_other)
    tok_came = after([turn(du_tok[k], Z, nz - k) for k in range(1, nz)], grad_kernel)
    chr_came = [turn(after(du_chr[k], grad_kernel), Z, nz - k) for k in range(1, nz)]
    dfa, part = join_back([du_tok[0]] + tok_came, w_token)
    grad_kernel = lax.psum_scatter(grad_kernel, C, scatter_dimension=0)

    d_res_two, d_ffn, d_pre, part, stats_two = feed_back(
        d_res_three, part, swap(part, T, 1), n_two, inv_two, gains, pre, w_upper, w_lower_t
    )

    dfb = summed(du_chr[0], after(chr_came, d_pre))
    dfb_full = core_join(dfb, 1)
    d_hidden, *scans, ends_here = gru_back_open(dfb_full, proj, bias, marks, pick, notes, w_charp_t)
    ends_all = neighbours(ends_here)
    pre_own, pre_came = exchange(d_ffn, d_pre, ends_all[1:])
    gathered = [lax.dynamic_index_in_dim(gathered, jnp.bitwise_xor(c, m), 0, keepdims=False) for m in range(4)]
    act_part = jnp.concatenate([own_part(x[:, half:], 4, c, 1) for x in gathered])
    first_all = core_join(jnp.concatenate([x[:, :half] for x in gathered]), 1)
    d_low, d_high, stats_bias, part_chr = gru_back_close(
        scans, ends_all, d_hidden, proj, bias, marks, states, (entries,), w_recur
    )
    d_chr_in = d_res_four + core_sum(part_chr)
    sent = sent_apart(((second_low, dfa), (dfb_full, pooled_low), (chars_in, d_low), (chars_in, d_high)), 1, None)
    chars_own, *chars_sent = sent

    grad_kernel = lax.all_gather(grad_kernel, C)

    pre_came = after(pre_came, chars_sent)
    chars_came = [swap(x, C, m) for m, x in zip((1, 2, 3), chars_sent)]
    d_res_one, d_att, stats_one, dq, dkv_own, *dkv_sends = attend_back(
        after(d_res_two, pre_came), part, swap(part, T, 1), n_one, inv_one, gains, w_mix_t, q, kv, lse, seg_keys, seg_row
    )
    came = [swap(x, C, m) for m, x in zip((1, 2, 3), dkv_sends)]
    ffn_all, pre_part = collected(d_ffn, pre_own, after(pre_came, dq))
    g_up = dot(first_all, pre_part, 0, 0).astype(BF)
    g_down = dot(ffn_all, act_part, 0, 0).astype(BF)
    ffn_piece = lax.psum_scatter(jnp.concatenate([g_up, g_down], axis=1), Z, scatter_dimension=0, tiled=True)
    chars_came = after(chars_came, dq)
    chars_piece = lax.psum_scatter(summed(chars_own, chars_came), Z, scatter_dimension=0, tiled=True)

    counted = jnp.full((1, width), jnp.sum(valid_tok))
    packed = jnp.concatenate([stats[:5], counted, stats_bias[:2], stats_one[:2], stats_two[:2]])
    packed = after(packed, chars_came)
    packed = packed + swap(packed, C, 1)

    *sent, part = query_grads(tokens_in, d_att, mixed_low, dq, dkv_own, came, w_query)
    query_own, *query_sent = sent
    query_came = [swap(x, C, m) for m, x in zip((1, 2, 3), query_sent)]
    d_tok_in = d_res_one + core_sum(part)
    query_blocks = z_split([query_own] + query_came)
    query_turned = turned(query_blocks)
    copies = lax.all_gather(jnp.concatenate(after([ffn_piece, chars_piece], query_sent), axis=1), C)
    copies = after(copies, query_blocks)
    grad_kernel = after(grad_kernel, query_blocks).reshape(2, 2, 3, half // 2, cols).astype(F32)
    grad_kernel = grad_kernel.transpose(2, 0, 1, 3, 4)
    g_up, g_down, g_tok, g_char, g_gru = early_join(copies)
    query_turned = after(query_turned, g_up)
    query_piece = summed(query_blocks[0], query_turned)
    g_out, g_query = query_join([query_piece] + swapped(query_piece))

    packed = after(packed, query_sent)
    packed = packed + swap(packed, C, 2)
    bit = 1
    while bit < nz:
        packed = packed + swap(packed, Z, bit)
        bit *= 2
    loss = jnp.sum(packed[4]) / packed[5, 0]
    gain_total = jnp.stack([packed[8], packed[10], packed[0], packed[1]])[None]
    shift_total = jnp.stack([packed[9], packed[11], packed[2], packed[3]])[None]
    bias_total = packed[None, 6:8, :units]
    return (
        out_tok,
        out_chr,
        loss,
        d_tok_in,
        d_chr_in,
        g_query[None],
        g_out[None],
        g_up[None],
        g_down[None],
        g_gru.reshape(w_gru.shape),
        bias_total,
        g_tok[None],
        g_char.reshape(w_char.shape),
        grad_kernel.reshape(w_conv.shape),
        gain_total,
        shift_total,
    )


def solution(mesh):
    tok = P((Z, C), None)
    seq = P(Z, None)
    placed = (
        tok, tok, seq, tok, P(Z, C), tok, tok,
        P(None, Z, None, T), P(None, T, Z), P(None, Z, T), P(None, T, Z), P(None, Z, None, T),
        P(None, None, T), P(None, Z, T), P(None, None, T, Z), P(None, None, None, T, Z), P(), P(),
    )
    given = (
        tok, tok, P(), tok, tok,
        P(None, Z, None, T), P(None, T, Z), P(None, Z, T), P(None, T, Z), P(None, Z, None, T),
        P(None, None, T), P(None, Z, T), P(None, None, T, Z), P(None, None, None, T, Z), P(), P(),
    )
    return jax.shard_map(body, mesh=mesh, in_specs=placed, out_specs=given, check_vma=False)
```

```python
import functools

import jax
import jax.numpy as jnp
from jax import lax
from jax.experimental import pallas as pl
from jax.experimental.pallas import tpu as pltpu
from jax.sharding import PartitionSpec as P

HD = 64
EPSILON = 1e-05
MASKED_SCORE = -1000000000.0
BF = jnp.bfloat16
F32 = jnp.float32
Z = "fsdp"
C = "context"
T = "tensor"
ROOM = 56 * 1024 * 1024


def dot(a, b, ca=1, cb=0):
    return lax.dot_general(a, b, (((ca,), (cb,)), ((), ())), preferred_element_type=F32)


def swap(x, axis, bit):
    size = lax.axis_size(axis)
    return lax.ppermute(x, axis, [(i, i ^ bit) for i in range(size)])


def turn(x, axis, k):
    size = lax.axis_size(axis)
    return lax.ppermute(x, axis, [(i, (i + k) % size) for i in range(size)])


def core_sum(x):
    return x + swap(x, T, 1)


def own_part(x, count, index, dim=0):
    width = x.shape[dim] // count
    return lax.dynamic_slice_in_dim(x, index * width, width, axis=dim)


def ordered(mine, other, first):
    return jnp.where(first, mine, other), jnp.where(first, other, mine)


def core_join(x, dim):
    other = swap(x, T, 1)
    low, high = ordered(x, other, lax.axis_index(T) == 0)
    return jnp.concatenate([low, high], axis=dim)


def after(x, *deps):
    return lax.optimization_barrier((x, deps))[0]


def whole(shape, dtype):
    return jax.ShapeDtypeStruct(shape, dtype)


def call(kernel, outs, name, scratch=()):
    return pl.pallas_call(
        kernel,
        out_shape=outs,
        scratch_shapes=list(scratch),
        compiler_params=pltpu.CompilerParams(vmem_limit_bytes=ROOM),
        cost_estimate=pl.CostEstimate(flops=1, bytes_accessed=1, transcendentals=0),
        name=name,
    )


def context_quarter(shard):
    return own_part(shard, 4, lax.axis_index(C))


def first_round(stack, wait_for):
    nz, _, n = stack.shape
    z = lax.axis_index(Z)
    half = n // 256 * 128
    index = [lax.rem(z + k, nz) for k in range(1, nz)]
    others = jnp.concatenate([lax.dynamic_slice_in_dim(stack, i, 1) for i in index])
    firsts = [after(others[:, :, cut], *wait_for) for cut in (slice(half), slice(half, n))]
    return firsts, [swap(a, C, b0) for a, (b0, _) in zip(firsts, BOTH)]


def second_round(firsts, nears, wait_for=()):
    both = [jnp.concatenate([a, b]) for a, b in zip(firsts, nears)]
    return [swap(after(x, *wait_for), C, b1) for x, (_, b1) in zip(both, BOTH)]


def assemble(shard, quads, widths):
    count, q = quads[0][0].shape[:2]
    nz = count + 1
    starts = [sum(widths[:i]) for i in range(len(widths))]

    def kernel(*refs):
        outs = refs[7:]
        z = lax.axis_index(Z)
        c = lax.axis_index(C)
        own = pl.ds(pl.multiple_of(z * 4 * q, 16), 4 * q)
        for out, begin, size in zip(outs, starts, widths):
            out[own] = refs[6][:, begin : begin + size]
        col = 0
        for side, (b0, b1) in enumerate(BOTH):
            first, near, far = refs[3 * side : 3 * side + 3]
            width = first.shape[-1]
            spans = []
            for out, begin, size in zip(outs, starts, widths):
                low, high = max(begin, col), min(begin + size, col + width)
                if low < high:
                    spans.append((out, slice(low - col, high - col), slice(low - begin, high - begin)))
            for ref, base, mask in ((first, 0, 0), (near, 0, b0), (far, 0, b1), (far, count, b0 ^ b1)):
                for s in range(count):
                    block = lax.rem(z + 1 + s, nz) * 4 + jnp.bitwise_xor(c, mask)
                    row = pl.multiple_of(block * q, 16)
                    for out, src, dst in spans:
                        out[pl.ds(row, q), dst] = ref[base + s, :, src]
            col += width

    shapes = tuple(whole((nz * 4 * q, w), BF) for w in widths)
    return call(kernel, shapes, "assemble")(*[x for quad in quads for x in quad], shard)


BOTH = ((1, 2), (2, 1))


def side_grads(products):
    rows, width = products[0][0].shape[1], products[0][1].shape[1]

    def kernel(*refs):
        for j in range(len(products)):
            grad = dot(refs[2 * j][...], refs[2 * j + 1][...], 0, 0)
            refs[-1][:, j * width : (j + 1) * width] = grad.astype(BF)

    arrays = [x for pair in products for x in pair]
    return call(kernel, whole((rows, width * len(products)), BF), "grads")(*arrays)


def z_split(parts):
    nz = lax.axis_size(Z)
    rows, width = parts[0].shape
    block = rows // nz

    def kernel(*refs):
        z = lax.axis_index(Z)
        for k, out in enumerate(refs[len(parts) :]):
            at = pl.ds(pl.multiple_of(lax.rem(z + k, nz) * block, 16), block)
            total = refs[0][at].astype(F32)
            for ref in refs[1 : len(parts)]:
                total = total + ref[at].astype(F32)
            out[...] = total.astype(BF)

    return call(kernel, (whole((block, width), BF),) * nz, "z_split")(*parts)


def exchange(copied, split, wait_for=()):
    c = lax.axis_index(C)
    half = after(own_part(copied, 2, lax.axis_index(T), 1), *wait_for)
    pieces = [own_part(split, 4, jnp.bitwise_xor(c, m), 1) for m in range(4)]
    if half.shape[1] != pieces[0].shape[1]:
        return pieces[0], [(swap(half, C, m), swap(pieces[m], C, m)) for m in (1, 2, 3)]
    return pieces[0], [swap(jnp.concatenate([half, pieces[m]]), C, m) for m in (1, 2, 3)]


def collected(copied, own, came):
    rows = copied.shape[0]
    came = [x if isinstance(x, tuple) else (x[:rows], x[rows:]) for x in came]
    halves = jnp.concatenate([a for a, _ in came])
    return jnp.concatenate([copied, core_join(halves, 1)]), jnp.concatenate([own] + [b for _, b in came])


def by_context(parts, outs, stores, name):
    def kernel(*refs):
        c = lax.axis_index(C)
        for m in range(4):
            for j, store in enumerate(stores):

                @pl.when(jnp.bitwise_xor(c, m) == j)
                def _():
                    store(refs[m][...].astype(F32), refs[4:])

    return call(kernel, outs, name)(*parts)


def early_join(parts):
    rows, width = parts[0].shape
    third = width // 3

    def store(j):
        at = slice(j * third, (j + 1) * third)

        def put(x, outs):
            outs[0][:, at] = x[:, :third]
            outs[1][at] = x[:, third : 2 * third].T
            rest = x[:, 2 * third :]
            if j == 0:
                outs[2][...] = rest
            elif j == 1:
                outs[3][...] = rest.T
            else:
                outs[4][:, (j - 2) * third : (j - 1) * third] = rest

        return put

    outs = (
        whole((rows, 4 * third), F32), whole((4 * third, rows), F32), whole((rows, third), F32),
        whole((third, rows), F32), whole((rows, 2 * third), F32),
    )
    return by_context(parts, outs, [store(j) for j in range(4)], "early_join")


def query_join(parts):
    rows, width = parts[0].shape

    def put_out(x, outs):
        outs[0][...] = x.T

    def store(i):
        def put(x, outs):
            outs[1][:, i] = x

        return put

    outs = (whole((width, rows), F32), whole((rows, 3, width), F32))
    return by_context(parts, outs, (put_out, store(0), store(1), store(2)), "query_join")


def turned(blocks):
    return [turn(blocks[k], Z, k) for k in range(1, len(blocks))]


def summed(own, came):
    total = own.astype(F32)
    for x in came:
        total = total + x.astype(F32)
    return total.astype(BF)


def turned_all(x):
    return [x] + [turn(x, Z, k) for k in range(1, lax.axis_size(Z))]


def swapped(x):
    return [swap(x, C, m) for m in (1, 2, 3)]


BESIDE = 1 << 20


def gather_beside(x, dim):
    nz = lax.axis_size(Z)
    extent = x.shape[dim]
    other = x.size // extent
    unit = 128 if dim else 16
    need = -(-BESIDE // (2 * nz * other * unit)) * unit
    if need > extent:
        pads = [(0, 0)] * x.ndim
        pads[dim] = (0, need - extent)
        x = jnp.pad(x, pads)
    return lax.all_gather(x, Z)


def from_neighbours(first, last):
    c = lax.axis_index(C)
    size = lax.axis_size(C)
    both = jnp.stack([first, last])
    near, far = swap(both, C, 1), swap(both, C, 3)
    odd = jnp.bitwise_and(c, 1) == 1
    before = jnp.where(odd, near[1], far[1])
    beyond = jnp.where(odd, far[0], near[0])
    return jnp.where(c > 0, before, 0), jnp.where(c < size - 1, beyond, 0)


def shifted(x, by):
    rows = x.shape[0]
    at = lax.broadcasted_iota(jnp.int32, x.shape, 0)
    if by > 0:
        return jnp.where(at >= by, pltpu.roll(x, by, 0), 0.0)
    return jnp.where(at < rows + by, pltpu.roll(x, rows + by, 0), 0.0)


def block_of(k, nz):
    return lax.rem(lax.axis_index(Z) - k + nz, nz)


def conv_main(toks, chrs, kernel):
    nz = len(toks)
    half = toks[0].shape[1]
    rows = toks[0].shape[0] - 16
    cols = kernel.shape[-1]
    part = rows // 2

    def run(*refs):
        c_ref, w_ref, keep_ref, send_ref, u_ref, rim_ref = refs[nz:]
        t = lax.axis_index(T)
        for k in range(nz):
            at = slice(k * rows, (k + 1) * rows)
            u_ref[at, :half] = refs[k][:rows]
            u_ref[at, half:] = c_ref[block_of(k, nz), :rows]
            at = slice(16 * k, 16 * k + 16)
            rim = refs[k][rows:]
            rim_ref[at, :half] = rim
            rim_ref[at, half:] = jnp.concatenate([rim[2:4], jnp.zeros((14, half), BF)])
        before = dot(rim_ref[...], w_ref[0])
        beyond = dot(rim_ref[...], w_ref[2])
        taps = [dot(u_ref[...], w_ref[m]) for m in range(3)]
        at = lax.broadcasted_iota(jnp.int32, (rows, cols), 0)
        for k in range(nz):
            here = slice(k * rows, (k + 1) * rows)
            total = taps[1][here]
            total = total + jnp.where(at == 0, before[16 * k : 16 * k + 1], pltpu.roll(taps[0][here], 1, 0))
            total = total + jnp.where(
                at == rows - 1, beyond[16 * k + 1 : 16 * k + 2], pltpu.roll(taps[2][here], rows - 1, 0)
            )

            @pl.when(t == 0)
            def _():
                keep_ref[k] = total[:part]
                send_ref[k] = total[part:]

            @pl.when(t != 0)
            def _():
                keep_ref[k] = total[part:]
                send_ref[k] = total[:part]

    shape = whole((nz, part, cols), F32)
    scratch = (pltpu.VMEM((nz * rows, 2 * half), BF), pltpu.VMEM((16 * nz, 2 * half), BF))
    return call(run, (shape, shape), "conv", scratch)(*toks, chrs, kernel)


def add_split(keep, came):
    nz = keep.shape[0]

    def run(*refs):
        for k in range(nz):
            refs[2 + k][...] = (refs[0][k] + refs[1][k]).astype(BF)

    return call(run, (whole(keep.shape[1:], BF),) * nz, "add_split")(keep, came)


def side_by_side(parts, forward):
    nz = len(parts)
    rows, cols = parts[0].shape
    z = lax.axis_index(Z)
    if cols % 128:
        stacked = jnp.stack(parts)
        order = [lax.rem((s - z if forward else z - s) + nz, nz) for s in range(nz)]
        return jnp.concatenate([lax.dynamic_index_in_dim(stacked, i, 0, keepdims=False) for i in order], axis=1)

    def run(*refs):
        z = lax.axis_index(Z)
        for k in range(nz):
            s = lax.rem((z + k if forward else z - k + nz), nz)
            refs[nz][:, pl.ds(pl.multiple_of(s * cols, 128), cols)] = refs[k][...]

    return call(run, whole((rows, nz * cols), BF), "side_by_side")(*parts)


def column_slices(x, nz):
    cols = x.shape[1] // nz
    z = lax.axis_index(Z)
    return [lax.dynamic_slice_in_dim(x, lax.rem(z + k, nz) * cols, cols, axis=1) for k in range(nz)]


def row_norm(v):
    average = jnp.mean(v, axis=-1, keepdims=True)
    centered = v - average
    spread = jnp.mean(centered * centered, axis=-1, keepdims=True)
    inverse = lax.rsqrt(spread + EPSILON)
    return centered * inverse, inverse


def row_norm_back(e, n, inverse, gain):
    ge = e * gain
    one = jnp.mean(ge, axis=-1, keepdims=True)
    two = jnp.mean(ge * n, axis=-1, keepdims=True)
    return inverse * (ge - one - n * two)


def column_sum(x):
    return jnp.sum(x, axis=0, keepdims=True)


def close(second, y_mine, y_other, chars_in, teacher_tok, teacher_chr, pick, notes, marks, gains, shifts):
    rows, width = second.shape
    chars = chars_in.shape[0]
    half = rows // 2
    step = 128

    def run(
        s_ref, ym_ref, yo_ref, c_ref, tt_ref, tc_ref, pick_ref, vt_ref, vc_ref, g_ref, b_ref,
        tok_ref, chr_ref, d3_ref, d4_ref, dy_ref, stat_ref, y_ref, hi_ref, lo_ref,
    ):
        t = lax.axis_index(T)
        y_ref[pl.ds(pl.multiple_of(t * half, 16), half)] = ym_ref[...]
        y_ref[pl.ds(pl.multiple_of((1 - t) * half, 16), half)] = yo_ref[...]
        zero = jnp.zeros((1, width), F32)
        gain_sum, shift_sum, loss = zero, zero, zero
        for i in range(0, rows, step):
            at = slice(i, i + step)
            n, inverse = row_norm(s_ref[at] + y_ref[at, :width].astype(F32))
            out = n * g_ref[2:3] + b_ref[2:3]
            tok_ref[at] = out
            diff = out - tt_ref[at].astype(F32)
            e = vt_ref[at, 1:2] * diff
            loss += column_sum(e * diff)
            gain_sum += column_sum(e * n)
            shift_sum += column_sum(e)
            d3_ref[at] = row_norm_back(e, n, inverse, g_ref[2:3])
        stat_ref[0:1] = gain_sum
        stat_ref[2:3] = shift_sum
        gain_sum, shift_sum = zero, zero
        for i in range(0, chars, step):
            at = slice(i, i + step)
            spread = dot(pick_ref[:, at], y_ref[:, width:], 0, 0)
            n, inverse = row_norm(c_ref[at].astype(F32) + spread)
            out = n * g_ref[3:4] + b_ref[3:4]
            chr_ref[at] = out
            diff = out - tc_ref[at].astype(F32)
            e = vc_ref[at, 2:3] * diff
            loss += column_sum(e * diff)
            gain_sum += column_sum(e * n)
            shift_sum += column_sum(e)
            d = row_norm_back(e, n, inverse, g_ref[3:4])
            d4_ref[at] = d
            high = d.astype(BF)
            hi_ref[at] = high
            lo_ref[at] = (d - high.astype(F32)).astype(BF)
        stat_ref[1:2] = gain_sum
        stat_ref[3:4] = shift_sum
        stat_ref[4:5] = 0.5 * loss
        stat_ref[5:8] = jnp.zeros((3, width), F32)
        mine = pl.ds(pl.multiple_of(t * half, 16), half)
        own = pick_ref[mine]
        dy_ref[:, :width] = d3_ref[mine].astype(BF)
        dy_ref[:, width:] = (dot(own, hi_ref[...]) + dot(own, lo_ref[...])).astype(BF)

    return call(
        run,
        (
            whole((rows, width), F32), whole((chars, width), F32), whole((rows, width), F32),
            whole((chars, width), F32), whole((half, 2 * width), BF), whole((8, width), F32),
        ),
        "close",
        (pltpu.VMEM((rows, 2 * width), BF), pltpu.VMEM((chars, width), BF), pltpu.VMEM((chars, width), BF)),
    )(second, y_mine, y_other, chars_in, teacher_tok, teacher_chr, pick, notes, marks, gains, shifts)


def spread_taps(mine_ref, other_ref, wide, whole_ref):
    nz, part, cols = mine_ref.shape
    part -= 16
    rows = 2 * part
    t = lax.axis_index(T)
    at = lax.broadcasted_iota(jnp.int32, (rows, cols), 0)
    for k in range(nz):
        whole_ref[pl.ds(pl.multiple_of(t * part, 16), part)] = mine_ref[k, :part]
        whole_ref[pl.ds(pl.multiple_of((1 - t) * part, 16), part)] = other_ref[k, :part]
        a = mine_ref[k, part:].astype(F32)[0:1]
        b = other_ref[k, part:].astype(F32)[0:1]
        above, below = jnp.where(t == 0, a, b), jnp.where(t == 0, b, a)
        d = whole_ref[...].astype(F32)
        wide[1, k] = whole_ref[...]
        wide[0, k] = jnp.where(at == rows - 1, above, pltpu.roll(d, rows - 1, 0)).astype(BF)
        wide[2, k] = jnp.where(at == 0, below, pltpu.roll(d, 1, 0)).astype(BF)


def tap_scratch(mine):
    nz, part, cols = mine.shape
    rows = 2 * (part - 16)
    return pltpu.VMEM((3, nz, rows, cols), BF), pltpu.VMEM((rows, cols), BF)


def conv_back(mine, other, kernel):
    nz, part, cols = mine.shape
    rows = 2 * (part - 16)
    half = kernel.shape[1] // 2

    def run(*refs):
        m_ref, o_ref, w_ref = refs[:3]
        outs, (wide, whole_ref) = refs[3 : 3 + 2 * nz], refs[3 + 2 * nz :]
        spread_taps(m_ref, o_ref, wide, whole_ref)
        for side in range(2):
            at = slice(side * half, (side + 1) * half)
            x = sum(dot(wide[m].reshape(nz * rows, cols), w_ref[m, at], 1, 1) for m in range(3)).astype(BF)
            for k in range(nz):
                outs[side * nz + k][...] = x[k * rows : (k + 1) * rows]

    shapes = (whole((rows, half), BF),) * (2 * nz)
    outs = call(run, shapes, "conv_back", tap_scratch(mine))(mine, other, kernel)
    return outs[:nz], outs[nz:]


def conv_grads(toks, chrs, mine, other):
    nz, part, cols = mine.shape
    rows = 2 * (part - 16)
    half = toks[0].shape[1]

    def run(*refs):
        c_ref, m_ref, o_ref, out_ref, wide, whole_ref = refs[nz:]
        spread_taps(m_ref, o_ref, wide, whole_ref)
        for m in range(3):
            for side in range(2):
                total = jnp.zeros((half, cols), F32)
                for k in range(nz):
                    u = c_ref[block_of(k, nz), :rows] if side else refs[k][:rows]
                    total += dot(u, wide[m, k], 0, 0)
                for r in range(2):
                    out_ref[2 * side + r, m] = total[r * half // 2 : (r + 1) * half // 2].astype(BF)

    shape = whole((4, 3, half // 2, cols), BF)
    return call(run, shape, "conv_grads", tap_scratch(mine))(*toks, chrs, mine, other)


def scan_pair(a, b, e, f):
    n = a.shape[0]
    rows = lax.broadcasted_iota(jnp.int32, a.shape, 0)
    step = 1
    while step < n:
        has = rows >= step
        pa = jnp.where(has, pltpu.roll(a, step, 0), 1.0)
        pb = jnp.where(has, pltpu.roll(b, step, 0), 0.0)
        b = b + a * pb
        a = a * pa
        has = rows < n - step
        pe = jnp.where(has, pltpu.roll(e, n - step, 0), 1.0)
        pf = jnp.where(has, pltpu.roll(f, n - step, 0), 0.0)
        f = f + e * pf
        e = e * pe
        step *= 2
    return a, b, e, f


def store_scans(scans, refs):
    a, b, e, f = scans
    n = a.shape[0]
    for ref, x in zip(refs[:4], scans):
        ref[...] = x
    ends = refs[4]
    ends[...] = jnp.zeros(ends.shape, F32)
    ends[0:1], ends[1:2], ends[2:3], ends[3:4] = a[n - 1 :], b[n - 1 :], e[:1], f[:1]


def scan_shapes(chars, units):
    return (whole((chars, units), F32),) * 4 + (whole((8, units), F32),)


def entering(refs):
    c = lax.axis_index(C)
    up = jnp.zeros((1, refs[0].shape[1]), F32)
    down = up
    for j in range(4):
        for m, ref in enumerate(refs):
            now = jnp.bitwise_xor(c, j) == m
            up = jnp.where(jnp.logical_and(now, j < c), ref[0:1] * up + ref[1:2], up)
    for j in (3, 2, 1, 0):
        for m, ref in enumerate(refs):
            now = jnp.bitwise_xor(c, j) == m
            down = jnp.where(jnp.logical_and(now, j > c), ref[2:3] * down + ref[3:4], down)
    return up, down


def gates(proj_ref, bias_ref, units):
    up = jax.nn.sigmoid(proj_ref[:, :units] + bias_ref[0:1])
    down = jax.nn.sigmoid(proj_ref[:, 2 * units : 3 * units] + bias_ref[1:2])
    return up, down


def gru_open(chars_in, w_recur, bias, marks):
    chars = chars_in.shape[0]
    units = bias.shape[1]

    def run(c_ref, w_ref, b_ref, m_ref, proj_ref, *outs):
        proj_ref[...] = dot(c_ref[...], w_ref[...])
        up, down = gates(proj_ref, b_ref, units)
        store_scans(
            scan_pair(
                (1.0 - up) * m_ref[:, 0:1], up * proj_ref[:, units : 2 * units],
                (1.0 - down) * m_ref[:, 1:2], down * proj_ref[:, 3 * units :],
            ),
            outs,
        )

    return call(run, (whole((chars, 4 * units), F32),) + scan_shapes(chars, units), "gru_open")(
        chars_in, w_recur, bias, marks
    )


def gru_close(scans, ends, pick, notes, w_charp_t):
    chars, units = scans[0].shape
    rows = pick.shape[0]
    half = w_charp_t.shape[0] // 2

    def run(cu, hu, cd, hd, e0, e1, e2, e3, p_ref, n_ref, w_ref, up_ref, down_ref, in_ref, pool_ref, keep_ref, send_ref):
        up, down = entering((e0, e1, e2, e3))
        in_ref[...] = jnp.zeros(in_ref.shape, F32)
        in_ref[0:1], in_ref[1:2] = up, down
        up_ref[...] = hu[...] + cu[...] * up
        down_ref[...] = hd[...] + cd[...] * down
        for ref, at in ((up_ref, slice(units)), (down_ref, slice(units, 2 * units))):
            pool_ref[:, at] = (dot(p_ref[...], ref[...].astype(BF)) / n_ref[:, 0:1]).astype(BF)
        t = lax.axis_index(T)
        low = dot(pool_ref[...], w_ref[:half], 1, 1)
        high = dot(pool_ref[...], w_ref[half:], 1, 1)
        keep_ref[...] = jnp.where(t == 0, low, high)
        send_ref[...] = jnp.where(t == 0, high, low)

    state = whole((chars, units), F32)
    return call(
        run,
        (
            state, state, whole((8, units), F32), whole((rows, 2 * units), BF),
            whole((rows, half), F32), whole((rows, half), F32),
        ),
        "gru_close",
    )(*scans, *ends, pick, notes, w_charp_t)


def gru_back_open(dfb, proj, bias, marks, pick, notes, w_charp_t):
    chars = proj.shape[0]
    units = bias.shape[1]

    def run(d_ref, proj_ref, b_ref, m_ref, p_ref, n_ref, w_ref, dh_ref, *outs):
        pooled = dot(d_ref[...], w_ref[...]) / n_ref[:, 0:1]
        high = pooled.astype(BF)
        low = (pooled - high.astype(F32)).astype(BF)
        dh_ref[...] = dot(p_ref[...], high, 0, 0) + dot(p_ref[...], low, 0, 0)
        up, down = gates(proj_ref, b_ref, units)
        up = (1.0 - up) * m_ref[:, 0:1]
        down = (1.0 - down) * m_ref[:, 1:2]
        store_scans(scan_pair(down, down * dh_ref[:, units:], up, up * dh_ref[:, :units]), outs)

    return call(run, (whole((chars, 2 * units), F32),) + scan_shapes(chars, units), "gru_back_open")(
        dfb, proj, bias, marks, pick, notes, w_charp_t
    )


def gru_back_close(scans, ends, d_hidden, proj, bias, marks, states, entries, w_recur):
    chars, units = scans[0].shape
    width = w_recur.shape[0]

    def run(
        cd, md, cu, mu, e0, e1, e2, e3, dh_ref, proj_ref, b_ref, m_ref, hu_ref, hd_ref, in_ref, w_ref,
        low_ref, high_ref, stat_ref, part_ref,
    ):
        from_below, from_above = entering((e0, e1, e2, e3))
        at = lax.broadcasted_iota(jnp.int32, (chars, units), 0)
        first, last = at == 0, at == chars - 1
        up, down = gates(proj_ref, b_ref, units)
        m = mu[...] + cu[...] * from_above
        lam = dh_ref[:, :units] + jnp.where(last, from_above, pltpu.roll(m, chars - 1, 0))
        before = jnp.where(first, in_ref[0:1], pltpu.roll(hu_ref[...], 1, 0))
        d_gate = lam * (proj_ref[:, units : 2 * units] - m_ref[:, 0:1] * before) * up * (1.0 - up)
        low_ref[:, :units] = d_gate.astype(BF)
        low_ref[:, units:] = (lam * up).astype(BF)
        stat_ref[...] = jnp.zeros(stat_ref.shape, F32)
        stat_ref[0:1, :units] = column_sum(d_gate)
        m = md[...] + cd[...] * from_below
        lam = dh_ref[:, units:] + jnp.where(first, from_below, pltpu.roll(m, 1, 0))
        beyond = jnp.where(last, in_ref[1:2], pltpu.roll(hd_ref[...], chars - 1, 0))
        d_gate = lam * (proj_ref[:, 3 * units :] - m_ref[:, 1:2] * beyond) * down * (1.0 - down)
        high_ref[:, :units] = d_gate.astype(BF)
        high_ref[:, units:] = (lam * down).astype(BF)
        stat_ref[1:2, :units] = column_sum(d_gate)
        part_ref[...] = dot(low_ref[...], w_ref[:, : 2 * units], 1, 1) + dot(high_ref[...], w_ref[:, 2 * units :], 1, 1)

    part = whole((chars, 2 * units), BF)
    return call(
        run, (part, part, whole((8, width), F32), whole((chars, width), F32)), "gru_back_close"
    )(*scans, *ends, d_hidden, proj, bias, marks, *states, *entries, w_recur)


def score_block(k, q, seg_k, seg_q):
    s = dot(k, q, 1, 1) * HD ** (-0.5)
    return jnp.where(seg_k == seg_q, s, MASKED_SCORE)


def attend(x, others, w_query, w_mix_t, seg_keys, seg_here):
    rows, width = x.shape
    half = w_mix_t.shape[1]
    heads = half // HD
    keys = rows * (1 + others.shape[0])

    def run(x_ref, o_ref, w_ref, wm_ref, sk_ref, sq_ref, q_ref, kv_ref, lse_ref, att_ref, part_ref, turned):
        q_ref[...] = dot(x_ref[...], w_ref[:, :half]).astype(BF)
        kv_ref[:rows] = dot(x_ref[...], w_ref[:, half:]).astype(BF)
        for m in range(others.shape[0]):
            kv_ref[(m + 1) * rows : (m + 2) * rows] = dot(o_ref[m], w_ref[:, half:]).astype(BF)
        lse_ref[...] = jnp.zeros(lse_ref.shape, F32)
        for h in range(heads):
            at = slice(h * HD, (h + 1) * HD)
            s = score_block(kv_ref[:, at], q_ref[:, at], sk_ref[...], sq_ref[...])
            highest = jnp.max(s, axis=0, keepdims=True)
            lse = highest + jnp.log(jnp.sum(jnp.exp(s - highest), axis=0, keepdims=True))
            lse_ref[h : h + 1] = lse
            probs = jnp.exp(s - lse).astype(BF)
            turned[at] = dot(kv_ref[:, half + h * HD : half + (h + 1) * HD], probs, 0, 0)
        att_ref[...] = turned[...].T.astype(BF)
        part_ref[...] = dot(att_ref[...], wm_ref[...], 1, 1)

    return call(
        run,
        (
            whole((rows, half), BF), whole((keys, 2 * half), BF), whole((8, rows), F32),
            whole((rows, half), BF), whole((rows, width), F32),
        ),
        "attend",
        (pltpu.VMEM((half, rows), F32),),
    )(x, others, w_query, w_mix_t, seg_keys, seg_here)


def attend_back(d_two, mine, other, n_one, inv_one, gains, w_mix_t, q, kv, lse, seg_keys, seg_here):
    rows, width = d_two.shape
    half = q.shape[1]
    heads = half // HD
    keys = kv.shape[0]
    count = keys // rows

    def run(
        d_ref, a_ref, b_ref, n_ref, i_ref, g_ref, wm_ref, q_ref, kv_ref, lse_ref, sk_ref, sq_ref,
        d1_ref, datt_ref, stat_ref, dq_ref, own_ref, s1_ref, s2_ref, s3_ref, da_ref, turned,
    ):
        e = d_ref[...] + (a_ref[...] + b_ref[...])
        n = n_ref[...]
        stat_ref[...] = jnp.zeros(stat_ref.shape, F32)
        stat_ref[0:1] = column_sum(e * n)
        stat_ref[1:2] = column_sum(e)
        d = row_norm_back(e, n, i_ref[...], g_ref[0:1])
        d1_ref[...] = d
        datt_ref[...] = d.astype(BF)
        da_ref[...] = dot(datt_ref[...], wm_ref[...]).astype(BF)
        scale = HD ** (-0.5)
        sends = (None, s1_ref, s2_ref, s3_ref)
        for h in range(heads):
            at = slice(h * HD, (h + 1) * HD)
            vt = slice(half + h * HD, half + (h + 1) * HD)
            s = score_block(kv_ref[:, at], q_ref[:, at], sk_ref[...], sq_ref[...])
            p = jnp.exp(s - lse_ref[h : h + 1])
            dp = dot(kv_ref[:, vt], da_ref[:, at], 1, 1)
            delta = jnp.sum(p * dp, axis=0, keepdims=True)
            ds = (p * (dp - delta)).astype(BF)
            turned[at] = dot(kv_ref[:, at], ds, 0, 0) * scale
            dk = dot(ds, q_ref[:, at]) * scale
            dv = dot(p.astype(BF), da_ref[:, at])
            own_ref[:, at] = dk[:rows]
            own_ref[:, vt] = dv[:rows]
            for m in range(1, count):
                sends[m][:, at] = dk[m * rows : (m + 1) * rows].astype(BF)
                sends[m][:, vt] = dv[m * rows : (m + 1) * rows].astype(BF)
        dq_ref[...] = turned[...].T.astype(BF)

    send = whole((rows, 2 * half), BF)
    return call(
        run,
        (
            whole((rows, width), F32), whole((rows, width), BF), whole((8, width), F32), whole((rows, half), BF),
            whole((rows, 2 * half), F32), send, send, send,
        ),
        "attend_back",
        (pltpu.VMEM((rows, half), BF), pltpu.VMEM((half, rows), F32)),
    )(d_two, mine, other, n_one, inv_one, gains, w_mix_t, q, kv, lse, seg_keys, seg_here)


def query_grads(x, d_att, att, dq, own, came, w_query):
    rows, width = x.shape
    half = att.shape[1]

    def run(x_ref, da_ref, att_ref, dq_ref, own_ref, c1, c2, c3, w_ref, o0, o1, o2, o3, part_ref, kv_ref):
        c = lax.axis_index(C)
        kv_ref[...] = (own_ref[...] + c1[...].astype(F32) + c2[...].astype(F32) + c3[...].astype(F32)).astype(BF)
        pairs = (
            (da_ref, att_ref[...]), (x_ref, dq_ref[...]), (x_ref, kv_ref[:, :half]), (x_ref, kv_ref[:, half:]),
        )
        for j, (left, right) in enumerate(pairs):
            grad = dot(left[...], right, 0, 0).astype(BF)
            for m, out in enumerate((o0, o1, o2, o3)):

                @pl.when(jnp.bitwise_xor(c, j) == m)
                def _():
                    out[...] = grad

        part_ref[...] = dot(dq_ref[...], w_ref[:, :half], 1, 1) + dot(kv_ref[...], w_ref[:, half:], 1, 1)

    return call(
        run,
        (whole((width, half), BF),) * 4 + (whole((rows, width), F32),),
        "query_grads",
        (pltpu.VMEM((rows, 2 * half), BF),),
    )(x, d_att, att, dq, own, *came, w_query)


def gelu_parts(x):
    cdf = 0.5 * (1.0 + lax.erf(x * 0.7071067811865476))
    return cdf, jnp.exp(-0.5 * x * x) * 0.3989422804014327


def feed(x, mine, other, gains, shifts, w_upper, w_lower_t):
    rows, width = x.shape
    hidden = w_upper.shape[1]

    def run(x_ref, a_ref, b_ref, g_ref, s_ref, wu_ref, wd_ref, n_ref, i_ref, low_ref, pre_ref, act_ref, part_ref):
        n, inverse = row_norm(x_ref[...].astype(F32) + (a_ref[...] + b_ref[...]))
        n_ref[...] = n
        i_ref[...] = inverse
        low_ref[...] = (n * g_ref[0:1] + s_ref[0:1]).astype(BF)
        step = hidden // 4
        total = jnp.zeros((rows, width), F32)
        for i in range(4):
            at = slice(i * step, (i + 1) * step)
            pre = dot(low_ref[...], wu_ref[:, at])
            pre_ref[:, at] = pre
            act_ref[:, at] = (pre * gelu_parts(pre)[0]).astype(BF)
            total += dot(act_ref[:, at], wd_ref[:, at], 1, 1)
        part_ref[...] = total

    return call(
        run,
        (
            whole((rows, width), F32), whole((rows, 1), F32), whole((rows, width), BF), whole((rows, hidden), F32),
            whole((rows, hidden), BF), whole((rows, width), F32),
        ),
        "feed",
    )(x, mine, other, gains, shifts, w_upper, w_lower_t)


def feed_close(n_one, mine, other, gains, shifts, w_token):
    rows, width = n_one.shape
    half = w_token.shape[1]

    def run(n1_ref, a_ref, b_ref, g_ref, s_ref, w_ref, n_ref, i_ref, x2_ref, low_ref, fa_ref):
        first = n1_ref[...] * g_ref[0:1] + s_ref[0:1]
        n, inverse = row_norm(first + (a_ref[...] + b_ref[...]))
        n_ref[...] = n
        i_ref[...] = inverse
        second = n * g_ref[1:2] + s_ref[1:2]
        x2_ref[...] = second
        low_ref[...] = second.astype(BF)
        fa_ref[...] = dot(low_ref[...], w_ref[...]).astype(BF)

    return call(
        run,
        (
            whole((rows, width), F32), whole((rows, 1), F32), whole((rows, width), F32), whole((rows, width), BF),
            whole((rows, half), BF),
        ),
        "feed_close",
    )(n_one, mine, other, gains, shifts, w_token)


def join_back(parts, w_token):
    rows, half = parts[0].shape
    width = w_token.shape[0]

    def run(*refs):
        w_ref, low_ref, part_ref = refs[len(parts) :]
        total = refs[0][...].astype(F32)
        for ref in refs[1 : len(parts)]:
            total = total + ref[...].astype(F32)
        low_ref[...] = total.astype(BF)
        part_ref[...] = dot(low_ref[...], w_ref[...], 1, 1)

    return call(run, (whole((rows, half), BF), whole((rows, width), F32)), "join_back")(*parts, w_token)


def feed_back(d_three, mine, other, n_two, inv_two, gains, pre, w_upper, w_lower_t):
    rows, width = d_three.shape
    hidden = pre.shape[1]

    def run(d_ref, a_ref, b_ref, n_ref, i_ref, g_ref, pre_ref, wu_ref, wd_ref, d2_ref, low_ref, dpre_ref, part_ref, stat_ref):
        e = d_ref[...] + (a_ref[...] + b_ref[...])
        n = n_ref[...]
        stat_ref[...] = jnp.zeros(stat_ref.shape, F32)
        stat_ref[0:1] = column_sum(e * n)
        stat_ref[1:2] = column_sum(e)
        d = row_norm_back(e, n, i_ref[...], g_ref[1:2])
        d2_ref[...] = d
        low_ref[...] = d.astype(BF)
        step = hidden // 4
        total = jnp.zeros((rows, width), F32)
        for i in range(4):
            at = slice(i * step, (i + 1) * step)
            x = pre_ref[:, at]
            cdf, pdf = gelu_parts(x)
            dpre_ref[:, at] = (dot(low_ref[...], wd_ref[:, at]) * (cdf + x * pdf)).astype(BF)
            total += dot(dpre_ref[:, at], wu_ref[:, at], 1, 1)
        part_ref[...] = total

    return call(
        run,
        (
            whole((rows, width), F32), whole((rows, width), BF), whole((rows, hidden), BF), whole((rows, width), F32),
            whole((8, width), F32),
        ),
        "feed_back",
    )(d_three, mine, other, n_two, inv_two, gains, pre, w_upper, w_lower_t)


def neighbours(x):
    return [x] + [swap(x, C, m) for m in (1, 2, 3)]


def body(
    tokens_in, chars_in, segment_ids, char_counts, valid, teacher_tokens, teacher_chars,
    w_qkv, w_out, w_up, w_down, w_gru, gru_bias, w_tok, w_char, w_conv, ln_gain, ln_bias,
):
    nz = lax.axis_size(Z)
    c = lax.axis_index(C)
    t = lax.axis_index(T)
    rows, width = tokens_in.shape
    chars = chars_in.shape[0]
    half = width // 2
    units = gru_bias.shape[2]
    shard = w_qkv.shape[1]
    hidden = w_up.shape[2]
    gains, shifts, bias = ln_gain[0], ln_bias[0], gru_bias[0]

    mine = own_part(tokens_in, 2, t)
    others = core_join(jnp.stack([swap(mine, C, m) for m in (1, 2, 3)]), 1)
    widths = ((3 * half, 4 * units, half, half), (hidden, half, hidden))
    shards = (
        jnp.concatenate(
            [w_qkv[0].reshape(shard, -1), w_gru[0].reshape(shard, -1), w_char[0].reshape(-1, shard).T, w_out[0].T], axis=1
        ),
        jnp.concatenate([w_up[0], w_tok[0], w_down[0].T], axis=1),
    )
    quartered = shard % 64 == 0
    if quartered:
        stacks = [gather_beside(context_quarter(x), 1) for x in shards]
        firsts, nears = first_round(stacks[0][:, :, : shards[0].shape[1]], (others,))
        fars = second_round(firsts, nears)
        stacks[1] = after(stacks[1], fars)
        w_query, w_recur, w_charp_t, w_mix_t = assemble(shards[0], list(zip(firsts, nears, fars)), widths[0])
        firsts, nears = first_round(stacks[1][:, :, : shards[1].shape[1]], ())
    else:
        full = [lax.all_gather(x, Z, axis=0, tiled=True) for x in shards]
        w_query, w_recur, w_charp_t, w_mix_t = jnp.split(full[0], [3 * half, 3 * half + 4 * units, 4 * half + 4 * units], axis=1)
    seq_len = segment_ids.shape[1]
    offset_here = c * rows
    seg_full = segment_ids[0]
    seg_here = lax.dynamic_slice_in_dim(seg_full, offset_here, rows)
    seg_keys = jnp.concatenate(
        [lax.dynamic_slice_in_dim(seg_full, jnp.bitwise_xor(c, m) * rows, rows) for m in range(4)]
    )[:, None]
    counts = char_counts[0]
    ends = jnp.cumsum(counts)
    starts = ends - counts
    places = jnp.arange(chars, dtype=jnp.int32)
    chosen = jnp.logical_and(starts[:, None] <= places[None, :], places[None, :] < ends[:, None])
    pick = chosen.astype(BF)
    valid_tok = valid[0].astype(F32)
    char_seg = jnp.sum(jnp.where(chosen, seg_here[:, None], 0), axis=0)
    valid_chr = jnp.sum(jnp.where(chosen, valid_tok[:, None], 0.0), axis=0)
    prev_seg = seg_full[jnp.maximum(offset_here - 1, 0)]
    next_seg = seg_full[jnp.minimum(offset_here + rows, seq_len - 1)]
    first_keep = jnp.logical_and(c > 0, prev_seg == char_seg[0])
    last_keep = jnp.logical_and(c < lax.axis_size(C) - 1, next_seg == char_seg[-1])
    same = char_seg[1:] == char_seg[:-1]
    keep_up = jnp.concatenate([first_keep[None], same]).astype(F32)
    keep_down = jnp.concatenate([same, last_keep[None]]).astype(F32)
    marks = jnp.stack([keep_up, keep_down, valid_chr], axis=1)
    notes = jnp.stack([counts.astype(F32), valid_tok], axis=1)
    seg_row = seg_here[None, :]

    proj, *scans, ends_here = gru_open(chars_in, w_recur, bias, marks)
    ends_all = neighbours(ends_here)
    if quartered:
        fars = second_round(firsts, nears, ends_all[1:])
    *states, entries, pooled_low, keep, send = gru_close(
        scans, ends_all, pick, after(notes, nears) if quartered else notes, w_charp_t
    )
    fb = (keep + swap(send, T, 1)).astype(BF)
    fbs = gather_beside(fb, 0)

    q, kv, lse, mixed_low, part = attend(after(tokens_in, fb), others, w_query, w_mix_t, seg_keys, seg_row)
    if quartered:
        fars = after(fars, part)
        w_upper, w_token, w_lower_t = assemble(shards[1], list(zip(firsts, nears, fars)), widths[1])
    else:
        w_upper, w_token, w_lower_t = jnp.split(full[1], [hidden, hidden + half], axis=1)
    n_one, inv_one, first_low, pre, act_low, part2 = feed(
        after(tokens_in, fbs), part, swap(part, T, 1), gains, shifts, w_upper, w_lower_t
    )
    gathered = lax.all_gather(jnp.concatenate([own_part(first_low, 2, t, 1), act_low], axis=1), C)
    n_two, inv_two, second, second_low, fa = feed_close(n_one, part2, swap(part2, T, 1), gains, shifts, w_token)
    ends_u = [jnp.concatenate([fa[at], fb[at]]) for at in (slice(0, 1), slice(rows - 1, rows))]
    before, beyond = from_neighbours(*ends_u)
    rim = jnp.concatenate([before[:1], beyond[:1], before[1:], beyond[1:], jnp.zeros((12, half), BF)])
    fas = turned_all(jnp.concatenate([fa, rim]))

    cols = w_conv.shape[-1]
    kernel = w_conv[0].reshape(3, width, cols)
    keep, send = conv_main(fas, fbs, kernel)
    conv = add_split(keep, swap(send, T, 1))
    y_half = side_by_side([conv[0]] + [turn(conv[k], Z, nz - k) for k in range(1, nz)], True)
    out_tok, out_chr, d_res_three, d_res_four, d_mine, stats = close(
        second, y_half, swap(y_half, T, 1), chars_in, teacher_tokens, teacher_chars, pick,
        notes, marks, gains, shifts,
    )

    before, beyond = from_neighbours(d_mine[:1], d_mine[-1:])
    rim = jnp.where(t == 0, beyond, before)
    d_mine = jnp.concatenate([d_mine, rim, jnp.zeros((15, 2 * width), BF)])
    slices = column_slices(d_mine, nz)
    dy_mine = jnp.stack([slices[0]] + [turn(slices[k], Z, k) for k in range(1, nz)])
    dy_other = swap(dy_mine, T, 1)
    du_tok, du_chr = conv_back(after(dy_mine, gathered), dy_other, kernel)
    grad_kernel = conv_grads(fas, fbs, dy_mine, dy_other)
    tok_came = after([turn(du_tok[k], Z, nz - k) for k in range(1, nz)], grad_kernel)
    chr_came = [turn(after(du_chr[k], grad_kernel), Z, nz - k) for k in range(1, nz)]
    dfa, part = join_back([du_tok[0]] + tok_came, w_token)
    grad_kernel = lax.psum_scatter(grad_kernel, C, scatter_dimension=0)

    d_res_two, d_ffn, d_pre, part, stats_two = feed_back(
        d_res_three, part, swap(part, T, 1), n_two, inv_two, gains, pre, w_upper, w_lower_t
    )

    dfb = summed(du_chr[0], after(chr_came, d_pre))
    dfb_full = core_join(dfb, 1)
    d_hidden, *scans, ends_here = gru_back_open(dfb_full, proj, bias, marks, pick, notes, w_charp_t)
    ends_all = neighbours(ends_here)
    pre_own, pre_came = exchange(d_ffn, d_pre, ends_all[1:])
    gathered = [lax.dynamic_index_in_dim(gathered, jnp.bitwise_xor(c, m), 0, keepdims=False) for m in range(4)]
    act_part = jnp.concatenate([own_part(x[:, half:], 4, c, 1) for x in gathered])
    first_all = core_join(jnp.concatenate([x[:, :half] for x in gathered]), 1)
    d_low, d_high, stats_bias, part_chr = gru_back_close(
        scans, ends_all, d_hidden, proj, bias, marks, states, (entries,), w_recur
    )
    d_chr_in = d_res_four + core_sum(part_chr)
    chars_grads = side_grads(((second_low, dfa), (dfb_full, pooled_low), (chars_in, d_low), (chars_in, d_high)))
    chars_grads_z = lax.psum_scatter(chars_grads, Z, scatter_dimension=0, tiled=True)
    grad_kernel = lax.all_gather(grad_kernel, C)

    d_res_one, d_att, stats_one, dq, dkv_own, *dkv_sends = attend_back(
        after(d_res_two, chars_grads), part, swap(part, T, 1), n_one, inv_one, gains, w_mix_t, q, kv, lse, seg_keys, seg_row
    )
    came = [swap(x, C, m) for m, x in zip((1, 2, 3), dkv_sends)]
    ffn_all, pre_part = collected(d_ffn, pre_own, after(pre_came, dq))
    g_up = dot(first_all, pre_part, 0, 0).astype(BF)
    g_down = dot(ffn_all, act_part, 0, 0).astype(BF)
    ffn_piece = lax.psum_scatter(jnp.concatenate([g_up, g_down], axis=1), Z, scatter_dimension=0, tiled=True)
    counted = jnp.full((1, width), jnp.sum(valid_tok))
    packed = jnp.concatenate([stats[:5], counted, stats_bias[:2], stats_one[:2], stats_two[:2]])
    bit = 1
    while bit < nz:
        packed = packed + swap(packed, Z, bit)
        bit *= 2

    *sent, part = query_grads(tokens_in, d_att, mixed_low, dq, dkv_own, after(came, packed), w_query)
    query_own, *query_sent = sent
    query_came = [swap(x, C, m) for m, x in zip((1, 2, 3), query_sent)]
    d_tok_in = d_res_one + core_sum(part)
    quarters = after(chars_grads_z, query_sent)
    quarters = [own_part(quarters, 4, jnp.bitwise_xor(c, m), 1) for m in range(4)]
    chars_came = [swap(quarters[m], C, m) for m in (1, 2, 3)]
    query_came = after(query_came, chars_came)
    query_blocks = z_split([query_own] + query_came)
    query_turned = turned(query_blocks)
    ffn_piece = after(ffn_piece, query_came)
    chars_piece = summed(quarters[0], chars_came)
    early = jnp.concatenate([ffn_piece, chars_piece], axis=1)
    early_copies = swapped(early)
    query_piece = summed(query_blocks[0], query_turned)
    query_copies = swapped(query_piece)
    g_up, g_down, g_tok, g_char, g_gru = early_join([early] + after(early_copies, query_piece))
    grad_kernel = after(grad_kernel, g_up).reshape(2, 2, 3, half // 2, cols).astype(F32)
    grad_kernel = grad_kernel.transpose(2, 0, 1, 3, 4)
    g_out, g_query = query_join([query_piece] + after(query_copies, g_up))

    packed = after(packed, query_came)
    for bit in (1, 2):
        packed = packed + swap(packed, C, bit)
    loss = jnp.sum(packed[4]) / packed[5, 0]
    gain_total = jnp.stack([packed[8], packed[10], packed[0], packed[1]])[None]
    shift_total = jnp.stack([packed[9], packed[11], packed[2], packed[3]])[None]
    bias_total = packed[None, 6:8, :units]
    return (
        out_tok,
        out_chr,
        loss,
        d_tok_in,
        d_chr_in,
        g_query[None],
        g_out[None],
        g_up[None],
        g_down[None],
        g_gru.reshape(w_gru.shape),
        bias_total,
        g_tok[None],
        g_char.reshape(w_char.shape),
        grad_kernel.reshape(w_conv.shape),
        gain_total,
        shift_total,
    )


def solution(mesh):
    tok = P((Z, C), None)
    seq = P(Z, None)
    placed = (
        tok, tok, seq, tok, P(Z, C), tok, tok,
        P(None, Z, None, T), P(None, T, Z), P(None, Z, T), P(None, T, Z), P(None, Z, None, T),
        P(None, None, T), P(None, Z, T), P(None, None, T, Z), P(None, None, None, T, Z), P(), P(),
    )
    given = (
        tok, tok, P(), tok, tok,
        P(None, Z, None, T), P(None, T, Z), P(None, Z, T), P(None, T, Z), P(None, Z, None, T),
        P(None, None, T), P(None, Z, T), P(None, None, T, Z), P(None, None, None, T, Z), P(), P(),
    )
    return jax.shard_map(body, mesh=mesh, in_specs=placed, out_specs=given, check_vma=False)
```

```python
import functools

import jax
import jax.numpy as jnp
from jax import lax
from jax.experimental import pallas as pl
from jax.experimental.pallas import tpu as pltpu
from jax.sharding import PartitionSpec as P

HD = 64
EPSILON = 1e-05
MASKED_SCORE = -1000000000.0
BF = jnp.bfloat16
F32 = jnp.float32
Z = "fsdp"
C = "context"
T = "tensor"
ROOM = 56 * 1024 * 1024


def dot(a, b, ca=1, cb=0):
    return lax.dot_general(a, b, (((ca,), (cb,)), ((), ())), preferred_element_type=F32)


def swap(x, axis, bit):
    size = lax.axis_size(axis)
    return lax.ppermute(x, axis, [(i, i ^ bit) for i in range(size)])


def turn(x, axis, k):
    size = lax.axis_size(axis)
    return lax.ppermute(x, axis, [(i, (i + k) % size) for i in range(size)])


def core_sum(x):
    return x + swap(x, T, 1)


def own_part(x, count, index, dim=0):
    width = x.shape[dim] // count
    return lax.dynamic_slice_in_dim(x, index * width, width, axis=dim)


def ordered(mine, other, first):
    return jnp.where(first, mine, other), jnp.where(first, other, mine)


def core_join(x, dim):
    other = swap(x, T, 1)
    low, high = ordered(x, other, lax.axis_index(T) == 0)
    return jnp.concatenate([low, high], axis=dim)


def after(x, *deps):
    return lax.optimization_barrier((x, deps))[0]


def whole(shape, dtype):
    return jax.ShapeDtypeStruct(shape, dtype)


def call(kernel, outs, name, scratch=()):
    return pl.pallas_call(
        kernel,
        out_shape=outs,
        scratch_shapes=list(scratch),
        compiler_params=pltpu.CompilerParams(vmem_limit_bytes=ROOM),
        cost_estimate=pl.CostEstimate(flops=1, bytes_accessed=1, transcendentals=0),
        name=name,
    )


def context_quarter(shard):
    return own_part(shard, 4, lax.axis_index(C))


def first_round(stack, wait_for):
    nz, _, n = stack.shape
    z = lax.axis_index(Z)
    half = n // 256 * 128
    index = [lax.rem(z + k, nz) for k in range(1, nz)]
    others = jnp.concatenate([lax.dynamic_slice_in_dim(stack, i, 1) for i in index])
    firsts = [after(others[:, :, cut], *wait_for) for cut in (slice(half), slice(half, n))]
    return firsts, [swap(a, C, b0) for a, (b0, _) in zip(firsts, BOTH)]


def second_round(firsts, nears, wait_for=()):
    both = [jnp.concatenate([a, b]) for a, b in zip(firsts, nears)]
    return [swap(after(x, *wait_for), C, b1) for x, (_, b1) in zip(both, BOTH)]


def assemble(shard, quads, widths):
    count, q = quads[0][0].shape[:2]
    nz = count + 1
    starts = [sum(widths[:i]) for i in range(len(widths))]

    def kernel(*refs):
        outs = refs[7:]
        z = lax.axis_index(Z)
        c = lax.axis_index(C)
        own = pl.ds(pl.multiple_of(z * 4 * q, 16), 4 * q)
        for out, begin, size in zip(outs, starts, widths):
            out[own] = refs[6][:, begin : begin + size]
        col = 0
        for side, (b0, b1) in enumerate(BOTH):
            first, near, far = refs[3 * side : 3 * side + 3]
            width = first.shape[-1]
            spans = []
            for out, begin, size in zip(outs, starts, widths):
                low, high = max(begin, col), min(begin + size, col + width)
                if low < high:
                    spans.append((out, slice(low - col, high - col), slice(low - begin, high - begin)))
            for ref, base, mask in ((first, 0, 0), (near, 0, b0), (far, 0, b1), (far, count, b0 ^ b1)):
                for s in range(count):
                    block = lax.rem(z + 1 + s, nz) * 4 + jnp.bitwise_xor(c, mask)
                    row = pl.multiple_of(block * q, 16)
                    for out, src, dst in spans:
                        out[pl.ds(row, q), dst] = ref[base + s, :, src]
            col += width

    shapes = tuple(whole((nz * 4 * q, w), BF) for w in widths)
    return call(kernel, shapes, "assemble")(*[x for quad in quads for x in quad], shard)


BOTH = ((1, 2), (2, 1))


def side_grads(products):
    rows, width = products[0][0].shape[1], products[0][1].shape[1]

    def kernel(*refs):
        for j in range(len(products)):
            grad = dot(refs[2 * j][...], refs[2 * j + 1][...], 0, 0)
            refs[-1][:, j * width : (j + 1) * width] = grad.astype(BF)

    arrays = [x for pair in products for x in pair]
    return call(kernel, whole((rows, width * len(products)), BF), "grads")(*arrays)


def z_split(parts):
    nz = lax.axis_size(Z)
    rows, width = parts[0].shape
    block = rows // nz

    def kernel(*refs):
        z = lax.axis_index(Z)
        for k, out in enumerate(refs[len(parts) :]):
            at = pl.ds(pl.multiple_of(lax.rem(z + k, nz) * block, 16), block)
            total = refs[0][at].astype(F32)
            for ref in refs[1 : len(parts)]:
                total = total + ref[at].astype(F32)
            out[...] = total.astype(BF)

    return call(kernel, (whole((block, width), BF),) * nz, "z_split")(*parts)


def exchange(copied, split, wait_for=()):
    c = lax.axis_index(C)
    half = after(own_part(copied, 2, lax.axis_index(T), 1), *wait_for)
    pieces = [own_part(split, 4, jnp.bitwise_xor(c, m), 1) for m in range(4)]
    if half.shape[1] != pieces[0].shape[1]:
        return pieces[0], [(swap(half, C, m), swap(pieces[m], C, m)) for m in (1, 2, 3)]
    return pieces[0], [swap(jnp.concatenate([half, pieces[m]]), C, m) for m in (1, 2, 3)]


def collected(copied, own, came):
    rows = copied.shape[0]
    came = [x if isinstance(x, tuple) else (x[:rows], x[rows:]) for x in came]
    halves = jnp.concatenate([a for a, _ in came])
    return jnp.concatenate([copied, core_join(halves, 1)]), jnp.concatenate([own] + [b for _, b in came])


def by_context(parts, outs, stores, name):
    def kernel(*refs):
        c = lax.axis_index(C)
        for m in range(4):
            for j, store in enumerate(stores):

                @pl.when(jnp.bitwise_xor(c, m) == j)
                def _():
                    store(refs[m][...].astype(F32), refs[4:])

    return call(kernel, outs, name)(*parts)


def early_join(parts):
    rows, width = parts[0].shape
    third = width // 3

    def store(j):
        at = slice(j * third, (j + 1) * third)

        def put(x, outs):
            outs[0][:, at] = x[:, :third]
            outs[1][at] = x[:, third : 2 * third].T
            rest = x[:, 2 * third :]
            if j == 0:
                outs[2][...] = rest
            elif j == 1:
                outs[3][...] = rest.T
            else:
                outs[4][:, (j - 2) * third : (j - 1) * third] = rest

        return put

    outs = (
        whole((rows, 4 * third), F32), whole((4 * third, rows), F32), whole((rows, third), F32),
        whole((third, rows), F32), whole((rows, 2 * third), F32),
    )
    return by_context(parts, outs, [store(j) for j in range(4)], "early_join")


def query_join(parts):
    rows, width = parts[0].shape

    def put_out(x, outs):
        outs[0][...] = x.T

    def store(i):
        def put(x, outs):
            outs[1][:, i] = x

        return put

    outs = (whole((width, rows), F32), whole((rows, 3, width), F32))
    return by_context(parts, outs, (put_out, store(0), store(1), store(2)), "query_join")


def turned(blocks):
    return [turn(blocks[k], Z, k) for k in range(1, len(blocks))]


def summed(own, came):
    total = own.astype(F32)
    for x in came:
        total = total + x.astype(F32)
    return total.astype(BF)


def turned_all(x):
    return [x] + [turn(x, Z, k) for k in range(1, lax.axis_size(Z))]


def swapped(x):
    return [swap(x, C, m) for m in (1, 2, 3)]


BESIDE = 1 << 20


def gather_beside(x, dim):
    nz = lax.axis_size(Z)
    extent = x.shape[dim]
    other = x.size // extent
    unit = 128 if dim else 16
    need = -(-BESIDE // (2 * nz * other * unit)) * unit
    if need > extent:
        pads = [(0, 0)] * x.ndim
        pads[dim] = (0, need - extent)
        x = jnp.pad(x, pads)
    return lax.all_gather(x, Z)


def from_neighbours(first, last):
    c = lax.axis_index(C)
    size = lax.axis_size(C)
    both = jnp.stack([first, last])
    near, far = swap(both, C, 1), swap(both, C, 3)
    odd = jnp.bitwise_and(c, 1) == 1
    before = jnp.where(odd, near[1], far[1])
    beyond = jnp.where(odd, far[0], near[0])
    return jnp.where(c > 0, before, 0), jnp.where(c < size - 1, beyond, 0)


def shifted(x, by):
    rows = x.shape[0]
    at = lax.broadcasted_iota(jnp.int32, x.shape, 0)
    if by > 0:
        return jnp.where(at >= by, pltpu.roll(x, by, 0), 0.0)
    return jnp.where(at < rows + by, pltpu.roll(x, rows + by, 0), 0.0)


def block_of(k, nz):
    return lax.rem(lax.axis_index(Z) - k + nz, nz)


def conv_main(toks, chrs, kernel):
    nz = len(toks)
    half = toks[0].shape[1]
    rows = toks[0].shape[0] - 16
    cols = kernel.shape[-1]
    part = rows // 2

    def run(*refs):
        c_ref, w_ref, keep_ref, send_ref, u_ref, rim_ref = refs[nz:]
        t = lax.axis_index(T)
        for k in range(nz):
            at = slice(k * rows, (k + 1) * rows)
            u_ref[at, :half] = refs[k][:rows]
            u_ref[at, half:] = c_ref[block_of(k, nz), :rows]
            at = slice(16 * k, 16 * k + 16)
            rim = refs[k][rows:]
            rim_ref[at, :half] = rim
            rim_ref[at, half:] = jnp.concatenate([rim[2:4], jnp.zeros((14, half), BF)])
        before = dot(rim_ref[...], w_ref[0])
        beyond = dot(rim_ref[...], w_ref[2])
        taps = [dot(u_ref[...], w_ref[m]) for m in range(3)]
        at = lax.broadcasted_iota(jnp.int32, (rows, cols), 0)
        for k in range(nz):
            here = slice(k * rows, (k + 1) * rows)
            total = taps[1][here]
            total = total + jnp.where(at == 0, before[16 * k : 16 * k + 1], pltpu.roll(taps[0][here], 1, 0))
            total = total + jnp.where(
                at == rows - 1, beyond[16 * k + 1 : 16 * k + 2], pltpu.roll(taps[2][here], rows - 1, 0)
            )

            @pl.when(t == 0)
            def _():
                keep_ref[k] = total[:part]
                send_ref[k] = total[part:]

            @pl.when(t != 0)
            def _():
                keep_ref[k] = total[part:]
                send_ref[k] = total[:part]

    shape = whole((nz, part, cols), F32)
    scratch = (pltpu.VMEM((nz * rows, 2 * half), BF), pltpu.VMEM((16 * nz, 2 * half), BF))
    return call(run, (shape, shape), "conv", scratch)(*toks, chrs, kernel)


def add_split(keep, came):
    nz = keep.shape[0]

    def run(*refs):
        for k in range(nz):
            refs[2 + k][...] = (refs[0][k] + refs[1][k]).astype(BF)

    return call(run, (whole(keep.shape[1:], BF),) * nz, "add_split")(keep, came)


def side_by_side(parts, forward):
    nz = len(parts)
    rows, cols = parts[0].shape
    z = lax.axis_index(Z)
    if cols % 128:
        stacked = jnp.stack(parts)
        order = [lax.rem((s - z if forward else z - s) + nz, nz) for s in range(nz)]
        return jnp.concatenate([lax.dynamic_index_in_dim(stacked, i, 0, keepdims=False) for i in order], axis=1)

    def run(*refs):
        z = lax.axis_index(Z)
        for k in range(nz):
            s = lax.rem((z + k if forward else z - k + nz), nz)
            refs[nz][:, pl.ds(pl.multiple_of(s * cols, 128), cols)] = refs[k][...]

    return call(run, whole((rows, nz * cols), BF), "side_by_side")(*parts)


def column_slices(x, nz):
    cols = x.shape[1] // nz
    z = lax.axis_index(Z)
    return [lax.dynamic_slice_in_dim(x, lax.rem(z + k, nz) * cols, cols, axis=1) for k in range(nz)]


def row_norm(v):
    average = jnp.mean(v, axis=-1, keepdims=True)
    centered = v - average
    spread = jnp.mean(centered * centered, axis=-1, keepdims=True)
    inverse = lax.rsqrt(spread + EPSILON)
    return centered * inverse, inverse


def row_norm_back(e, n, inverse, gain):
    ge = e * gain
    one = jnp.mean(ge, axis=-1, keepdims=True)
    two = jnp.mean(ge * n, axis=-1, keepdims=True)
    return inverse * (ge - one - n * two)


def column_sum(x):
    return jnp.sum(x, axis=0, keepdims=True)


def close(second, y_mine, y_other, chars_in, teacher_tok, teacher_chr, pick, notes, marks, gains, shifts):
    rows, width = second.shape
    chars = chars_in.shape[0]
    half = rows // 2
    step = 128

    def run(
        s_ref, ym_ref, yo_ref, c_ref, tt_ref, tc_ref, pick_ref, vt_ref, vc_ref, g_ref, b_ref,
        tok_ref, chr_ref, d3_ref, d4_ref, dy_ref, stat_ref, y_ref, hi_ref, lo_ref,
    ):
        t = lax.axis_index(T)
        y_ref[pl.ds(pl.multiple_of(t * half, 16), half)] = ym_ref[...]
        y_ref[pl.ds(pl.multiple_of((1 - t) * half, 16), half)] = yo_ref[...]
        zero = jnp.zeros((1, width), F32)
        gain_sum, shift_sum, loss = zero, zero, zero
        for i in range(0, rows, step):
            at = slice(i, i + step)
            n, inverse = row_norm(s_ref[at] + y_ref[at, :width].astype(F32))
            out = n * g_ref[2:3] + b_ref[2:3]
            tok_ref[at] = out
            diff = out - tt_ref[at].astype(F32)
            e = vt_ref[at, 1:2] * diff
            loss += column_sum(e * diff)
            gain_sum += column_sum(e * n)
            shift_sum += column_sum(e)
            d3_ref[at] = row_norm_back(e, n, inverse, g_ref[2:3])
        stat_ref[0:1] = gain_sum
        stat_ref[2:3] = shift_sum
        gain_sum, shift_sum = zero, zero
        for i in range(0, chars, step):
            at = slice(i, i + step)
            spread = dot(pick_ref[:, at], y_ref[:, width:], 0, 0)
            n, inverse = row_norm(c_ref[at].astype(F32) + spread)
            out = n * g_ref[3:4] + b_ref[3:4]
            chr_ref[at] = out
            diff = out - tc_ref[at].astype(F32)
            e = vc_ref[at, 2:3] * diff
            loss += column_sum(e * diff)
            gain_sum += column_sum(e * n)
            shift_sum += column_sum(e)
            d = row_norm_back(e, n, inverse, g_ref[3:4])
            d4_ref[at] = d
            high = d.astype(BF)
            hi_ref[at] = high
            lo_ref[at] = (d - high.astype(F32)).astype(BF)
        stat_ref[1:2] = gain_sum
        stat_ref[3:4] = shift_sum
        stat_ref[4:5] = 0.5 * loss
        stat_ref[5:8] = jnp.zeros((3, width), F32)
        mine = pl.ds(pl.multiple_of(t * half, 16), half)
        own = pick_ref[mine]
        dy_ref[:, :width] = d3_ref[mine].astype(BF)
        dy_ref[:, width:] = (dot(own, hi_ref[...]) + dot(own, lo_ref[...])).astype(BF)

    return call(
        run,
        (
            whole((rows, width), F32), whole((chars, width), F32), whole((rows, width), F32),
            whole((chars, width), F32), whole((half, 2 * width), BF), whole((8, width), F32),
        ),
        "close",
        (pltpu.VMEM((rows, 2 * width), BF), pltpu.VMEM((chars, width), BF), pltpu.VMEM((chars, width), BF)),
    )(second, y_mine, y_other, chars_in, teacher_tok, teacher_chr, pick, notes, marks, gains, shifts)


def spread_taps(mine_ref, other_ref, wide, whole_ref):
    nz, part, cols = mine_ref.shape
    part -= 16
    rows = 2 * part
    t = lax.axis_index(T)
    at = lax.broadcasted_iota(jnp.int32, (rows, cols), 0)
    for k in range(nz):
        whole_ref[pl.ds(pl.multiple_of(t * part, 16), part)] = mine_ref[k, :part]
        whole_ref[pl.ds(pl.multiple_of((1 - t) * part, 16), part)] = other_ref[k, :part]
        a = mine_ref[k, part:].astype(F32)[0:1]
        b = other_ref[k, part:].astype(F32)[0:1]
        above, below = jnp.where(t == 0, a, b), jnp.where(t == 0, b, a)
        d = whole_ref[...].astype(F32)
        wide[1, k] = whole_ref[...]
        wide[0, k] = jnp.where(at == rows - 1, above, pltpu.roll(d, rows - 1, 0)).astype(BF)
        wide[2, k] = jnp.where(at == 0, below, pltpu.roll(d, 1, 0)).astype(BF)


def tap_scratch(mine):
    nz, part, cols = mine.shape
    rows = 2 * (part - 16)
    return pltpu.VMEM((3, nz, rows, cols), BF), pltpu.VMEM((rows, cols), BF)


def conv_back(mine, other, kernel):
    nz, part, cols = mine.shape
    rows = 2 * (part - 16)
    half = kernel.shape[1] // 2

    def run(*refs):
        m_ref, o_ref, w_ref = refs[:3]
        outs, (wide, whole_ref) = refs[3 : 3 + 2 * nz], refs[3 + 2 * nz :]
        spread_taps(m_ref, o_ref, wide, whole_ref)
        for side in range(2):
            at = slice(side * half, (side + 1) * half)
            x = sum(dot(wide[m].reshape(nz * rows, cols), w_ref[m, at], 1, 1) for m in range(3)).astype(BF)
            for k in range(nz):
                outs[side * nz + k][...] = x[k * rows : (k + 1) * rows]

    shapes = (whole((rows, half), BF),) * (2 * nz)
    outs = call(run, shapes, "conv_back", tap_scratch(mine))(mine, other, kernel)
    return outs[:nz], outs[nz:]


def conv_grads(toks, chrs, mine, other):
    nz, part, cols = mine.shape
    rows = 2 * (part - 16)
    half = toks[0].shape[1]

    def run(*refs):
        c_ref, m_ref, o_ref, out_ref, wide, whole_ref = refs[nz:]
        spread_taps(m_ref, o_ref, wide, whole_ref)
        for m in range(3):
            for side in range(2):
                total = jnp.zeros((half, cols), F32)
                for k in range(nz):
                    u = c_ref[block_of(k, nz), :rows] if side else refs[k][:rows]
                    total += dot(u, wide[m, k], 0, 0)
                for r in range(2):
                    out_ref[2 * side + r, m] = total[r * half // 2 : (r + 1) * half // 2].astype(BF)

    shape = whole((4, 3, half // 2, cols), BF)
    return call(run, shape, "conv_grads", tap_scratch(mine))(*toks, chrs, mine, other)


def scan_pair(a, b, e, f):
    n = a.shape[0]
    rows = lax.broadcasted_iota(jnp.int32, a.shape, 0)
    step = 1
    while step < n:
        has = rows >= step
        pa = jnp.where(has, pltpu.roll(a, step, 0), 1.0)
        pb = jnp.where(has, pltpu.roll(b, step, 0), 0.0)
        b = b + a * pb
        a = a * pa
        has = rows < n - step
        pe = jnp.where(has, pltpu.roll(e, n - step, 0), 1.0)
        pf = jnp.where(has, pltpu.roll(f, n - step, 0), 0.0)
        f = f + e * pf
        e = e * pe
        step *= 2
    return a, b, e, f


def store_scans(scans, refs):
    a, b, e, f = scans
    n = a.shape[0]
    for ref, x in zip(refs[:4], scans):
        ref[...] = x
    ends = refs[4]
    ends[...] = jnp.zeros(ends.shape, F32)
    ends[0:1], ends[1:2], ends[2:3], ends[3:4] = a[n - 1 :], b[n - 1 :], e[:1], f[:1]


def scan_shapes(chars, units):
    return (whole((chars, units), F32),) * 4 + (whole((8, units), F32),)


def entering(refs):
    c = lax.axis_index(C)
    up = jnp.zeros((1, refs[0].shape[1]), F32)
    down = up
    for j in range(4):
        for m, ref in enumerate(refs):
            now = jnp.bitwise_xor(c, j) == m
            up = jnp.where(jnp.logical_and(now, j < c), ref[0:1] * up + ref[1:2], up)
    for j in (3, 2, 1, 0):
        for m, ref in enumerate(refs):
            now = jnp.bitwise_xor(c, j) == m
            down = jnp.where(jnp.logical_and(now, j > c), ref[2:3] * down + ref[3:4], down)
    return up, down


def gates(proj_ref, bias_ref, units):
    up = jax.nn.sigmoid(proj_ref[:, :units] + bias_ref[0:1])
    down = jax.nn.sigmoid(proj_ref[:, 2 * units : 3 * units] + bias_ref[1:2])
    return up, down


def gru_open(chars_in, w_recur, bias, marks):
    chars = chars_in.shape[0]
    units = bias.shape[1]

    def run(c_ref, w_ref, b_ref, m_ref, proj_ref, *outs):
        proj_ref[...] = dot(c_ref[...], w_ref[...])
        up, down = gates(proj_ref, b_ref, units)
        store_scans(
            scan_pair(
                (1.0 - up) * m_ref[:, 0:1], up * proj_ref[:, units : 2 * units],
                (1.0 - down) * m_ref[:, 1:2], down * proj_ref[:, 3 * units :],
            ),
            outs,
        )

    return call(run, (whole((chars, 4 * units), F32),) + scan_shapes(chars, units), "gru_open")(
        chars_in, w_recur, bias, marks
    )


def gru_close(scans, ends, pick, notes, w_charp_t):
    chars, units = scans[0].shape
    rows = pick.shape[0]
    half = w_charp_t.shape[0] // 2

    def run(cu, hu, cd, hd, e0, e1, e2, e3, p_ref, n_ref, w_ref, up_ref, down_ref, in_ref, pool_ref, keep_ref, send_ref):
        up, down = entering((e0, e1, e2, e3))
        in_ref[...] = jnp.zeros(in_ref.shape, F32)
        in_ref[0:1], in_ref[1:2] = up, down
        up_ref[...] = hu[...] + cu[...] * up
        down_ref[...] = hd[...] + cd[...] * down
        for ref, at in ((up_ref, slice(units)), (down_ref, slice(units, 2 * units))):
            pool_ref[:, at] = (dot(p_ref[...], ref[...].astype(BF)) / n_ref[:, 0:1]).astype(BF)
        t = lax.axis_index(T)
        low = dot(pool_ref[...], w_ref[:half], 1, 1)
        high = dot(pool_ref[...], w_ref[half:], 1, 1)
        keep_ref[...] = jnp.where(t == 0, low, high)
        send_ref[...] = jnp.where(t == 0, high, low)

    state = whole((chars, units), F32)
    return call(
        run,
        (
            state, state, whole((8, units), F32), whole((rows, 2 * units), BF),
            whole((rows, half), F32), whole((rows, half), F32),
        ),
        "gru_close",
    )(*scans, *ends, pick, notes, w_charp_t)


def gru_back_open(dfb, proj, bias, marks, pick, notes, w_charp_t):
    chars = proj.shape[0]
    units = bias.shape[1]

    def run(d_ref, proj_ref, b_ref, m_ref, p_ref, n_ref, w_ref, dh_ref, *outs):
        pooled = dot(d_ref[...], w_ref[...]) / n_ref[:, 0:1]
        high = pooled.astype(BF)
        low = (pooled - high.astype(F32)).astype(BF)
        dh_ref[...] = dot(p_ref[...], high, 0, 0) + dot(p_ref[...], low, 0, 0)
        up, down = gates(proj_ref, b_ref, units)
        up = (1.0 - up) * m_ref[:, 0:1]
        down = (1.0 - down) * m_ref[:, 1:2]
        store_scans(scan_pair(down, down * dh_ref[:, units:], up, up * dh_ref[:, :units]), outs)

    return call(run, (whole((chars, 2 * units), F32),) + scan_shapes(chars, units), "gru_back_open")(
        dfb, proj, bias, marks, pick, notes, w_charp_t
    )


def gru_back_close(scans, ends, d_hidden, proj, bias, marks, states, entries, w_recur):
    chars, units = scans[0].shape
    width = w_recur.shape[0]

    def run(
        cd, md, cu, mu, e0, e1, e2, e3, dh_ref, proj_ref, b_ref, m_ref, hu_ref, hd_ref, in_ref, w_ref,
        low_ref, high_ref, stat_ref, part_ref,
    ):
        from_below, from_above = entering((e0, e1, e2, e3))
        at = lax.broadcasted_iota(jnp.int32, (chars, units), 0)
        first, last = at == 0, at == chars - 1
        up, down = gates(proj_ref, b_ref, units)
        m = mu[...] + cu[...] * from_above
        lam = dh_ref[:, :units] + jnp.where(last, from_above, pltpu.roll(m, chars - 1, 0))
        before = jnp.where(first, in_ref[0:1], pltpu.roll(hu_ref[...], 1, 0))
        d_gate = lam * (proj_ref[:, units : 2 * units] - m_ref[:, 0:1] * before) * up * (1.0 - up)
        low_ref[:, :units] = d_gate.astype(BF)
        low_ref[:, units:] = (lam * up).astype(BF)
        stat_ref[...] = jnp.zeros(stat_ref.shape, F32)
        stat_ref[0:1, :units] = column_sum(d_gate)
        m = md[...] + cd[...] * from_below
        lam = dh_ref[:, units:] + jnp.where(first, from_below, pltpu.roll(m, 1, 0))
        beyond = jnp.where(last, in_ref[1:2], pltpu.roll(hd_ref[...], chars - 1, 0))
        d_gate = lam * (proj_ref[:, 3 * units :] - m_ref[:, 1:2] * beyond) * down * (1.0 - down)
        high_ref[:, :units] = d_gate.astype(BF)
        high_ref[:, units:] = (lam * down).astype(BF)
        stat_ref[1:2, :units] = column_sum(d_gate)
        part_ref[...] = dot(low_ref[...], w_ref[:, : 2 * units], 1, 1) + dot(high_ref[...], w_ref[:, 2 * units :], 1, 1)

    part = whole((chars, 2 * units), BF)
    return call(
        run, (part, part, whole((8, width), F32), whole((chars, width), F32)), "gru_back_close"
    )(*scans, *ends, d_hidden, proj, bias, marks, *states, *entries, w_recur)


def score_block(k, q, seg_k, seg_q):
    s = dot(k, q, 1, 1) * HD ** (-0.5)
    return jnp.where(seg_k == seg_q, s, MASKED_SCORE)


def attend(x, others, w_query, w_mix_t, seg_keys, seg_here):
    rows, width = x.shape
    half = w_mix_t.shape[1]
    heads = half // HD
    keys = rows * (1 + others.shape[0])

    def run(x_ref, o_ref, w_ref, wm_ref, sk_ref, sq_ref, q_ref, kv_ref, lse_ref, att_ref, part_ref, turned):
        q_ref[...] = dot(x_ref[...], w_ref[:, :half]).astype(BF)
        kv_ref[:rows] = dot(x_ref[...], w_ref[:, half:]).astype(BF)
        for m in range(others.shape[0]):
            kv_ref[(m + 1) * rows : (m + 2) * rows] = dot(o_ref[m], w_ref[:, half:]).astype(BF)
        lse_ref[...] = jnp.zeros(lse_ref.shape, F32)
        for h in range(heads):
            at = slice(h * HD, (h + 1) * HD)
            s = score_block(kv_ref[:, at], q_ref[:, at], sk_ref[...], sq_ref[...])
            highest = jnp.max(s, axis=0, keepdims=True)
            lse = highest + jnp.log(jnp.sum(jnp.exp(s - highest), axis=0, keepdims=True))
            lse_ref[h : h + 1] = lse
            probs = jnp.exp(s - lse).astype(BF)
            turned[at] = dot(kv_ref[:, half + h * HD : half + (h + 1) * HD], probs, 0, 0)
        att_ref[...] = turned[...].T.astype(BF)
        part_ref[...] = dot(att_ref[...], wm_ref[...], 1, 1)

    return call(
        run,
        (
            whole((rows, half), BF), whole((keys, 2 * half), BF), whole((8, rows), F32),
            whole((rows, half), BF), whole((rows, width), F32),
        ),
        "attend",
        (pltpu.VMEM((half, rows), F32),),
    )(x, others, w_query, w_mix_t, seg_keys, seg_here)


def attend_back(d_two, mine, other, n_one, inv_one, gains, w_mix_t, q, kv, lse, seg_keys, seg_here):
    rows, width = d_two.shape
    half = q.shape[1]
    heads = half // HD
    keys = kv.shape[0]
    count = keys // rows

    def run(
        d_ref, a_ref, b_ref, n_ref, i_ref, g_ref, wm_ref, q_ref, kv_ref, lse_ref, sk_ref, sq_ref,
        d1_ref, datt_ref, stat_ref, dq_ref, own_ref, s1_ref, s2_ref, s3_ref, da_ref, turned,
    ):
        e = d_ref[...] + (a_ref[...] + b_ref[...])
        n = n_ref[...]
        stat_ref[...] = jnp.zeros(stat_ref.shape, F32)
        stat_ref[0:1] = column_sum(e * n)
        stat_ref[1:2] = column_sum(e)
        d = row_norm_back(e, n, i_ref[...], g_ref[0:1])
        d1_ref[...] = d
        datt_ref[...] = d.astype(BF)
        da_ref[...] = dot(datt_ref[...], wm_ref[...]).astype(BF)
        scale = HD ** (-0.5)
        sends = (None, s1_ref, s2_ref, s3_ref)
        for h in range(heads):
            at = slice(h * HD, (h + 1) * HD)
            vt = slice(half + h * HD, half + (h + 1) * HD)
            s = score_block(kv_ref[:, at], q_ref[:, at], sk_ref[...], sq_ref[...])
            p = jnp.exp(s - lse_ref[h : h + 1])
            dp = dot(kv_ref[:, vt], da_ref[:, at], 1, 1)
            delta = jnp.sum(p * dp, axis=0, keepdims=True)
            ds = (p * (dp - delta)).astype(BF)
            turned[at] = dot(kv_ref[:, at], ds, 0, 0) * scale
            dk = dot(ds, q_ref[:, at]) * scale
            dv = dot(p.astype(BF), da_ref[:, at])
            own_ref[:, at] = dk[:rows]
            own_ref[:, vt] = dv[:rows]
            for m in range(1, count):
                sends[m][:, at] = dk[m * rows : (m + 1) * rows].astype(BF)
                sends[m][:, vt] = dv[m * rows : (m + 1) * rows].astype(BF)
        dq_ref[...] = turned[...].T.astype(BF)

    send = whole((rows, 2 * half), BF)
    return call(
        run,
        (
            whole((rows, width), F32), whole((rows, width), BF), whole((8, width), F32), whole((rows, half), BF),
            whole((rows, 2 * half), F32), send, send, send,
        ),
        "attend_back",
        (pltpu.VMEM((rows, half), BF), pltpu.VMEM((half, rows), F32)),
    )(d_two, mine, other, n_one, inv_one, gains, w_mix_t, q, kv, lse, seg_keys, seg_here)


def query_grads(x, d_att, att, dq, own, came, w_query):
    rows, width = x.shape
    half = att.shape[1]

    def run(x_ref, da_ref, att_ref, dq_ref, own_ref, c1, c2, c3, w_ref, o0, o1, o2, o3, part_ref, kv_ref):
        c = lax.axis_index(C)
        kv_ref[...] = (own_ref[...] + c1[...].astype(F32) + c2[...].astype(F32) + c3[...].astype(F32)).astype(BF)
        pairs = (
            (da_ref, att_ref[...]), (x_ref, dq_ref[...]), (x_ref, kv_ref[:, :half]), (x_ref, kv_ref[:, half:]),
        )
        for j, (left, right) in enumerate(pairs):
            grad = dot(left[...], right, 0, 0).astype(BF)
            for m, out in enumerate((o0, o1, o2, o3)):

                @pl.when(jnp.bitwise_xor(c, j) == m)
                def _():
                    out[...] = grad

        part_ref[...] = dot(dq_ref[...], w_ref[:, :half], 1, 1) + dot(kv_ref[...], w_ref[:, half:], 1, 1)

    return call(
        run,
        (whole((width, half), BF),) * 4 + (whole((rows, width), F32),),
        "query_grads",
        (pltpu.VMEM((rows, 2 * half), BF),),
    )(x, d_att, att, dq, own, *came, w_query)


def gelu_parts(x):
    cdf = 0.5 * (1.0 + lax.erf(x * 0.7071067811865476))
    return cdf, jnp.exp(-0.5 * x * x) * 0.3989422804014327


def feed(x, mine, other, gains, shifts, w_upper, w_lower_t):
    rows, width = x.shape
    hidden = w_upper.shape[1]

    def run(x_ref, a_ref, b_ref, g_ref, s_ref, wu_ref, wd_ref, n_ref, i_ref, low_ref, pre_ref, act_ref, part_ref):
        n, inverse = row_norm(x_ref[...].astype(F32) + (a_ref[...] + b_ref[...]))
        n_ref[...] = n
        i_ref[...] = inverse
        low_ref[...] = (n * g_ref[0:1] + s_ref[0:1]).astype(BF)
        step = hidden // 4
        total = jnp.zeros((rows, width), F32)
        for i in range(4):
            at = slice(i * step, (i + 1) * step)
            pre = dot(low_ref[...], wu_ref[:, at])
            pre_ref[:, at] = pre
            act_ref[:, at] = (pre * gelu_parts(pre)[0]).astype(BF)
            total += dot(act_ref[:, at], wd_ref[:, at], 1, 1)
        part_ref[...] = total

    return call(
        run,
        (
            whole((rows, width), F32), whole((rows, 1), F32), whole((rows, width), BF), whole((rows, hidden), F32),
            whole((rows, hidden), BF), whole((rows, width), F32),
        ),
        "feed",
    )(x, mine, other, gains, shifts, w_upper, w_lower_t)


def feed_close(n_one, mine, other, gains, shifts, w_token):
    rows, width = n_one.shape
    half = w_token.shape[1]

    def run(n1_ref, a_ref, b_ref, g_ref, s_ref, w_ref, n_ref, i_ref, x2_ref, low_ref, fa_ref):
        first = n1_ref[...] * g_ref[0:1] + s_ref[0:1]
        n, inverse = row_norm(first + (a_ref[...] + b_ref[...]))
        n_ref[...] = n
        i_ref[...] = inverse
        second = n * g_ref[1:2] + s_ref[1:2]
        x2_ref[...] = second
        low_ref[...] = second.astype(BF)
        fa_ref[...] = dot(low_ref[...], w_ref[...]).astype(BF)

    return call(
        run,
        (
            whole((rows, width), F32), whole((rows, 1), F32), whole((rows, width), F32), whole((rows, width), BF),
            whole((rows, half), BF),
        ),
        "feed_close",
    )(n_one, mine, other, gains, shifts, w_token)


def join_back(parts, w_token):
    rows, half = parts[0].shape
    width = w_token.shape[0]

    def run(*refs):
        w_ref, low_ref, part_ref = refs[len(parts) :]
        total = refs[0][...].astype(F32)
        for ref in refs[1 : len(parts)]:
            total = total + ref[...].astype(F32)
        low_ref[...] = total.astype(BF)
        part_ref[...] = dot(low_ref[...], w_ref[...], 1, 1)

    return call(run, (whole((rows, half), BF), whole((rows, width), F32)), "join_back")(*parts, w_token)


def feed_back(d_three, mine, other, n_two, inv_two, gains, pre, w_upper, w_lower_t):
    rows, width = d_three.shape
    hidden = pre.shape[1]

    def run(d_ref, a_ref, b_ref, n_ref, i_ref, g_ref, pre_ref, wu_ref, wd_ref, d2_ref, low_ref, dpre_ref, part_ref, stat_ref):
        e = d_ref[...] + (a_ref[...] + b_ref[...])
        n = n_ref[...]
        stat_ref[...] = jnp.zeros(stat_ref.shape, F32)
        stat_ref[0:1] = column_sum(e * n)
        stat_ref[1:2] = column_sum(e)
        d = row_norm_back(e, n, i_ref[...], g_ref[1:2])
        d2_ref[...] = d
        low_ref[...] = d.astype(BF)
        step = hidden // 4
        total = jnp.zeros((rows, width), F32)
        for i in range(4):
            at = slice(i * step, (i + 1) * step)
            x = pre_ref[:, at]
            cdf, pdf = gelu_parts(x)
            dpre_ref[:, at] = (dot(low_ref[...], wd_ref[:, at]) * (cdf + x * pdf)).astype(BF)
            total += dot(dpre_ref[:, at], wu_ref[:, at], 1, 1)
        part_ref[...] = total

    return call(
        run,
        (
            whole((rows, width), F32), whole((rows, width), BF), whole((rows, hidden), BF), whole((rows, width), F32),
            whole((8, width), F32),
        ),
        "feed_back",
    )(d_three, mine, other, n_two, inv_two, gains, pre, w_upper, w_lower_t)


def neighbours(x):
    return [x] + [swap(x, C, m) for m in (1, 2, 3)]


def body(
    tokens_in, chars_in, segment_ids, char_counts, valid, teacher_tokens, teacher_chars,
    w_qkv, w_out, w_up, w_down, w_gru, gru_bias, w_tok, w_char, w_conv, ln_gain, ln_bias,
):
    nz = lax.axis_size(Z)
    c = lax.axis_index(C)
    t = lax.axis_index(T)
    rows, width = tokens_in.shape
    chars = chars_in.shape[0]
    half = width // 2
    units = gru_bias.shape[2]
    shard = w_qkv.shape[1]
    hidden = w_up.shape[2]
    gains, shifts, bias = ln_gain[0], ln_bias[0], gru_bias[0]

    mine = own_part(tokens_in, 2, t)
    others = core_join(jnp.stack([swap(mine, C, m) for m in (1, 2, 3)]), 1)
    widths = ((3 * half, 4 * units, half, half), (hidden, half, hidden))
    shards = (
        jnp.concatenate(
            [w_qkv[0].reshape(shard, -1), w_gru[0].reshape(shard, -1), w_char[0].reshape(-1, shard).T, w_out[0].T], axis=1
        ),
        jnp.concatenate([w_up[0], w_tok[0], w_down[0].T], axis=1),
    )
    quartered = shard % 64 == 0
    if quartered:
        stacks = [gather_beside(context_quarter(x), 1) for x in shards]
        firsts, nears = first_round(stacks[0][:, :, : shards[0].shape[1]], (others,))
        fars = second_round(firsts, nears)
        stacks[1] = after(stacks[1], fars)
        w_query, w_recur, w_charp_t, w_mix_t = assemble(shards[0], list(zip(firsts, nears, fars)), widths[0])
        firsts, nears = first_round(stacks[1][:, :, : shards[1].shape[1]], ())
    else:
        full = [lax.all_gather(x, Z, axis=0, tiled=True) for x in shards]
        w_query, w_recur, w_charp_t, w_mix_t = jnp.split(full[0], [3 * half, 3 * half + 4 * units, 4 * half + 4 * units], axis=1)
    seq_len = segment_ids.shape[1]
    offset_here = c * rows
    seg_full = segment_ids[0]
    seg_here = lax.dynamic_slice_in_dim(seg_full, offset_here, rows)
    seg_keys = jnp.concatenate(
        [lax.dynamic_slice_in_dim(seg_full, jnp.bitwise_xor(c, m) * rows, rows) for m in range(4)]
    )[:, None]
    counts = char_counts[0]
    ends = jnp.cumsum(counts)
    starts = ends - counts
    places = jnp.arange(chars, dtype=jnp.int32)
    chosen = jnp.logical_and(starts[:, None] <= places[None, :], places[None, :] < ends[:, None])
    pick = chosen.astype(BF)
    valid_tok = valid[0].astype(F32)
    char_seg = jnp.sum(jnp.where(chosen, seg_here[:, None], 0), axis=0)
    valid_chr = jnp.sum(jnp.where(chosen, valid_tok[:, None], 0.0), axis=0)
    prev_seg = seg_full[jnp.maximum(offset_here - 1, 0)]
    next_seg = seg_full[jnp.minimum(offset_here + rows, seq_len - 1)]
    first_keep = jnp.logical_and(c > 0, prev_seg == char_seg[0])
    last_keep = jnp.logical_and(c < lax.axis_size(C) - 1, next_seg == char_seg[-1])
    same = char_seg[1:] == char_seg[:-1]
    keep_up = jnp.concatenate([first_keep[None], same]).astype(F32)
    keep_down = jnp.concatenate([same, last_keep[None]]).astype(F32)
    marks = jnp.stack([keep_up, keep_down, valid_chr], axis=1)
    notes = jnp.stack([counts.astype(F32), valid_tok], axis=1)
    seg_row = seg_here[None, :]

    proj, *scans, ends_here = gru_open(chars_in, w_recur, bias, marks)
    ends_all = neighbours(ends_here)
    if quartered:
        fars = second_round(firsts, nears, ends_all[1:])
    *states, entries, pooled_low, keep, send = gru_close(
        scans, ends_all, pick, after(notes, nears) if quartered else notes, w_charp_t
    )
    fb = (keep + swap(send, T, 1)).astype(BF)
    fbs = gather_beside(fb, 0)

    q, kv, lse, mixed_low, part = attend(after(tokens_in, fb), others, w_query, w_mix_t, seg_keys, seg_row)
    if quartered:
        fars = after(fars, part)
        w_upper, w_token, w_lower_t = assemble(shards[1], list(zip(firsts, nears, fars)), widths[1])
    else:
        w_upper, w_token, w_lower_t = jnp.split(full[1], [hidden, hidden + half], axis=1)
    n_one, inv_one, first_low, pre, act_low, part2 = feed(
        after(tokens_in, fbs), part, swap(part, T, 1), gains, shifts, w_upper, w_lower_t
    )
    gathered = lax.all_gather(jnp.concatenate([own_part(first_low, 2, t, 1), act_low], axis=1), C)
    n_two, inv_two, second, second_low, fa = feed_close(n_one, part2, swap(part2, T, 1), gains, shifts, w_token)
    ends_u = [jnp.concatenate([fa[at], fb[at]]) for at in (slice(0, 1), slice(rows - 1, rows))]
    before, beyond = from_neighbours(*ends_u)
    rim = jnp.concatenate([before[:1], beyond[:1], before[1:], beyond[1:], jnp.zeros((12, half), BF)])
    fas = turned_all(jnp.concatenate([fa, rim]))

    cols = w_conv.shape[-1]
    kernel = w_conv[0].reshape(3, width, cols)
    keep, send = conv_main(fas, fbs, kernel)
    conv = add_split(keep, swap(send, T, 1))
    y_half = side_by_side([conv[0]] + [turn(conv[k], Z, nz - k) for k in range(1, nz)], True)
    out_tok, out_chr, d_res_three, d_res_four, d_mine, stats = close(
        second, y_half, swap(y_half, T, 1), chars_in, teacher_tokens, teacher_chars, pick,
        notes, marks, gains, shifts,
    )

    before, beyond = from_neighbours(d_mine[:1], d_mine[-1:])
    rim = jnp.where(t == 0, beyond, before)
    d_mine = jnp.concatenate([d_mine, rim, jnp.zeros((15, 2 * width), BF)])
    slices = column_slices(d_mine, nz)
    dy_mine = jnp.stack([slices[0]] + [turn(slices[k], Z, k) for k in range(1, nz)])
    dy_other = swap(dy_mine, T, 1)
    du_tok, du_chr = conv_back(after(dy_mine, gathered), dy_other, kernel)
    grad_kernel = conv_grads(fas, fbs, dy_mine, dy_other)
    tok_came = after([turn(du_tok[k], Z, nz - k) for k in range(1, nz)], grad_kernel)
    chr_came = [turn(after(du_chr[k], grad_kernel), Z, nz - k) for k in range(1, nz)]
    dfa, part = join_back([du_tok[0]] + tok_came, w_token)
    grad_kernel = lax.psum_scatter(grad_kernel, C, scatter_dimension=0)

    d_res_two, d_ffn, d_pre, part, stats_two = feed_back(
        d_res_three, part, swap(part, T, 1), n_two, inv_two, gains, pre, w_upper, w_lower_t
    )

    dfb = summed(du_chr[0], after(chr_came, d_pre))
    dfb_full = core_join(dfb, 1)
    d_hidden, *scans, ends_here = gru_back_open(dfb_full, proj, bias, marks, pick, notes, w_charp_t)
    ends_all = neighbours(ends_here)
    pre_own, pre_came = exchange(d_ffn, d_pre, ends_all[1:])
    gathered = [lax.dynamic_index_in_dim(gathered, jnp.bitwise_xor(c, m), 0, keepdims=False) for m in range(4)]
    act_part = jnp.concatenate([own_part(x[:, half:], 4, c, 1) for x in gathered])
    first_all = core_join(jnp.concatenate([x[:, :half] for x in gathered]), 1)
    d_low, d_high, stats_bias, part_chr = gru_back_close(
        scans, ends_all, d_hidden, proj, bias, marks, states, (entries,), w_recur
    )
    d_chr_in = d_res_four + core_sum(part_chr)
    chars_grads = side_grads(((second_low, dfa), (dfb_full, pooled_low), (chars_in, d_low), (chars_in, d_high)))
    chars_grads_z = lax.psum_scatter(chars_grads, Z, scatter_dimension=0, tiled=True)
    grad_kernel = lax.all_gather(grad_kernel, C)

    d_res_one, d_att, stats_one, dq, dkv_own, *dkv_sends = attend_back(
        after(d_res_two, chars_grads), part, swap(part, T, 1), n_one, inv_one, gains, w_mix_t, q, kv, lse, seg_keys, seg_row
    )
    came = [swap(x, C, m) for m, x in zip((1, 2, 3), dkv_sends)]
    ffn_all, pre_part = collected(d_ffn, pre_own, after(pre_came, dq))
    g_up = dot(first_all, pre_part, 0, 0).astype(BF)
    g_down = dot(ffn_all, act_part, 0, 0).astype(BF)
    ffn_piece = lax.psum_scatter(jnp.concatenate([g_up, g_down], axis=1), Z, scatter_dimension=0, tiled=True)
    counted = jnp.full((1, width), jnp.sum(valid_tok))
    packed = jnp.concatenate([stats[:5], counted, stats_bias[:2], stats_one[:2], stats_two[:2]])
    bit = 1
    while bit < nz:
        packed = packed + swap(packed, Z, bit)
        bit *= 2

    *sent, part = query_grads(tokens_in, d_att, mixed_low, dq, dkv_own, after(came, packed), w_query)
    query_own, *query_sent = sent
    query_came = [swap(x, C, m) for m, x in zip((1, 2, 3), query_sent)]
    d_tok_in = d_res_one + core_sum(part)
    quarters = after(chars_grads_z, query_sent)
    quarters = [own_part(quarters, 4, jnp.bitwise_xor(c, m), 1) for m in range(4)]
    chars_came = [swap(quarters[m], C, m) for m in (1, 2, 3)]
    query_came = after(query_came, chars_came)
    query_blocks = z_split([query_own] + query_came)
    query_turned = turned(query_blocks)
    ffn_piece = after(ffn_piece, query_came)
    chars_piece = summed(quarters[0], chars_came)
    early = jnp.concatenate([ffn_piece, chars_piece], axis=1)
    early_copies = swapped(after(early, query_blocks))
    query_piece = summed(query_blocks[0], query_turned)
    query_copies = swapped(query_piece)
    g_up, g_down, g_tok, g_char, g_gru = early_join([early] + after(early_copies, query_piece))
    grad_kernel = after(grad_kernel, g_up).reshape(2, 2, 3, half // 2, cols).astype(F32)
    grad_kernel = grad_kernel.transpose(2, 0, 1, 3, 4)
    g_out, g_query = query_join([query_piece] + after(query_copies, g_up))

    packed = after(packed, query_came)
    for bit in (1, 2):
        packed = packed + swap(packed, C, bit)
    loss = jnp.sum(packed[4]) / packed[5, 0]
    gain_total = jnp.stack([packed[8], packed[10], packed[0], packed[1]])[None]
    shift_total = jnp.stack([packed[9], packed[11], packed[2], packed[3]])[None]
    bias_total = packed[None, 6:8, :units]
    return (
        out_tok,
        out_chr,
        loss,
        d_tok_in,
        d_chr_in,
        g_query[None],
        g_out[None],
        g_up[None],
        g_down[None],
        g_gru.reshape(w_gru.shape),
        bias_total,
        g_tok[None],
        g_char.reshape(w_char.shape),
        grad_kernel.reshape(w_conv.shape),
        gain_total,
        shift_total,
    )


def solution(mesh):
    tok = P((Z, C), None)
    seq = P(Z, None)
    placed = (
        tok, tok, seq, tok, P(Z, C), tok, tok,
        P(None, Z, None, T), P(None, T, Z), P(None, Z, T), P(None, T, Z), P(None, Z, None, T),
        P(None, None, T), P(None, Z, T), P(None, None, T, Z), P(None, None, None, T, Z), P(), P(),
    )
    given = (
        tok, tok, P(), tok, tok,
        P(None, Z, None, T), P(None, T, Z), P(None, Z, T), P(None, T, Z), P(None, Z, None, T),
        P(None, None, T), P(None, Z, T), P(None, None, T, Z), P(None, None, None, T, Z), P(), P(),
    )
    return jax.shard_map(body, mesh=mesh, in_specs=placed, out_specs=given, check_vma=False)
```
